32 devices in a mesh: group: 4 (over z), expert: 8 (over y, x, core).
Axes of the slice: x: 2, y: 2, z: 4, core: 2. Of those that a mesh axis runs over, the one named last changes fastest.
Arguments:
- tokens: bfloat16 [512, 3584], P(('group', 'expert')), parts along dimension 0, may hold values from -6 to 6
- w_in: bfloat16 [2, 3584, 4096], P(None, None, ('group', 'expert')), parts along dimension 2, may hold values from -0.09375 to 0.09375
- w_down: bfloat16 [4096, 3584], P(('group', 'expert')), parts along dimension 0, may hold values from -0.5 to 0.5
- old_place: int32 [32], P('group'), parts along dimension 0, may hold values from 0 to 5, as said below
- new_place: int32 [32], P('group'), parts along dimension 0, may hold values from 0 to 5, as said below
- expert_ids: int32 [512, 2], P(('group', 'expert')), parts along dimension 0, may hold values from 0 to 5, all different within a row
- replica: int32 [512, 2], P(('group', 'expert')), parts along dimension 0, may hold values from 0 to 1
- combine: float32 [512, 2], P(('group', 'expert')), parts along dimension 0, may hold values from 0.2 to 1
Outputs:
- mixed: bfloat16 [512, 3584], P(('group', 'expert')), parts along dimension 0
The draws below stay inside these ranges and needn't reach their ends.
There are 4 independent parts, one for each index of `group`. The reference program is written for one: setup_inputs(seed, part) draws one part's arguments, and reference() takes and returns one part's arrays. A program takes and returns all parts, laid end to end along the dimension named above; each array names one. Nothing has to cross between parts.
Inputs may be any that keep to these rules, and one draw needn't show every extreme that they name: Each of the 6 experts is held by one or two slots of old_place; exactly two experts are held twice. new_place is old_place with the entries of some pairs of slots 2 i and 2 i + 1 exchanged.
All inputs are finite; a program needn't handle non-finite values.
Results may differ from the reference program's by a relative error of at most 0.0057.
Values may be sent and summed in bfloat16 or wider, within the bound.
No kernel may reach another device: no remote copies, remote signals or barrier semaphores. Data moves between devices by JAX's collectives and lax.ppermute only.
A program may use at most 64 MiB of HBM per device.

```python
import jax
import jax.numpy as jnp
from jax import lax

D = 3584
H_DEV = 128
SLOTS = 8
EXPERTS = 6
TOP = 2
CAP = 4
ROWS_DEV = 16
HID = 128
ROWS = 128
N_EXPERT = 8


def placements(key):
    key_first, key_second, key_order, key_flags, key_forced = jax.random.split(jax.random.fold_in(key, 11), 5)
    first = jax.random.randint(key_first, (), 0, EXPERTS)
    second = (first + jax.random.randint(key_second, (), 1, EXPERTS)) % EXPERTS
    pool_ids = jnp.concatenate([jnp.arange(EXPERTS, dtype=jnp.int32), jnp.stack([first, second]).astype(jnp.int32)])
    old_ids = pool_ids[jax.random.permutation(key_order, SLOTS)]
    swapped = jax.random.randint(key_flags, (SLOTS // 2,), 0, 2)
    forced = jax.random.randint(key_forced, (), 0, SLOTS // 2)
    swapped = swapped.at[forced].set(1)
    slot_ids = jnp.arange(SLOTS, dtype=jnp.int32)
    anchor = slot_ids + swapped[slot_ids // 2] * (1 - 2 * (slot_ids % 2))
    new_ids = old_ids[anchor]
    return (old_ids.astype(jnp.int32), new_ids.astype(jnp.int32))


def draw_old_place(key, part):
    return placements(key)[0]


def draw_new_place(key, part):
    return placements(key)[1]


def place_ends(result, key, smallest, high):
    spot = [jax.random.randint(jax.random.fold_in(key, axis), (), 0, length) for axis, length in enumerate(result.shape)]
    longest = result.shape.index(max(result.shape))
    beside = spot[:longest] + [(spot[longest] + 1) % result.shape[longest]] + spot[longest + 1:]
    return result.at[tuple(spot)].set(smallest).at[tuple(beside)].set(high)


def shard_levels(own_key, shape, cuts, smallest, largest):
    def one(axis_at, blocks):
        steps = jax.random.uniform(jax.random.fold_in(jax.random.fold_in(own_key, 6), axis_at), (blocks,), jnp.float32, smallest / len(cuts), largest / len(cuts))
        return jnp.repeat(jnp.exp(steps), shape[axis_at] // blocks).reshape((-1,) + (1,) * (len(shape) - axis_at - 1))

    factor_of = one(*cuts[0])
    for cut in cuts[1:]:
        factor_of = factor_of * one(*cut)
    return factor_of


def picks_of(own_key, rows, count, top, lift):
    ranking = jax.random.permutation(jax.random.fold_in(own_key, 1), count)
    favour = ranking
    for power in range(3):
        favour = favour * favour // count
    favour = favour * lift // count
    tickets = jax.random.randint(jax.random.fold_in(own_key, 2), (rows, count), 0, 4096) + favour
    fixed_rows = jax.random.permutation(jax.random.fold_in(own_key, 3), rows)[jnp.arange(count) % rows]
    tickets = jnp.where(jnp.arange(rows)[:, None] == fixed_rows[None, :], 1 << 14, tickets)
    priority = tickets * count + jnp.arange(count)
    return lax.top_k(priority.astype(jnp.int32), top)[1].astype(jnp.int32)


def noise(rng, dims, deviation, reach, cuts=(), held_as=jnp.bfloat16):
    array = jax.random.normal(rng, dims, jnp.float32) * deviation
    if len(cuts) > 0:
        array = shard_levels(rng, dims, cuts, -0.22, 0.18) * array
    return jnp.clip(array, min=-reach, max=reach).astype(held_as)


def setup_inputs(seed: int = 0, part: int = 0) -> dict:
    key_of = jax.random.split(jax.random.key(seed), 9)
    part_keys = jax.random.split(jax.random.fold_in(key_of[8], part), 9)
    return {
        "tokens": noise(part_keys[0], (ROWS, D), 1.0, 6.0, ((0, 8),)),
        "w_in": noise(part_keys[1], (2, D, SLOTS * HID), D ** -0.5, 0.09375, ((2, 8),)),
        "w_down": noise(part_keys[2], (SLOTS * HID, D), HID ** -0.5, 0.5, ((0, 8),)),
        "old_place": draw_old_place(jax.random.fold_in(jax.random.fold_in(key_of[8], part), 71), part),
        "new_place": draw_new_place(jax.random.fold_in(jax.random.fold_in(key_of[8], part), 71), part),
        "expert_ids": picks_of(part_keys[5], ROWS, EXPERTS, TOP, 5461),
        "replica": place_ends(jax.random.randint(part_keys[6], (ROWS, TOP), 0, 2), jax.random.fold_in(part_keys[6], 1), 0, 1).astype(jnp.int32),
        "combine": jnp.clip(0.2 + 0.8 * jax.random.uniform(part_keys[7], (ROWS, TOP), jnp.float32) ** shard_levels(part_keys[7], (ROWS, TOP), ((0, 8),), -0.2, 0.2), 0.2, 1.0),
    }


def routing(new_place, expert_ids, replica):
    slot_ids = jnp.arange(SLOTS, dtype=jnp.int32)
    experts = jnp.arange(EXPERTS, dtype=jnp.int32)
    holders = (new_place[None, :] == experts[:, None]).astype(jnp.int32)
    counts = jnp.sum(holders, axis=1)
    before = jnp.cumsum(holders, axis=1) - holders
    expert_hot = (expert_ids[..., None] == experts).astype(jnp.int32)
    count_sel = jnp.sum(expert_hot * counts, axis=-1)
    wanted = replica % jnp.maximum(count_sel, 1)
    holder_sel = jnp.sum(expert_hot[..., None] * holders, axis=2)
    rank_sel = jnp.sum(expert_hot[..., None] * before, axis=2)
    chosen = holder_sel * (rank_sel == wanted[..., None]).astype(jnp.int32)
    return chosen, jnp.sum(chosen * slot_ids, axis=-1)


def reference(tokens, w_in, w_down, old_place, new_place, expert_ids, replica, combine):
    shards = N_EXPERT // SLOTS
    hid = H_DEV * shards
    slot_ids = jnp.arange(SLOTS, dtype=jnp.int32)
    source = jnp.where(new_place == old_place, slot_ids, slot_ids + 1 - 2 * (slot_ids % 2))
    chosen, dest_slot = routing(new_place, expert_ids, replica)
    per_dev = chosen.reshape(N_EXPERT, ROWS_DEV * TOP, SLOTS)
    position = (jnp.cumsum(per_dev, axis=1) - per_dev).reshape(ROWS, TOP, SLOTS)
    position = jnp.sum(chosen * position, axis=-1)
    is_kept = position < CAP
    device = (jnp.arange(ROWS, dtype=jnp.int32) // ROWS_DEV)[:, None]
    total = SLOTS * N_EXPERT * CAP
    target = jnp.where(is_kept, (dest_slot * N_EXPERT + device) * CAP + position, total).astype(jnp.int32)
    row_ids = jnp.broadcast_to(jnp.arange(ROWS, dtype=jnp.int32)[:, None], (ROWS, TOP))
    row_index = jnp.zeros((total + 1,), jnp.int32).at[target.reshape(-1)].set(row_ids.reshape(-1))
    filled = jnp.zeros((total + 1,), jnp.bfloat16).at[target.reshape(-1)].set(jnp.ones((ROWS * TOP,), jnp.bfloat16))
    gathered = tokens[row_index[:total]] * filled[:total, None]
    buffers = gathered.reshape(SLOTS, N_EXPERT * CAP, D)

    def slot_output(slot):
        start = (source[slot] * hid).astype(jnp.int32)
        slab_in = lax.dynamic_slice_in_dim(w_in, start, hid, 2)
        slab_down = lax.dynamic_slice_in_dim(w_down, start, hid, 0)
        rows_in = buffers[slot]
        gate = jnp.dot(rows_in, slab_in[0], preferred_element_type=jnp.float32)
        up = jnp.dot(rows_in, slab_in[1], preferred_element_type=jnp.float32)
        hidden = (jax.nn.silu(gate) * up).astype(jnp.bfloat16)
        pieces = jnp.einsum("rsh,shd->rsd", hidden.reshape(-1, shards, H_DEV).astype(jnp.float32),
                            slab_down.reshape(shards, H_DEV, D).astype(jnp.float32))
        pieces = lax.optimization_barrier(pieces.astype(jnp.bfloat16))
        return jnp.sum(pieces.astype(jnp.float32), axis=1)

    outputs = lax.map(slot_output, jnp.arange(SLOTS, dtype=jnp.int32))
    flat_out = jnp.concatenate([outputs.reshape(total, D), jnp.zeros((1, D), jnp.float32)], axis=0)
    picked = flat_out[target]
    mixed = jnp.sum(combine[..., None] * picked, axis=1)
    return mixed.astype(jnp.bfloat16)
```

```python
import functools

import jax
import jax.numpy as jnp
from jax import lax
from jax.experimental import pallas as pl
from jax.experimental.pallas import tpu as pltpu
from jax.sharding import PartitionSpec as P

SLOTS = 8
CAP = 4

VMEM = pl.BlockSpec(memory_space=pltpu.VMEM)


def targets(shards, new_ref, old_ref, ids_ref, replica_ref):
    new, old = new_ref[...], old_ref[...]
    slots = new.shape[1]
    rows = ids_ref.shape[1]
    me = lax.axis_index("expert") // shards
    down = lax.broadcasted_iota(jnp.int32, (slots, slots), 0)
    across = lax.broadcasted_iota(jnp.int32, (slots, slots), 1)
    new_full = jnp.broadcast_to(new, (slots, slots)).astype(jnp.float32)
    source = jnp.where(new == old, across, across ^ 1)
    base = (CAP * (source ^ me)).astype(jnp.float32)
    diagonal = down == across
    mine = jnp.sum(jnp.where(diagonal, new_full, 0.0), axis=1, keepdims=True)
    line = jnp.sum(jnp.where(diagonal, base, 0.0), axis=1, keepdims=True)
    same = jnp.where(mine == new_full, 1.0, 0.0)
    count = jnp.sum(same, axis=1, keepdims=True).astype(jnp.int32)
    rank = jnp.sum(jnp.where(across < down, same, 0.0), axis=1, keepdims=True).astype(jnp.int32)
    expert = mine.astype(jnp.int32)
    chosen = []
    for k in range(ids_ref.shape[0]):
        wanted = replica_ref[k : k + 1, :] & (count - 1)
        hit = (ids_ref[k : k + 1, :] == expert) & (rank == wanted)
        chosen.append(jnp.where(hit, 1.0, 0.0))
    earlier = lax.broadcasted_iota(jnp.int32, (rows, rows), 0) < lax.broadcasted_iota(
        jnp.int32, (rows, rows), 1
    )
    any_choice = functools.reduce(jnp.add, chosen)
    position = jnp.dot(
        any_choice.astype(jnp.bfloat16),
        jnp.where(earlier, 1.0, 0.0).astype(jnp.bfloat16),
        preferred_element_type=jnp.float32,
    )
    found = []
    for hit in chosen:
        place = jnp.where(position < CAP, line + position + 1.0, 0.0)
        found.append((jnp.sum(hit * place, axis=0, keepdims=True) - 1.0).astype(jnp.int32))
        position = position + hit
    return found


def dispatch_kernel(shards, new_ref, old_ref, ids_ref, replica_ref, tokens_ref, *block_refs):
    found = targets(shards, new_ref, old_ref, ids_ref, replica_ref)
    lines = CAP * len(block_refs)
    line = lax.broadcasted_iota(jnp.int32, (lines, tokens_ref.shape[0]), 0)
    picked = functools.reduce(jnp.logical_or, [line == target for target in found])
    selector = jnp.where(picked, 1.0, 0.0).astype(jnp.bfloat16)
    buffer = jnp.dot(selector, tokens_ref[...], preferred_element_type=jnp.float32)
    for b, block_ref in enumerate(block_refs):
        block_ref[...] = buffer[CAP * b : CAP * (b + 1)].astype(jnp.bfloat16)


def combine_kernel(shards, new_ref, old_ref, ids_ref, replica_ref, combine_ref, weight_ref):
    found = targets(shards, new_ref, old_ref, ids_ref, replica_ref)
    line = lax.broadcasted_iota(jnp.int32, weight_ref.shape, 0)
    weight_ref[...] = functools.reduce(
        jnp.add,
        [
            jnp.where(line == target, combine_ref[k : k + 1, :], 0.0)
            for k, target in enumerate(found)
        ],
    )


def stack(refs):
    return jnp.concatenate([ref[...].astype(jnp.float32) for ref in refs], axis=0)


def expert_kernel(devices, w_in_ref, w_down_ref, *refs):
    rows = stack(refs[:devices]).astype(jnp.bfloat16)
    gate = jnp.dot(rows, w_in_ref[0], preferred_element_type=jnp.float32)
    up = jnp.dot(rows, w_in_ref[1], preferred_element_type=jnp.float32)
    hidden = (jax.nn.silu(gate) * up).astype(jnp.bfloat16)
    piece = jnp.dot(hidden, w_down_ref[...], preferred_element_type=jnp.float32)
    for b, out_ref in enumerate(refs[devices:]):
        out_ref[...] = piece[CAP * b : CAP * (b + 1)].astype(jnp.bfloat16)


def mix_kernel(shards, weight_ref, *refs):
    out_ref = refs[-1]
    total = functools.reduce(jnp.add, [stack(refs[j:-1:shards]) for j in range(shards)])
    weight = weight_ref[...]
    out_ref[...] = lax.dot_general(
        weight,
        total,
        (((0,), (0,)), ((), ())),
        precision=lax.Precision.HIGHEST,
        preferred_element_type=jnp.float32,
    ).astype(jnp.bfloat16)


def call(kernel, outs, args):
    return pl.pallas_call(
        kernel,
        out_shape=outs,
        in_specs=[VMEM] * len(args),
        out_specs=jax.tree.map(lambda _: VMEM, outs),
    )(*args)


def from_each(blocks, devices):
    return [
        block if b == 0 else lax.ppermute(block, "expert", [(i, i ^ b) for i in range(devices)])
        for b, block in enumerate(blocks)
    ]


def body(tokens, w_in, w_down, old_place, new_place, expert_ids, replica, combine):
    devices = lax.axis_size("expert")
    shards = devices // SLOTS
    rows, width = tokens.shape
    routing = (new_place[None], old_place[None], expert_ids.T, replica.T)
    block = jax.ShapeDtypeStruct((CAP, width), jnp.bfloat16)
    blocks = call(
        functools.partial(dispatch_kernel, shards), [block] * SLOTS, (*routing, tokens)
    )
    received = from_each([blocks[b // shards] for b in range(devices)], devices)
    weight = call(
        functools.partial(combine_kernel, shards),
        jax.ShapeDtypeStruct((SLOTS * CAP, rows), jnp.float32),
        (*routing, combine.T),
    )
    pieces = call(
        functools.partial(expert_kernel, devices), [block] * devices, (w_in, w_down, *received)
    )
    returned = from_each(pieces, devices)
    return call(
        functools.partial(mix_kernel, shards),
        jax.ShapeDtypeStruct((rows, width), jnp.bfloat16),
        (weight, *returned),
    )


def solution(mesh):
    placed = (
        P(("group", "expert"), None),
        P(None, None, ("group", "expert")),
        P(("group", "expert"), None),
        P("group"),
        P("group"),
        P(("group", "expert"), None),
        P(("group", "expert"), None),
        P(("group", "expert"), None),
    )
    return jax.shard_map(
        body, mesh=mesh, in_specs=placed, out_specs=P(("group", "expert"), None), check_vma=False
    )
```

```python
import functools

import jax
import jax.numpy as jnp
from jax import lax
from jax.experimental import pallas as pl
from jax.experimental.pallas import tpu as pltpu
from jax.sharding import PartitionSpec as P

SLOTS = 8
CAP = 4

VMEM = pl.BlockSpec(memory_space=pltpu.VMEM)


def targets(shards, new_ref, old_ref, ids_ref, replica_ref):
    new, old = new_ref[...], old_ref[...]
    slots = new.shape[1]
    rows = ids_ref.shape[1]
    me = lax.axis_index("expert") // shards
    down = lax.broadcasted_iota(jnp.int32, (slots, slots), 0)
    across = lax.broadcasted_iota(jnp.int32, (slots, slots), 1)
    new_full = jnp.broadcast_to(new, (slots, slots)).astype(jnp.float32)
    source = jnp.where(new == old, across, across ^ 1)
    base = (CAP * (source ^ me)).astype(jnp.float32)
    diagonal = down == across
    mine = jnp.sum(jnp.where(diagonal, new_full, 0.0), axis=1, keepdims=True)
    line = jnp.sum(jnp.where(diagonal, base, 0.0), axis=1, keepdims=True)
    same = jnp.where(mine == new_full, 1.0, 0.0)
    count = jnp.sum(same, axis=1, keepdims=True).astype(jnp.int32)
    rank = jnp.sum(jnp.where(across < down, same, 0.0), axis=1, keepdims=True).astype(jnp.int32)
    expert = mine.astype(jnp.int32)
    chosen = []
    for k in range(ids_ref.shape[0]):
        wanted = replica_ref[k : k + 1, :] & (count - 1)
        hit = (ids_ref[k : k + 1, :] == expert) & (rank == wanted)
        chosen.append(jnp.where(hit, 1.0, 0.0))
    earlier = lax.broadcasted_iota(jnp.int32, (rows, rows), 0) < lax.broadcasted_iota(
        jnp.int32, (rows, rows), 1
    )
    any_choice = functools.reduce(jnp.add, chosen)
    position = jnp.dot(
        any_choice.astype(jnp.bfloat16),
        jnp.where(earlier, 1.0, 0.0).astype(jnp.bfloat16),
        preferred_element_type=jnp.float32,
    )
    found = []
    for hit in chosen:
        place = jnp.where(position < CAP, line + position + 1.0, 0.0)
        found.append((jnp.sum(hit * place, axis=0, keepdims=True) - 1.0).astype(jnp.int32))
        position = position + hit
    return found


def dispatch_kernel(shards, new_ref, old_ref, ids_ref, replica_ref, tokens_ref, *block_refs):
    found = targets(shards, new_ref, old_ref, ids_ref, replica_ref)
    lines = sum(ref.shape[0] for ref in block_refs)
    line = lax.broadcasted_iota(jnp.int32, (lines, tokens_ref.shape[0]), 0)
    picked = functools.reduce(jnp.logical_or, [line == target for target in found])
    selector = jnp.where(picked, 1.0, 0.0).astype(jnp.bfloat16)
    buffer = jnp.dot(selector, tokens_ref[...], preferred_element_type=jnp.float32)
    size = block_refs[0].shape[0]
    for b, block_ref in enumerate(block_refs):
        block_ref[...] = buffer[size * b : size * (b + 1)].astype(jnp.bfloat16)


def combine_kernel(shards, new_ref, old_ref, ids_ref, replica_ref, combine_ref, weight_ref):
    found = targets(shards, new_ref, old_ref, ids_ref, replica_ref)
    line = lax.broadcasted_iota(jnp.int32, (weight_ref.shape[1], ids_ref.shape[1]), 0)
    weight = functools.reduce(
        jnp.add,
        [
            jnp.where(line == target, combine_ref[k : k + 1, :], 0.0)
            for k, target in enumerate(found)
        ],
    ).T
    high = weight.astype(jnp.bfloat16)
    low = (weight - high.astype(jnp.float32)).astype(jnp.bfloat16)
    weight_ref[...] = jnp.concatenate([high, low], axis=0)


def stack(refs):
    return jnp.concatenate([ref[...].astype(jnp.float32) for ref in refs], axis=0)


def expert_kernel(split, in_ref, down_ref, twin_in_ref, twin_down_ref, *refs):
    count = len(refs) // 2
    rows = stack(refs[:count]).astype(jnp.bfloat16)
    size = refs[0].shape[0]
    hidden = []
    for half, ref in enumerate((in_ref, twin_in_ref)):
        gate = jnp.dot(rows, ref[0], preferred_element_type=jnp.float32)
        up = jnp.dot(rows, ref[1], preferred_element_type=jnp.float32)
        value = jax.nn.silu(gate) * up
        if split:
            place = lax.broadcasted_iota(jnp.int32, value.shape, 0) & (size - 1)
            value = jnp.where((place >= size // 2) == bool(half), value, 0.0)
        hidden.append(value.astype(jnp.bfloat16))
    piece = jnp.dot(
        jnp.concatenate(hidden, axis=1),
        jnp.concatenate([down_ref[...], twin_down_ref[...]], axis=0),
        preferred_element_type=jnp.float32,
    )
    for b, out_ref in enumerate(refs[count:]):
        out_ref[...] = piece[size * b : size * (b + 1)].astype(jnp.bfloat16)


def mix_kernel(repeats, weight_ref, *refs):
    out_ref = refs[-1]
    total = functools.reduce(jnp.add, [stack(refs[j:-1:repeats]) for j in range(repeats)])
    high = total.astype(jnp.bfloat16)
    mixed = jnp.dot(weight_ref[...], high, preferred_element_type=jnp.float32)
    if repeats > 1:
        low = (total - high.astype(jnp.float32)).astype(jnp.bfloat16)
        mixed += jnp.dot(weight_ref[...], low, preferred_element_type=jnp.float32)
    rows = out_ref.shape[0]
    out_ref[...] = (mixed[:rows] + mixed[rows:]).astype(jnp.bfloat16)


def call(kernel, outs, args, flops=0):
    nbytes = sum(x.size * x.dtype.itemsize for x in jax.tree.leaves((outs, args)))
    return pl.pallas_call(
        kernel,
        out_shape=outs,
        in_specs=[VMEM] * len(args),
        out_specs=jax.tree.map(lambda _: VMEM, outs),
        compiler_params=pltpu.CompilerParams(vmem_limit_bytes=16 << 20),
        cost_estimate=pl.CostEstimate(flops=flops, bytes_accessed=nbytes, transcendentals=0),
    )(*args)


def swap(block, distance):
    if distance == 0:
        return block
    pairs = [(i, i ^ distance) for i in range(lax.axis_size("expert"))]
    return lax.ppermute(block, "expert", pairs)


def body(tokens, w_in, w_down, old_place, new_place, expert_ids, replica, combine):
    devices = lax.axis_size("expert")
    shards = devices // SLOTS
    split = shards == 1
    repeats = max(shards // 2, 1)
    rows, width = tokens.shape
    hidden = w_down.shape[0]
    twin_in, twin_down = swap(w_in, 1), swap(w_down, 1)
    routing = (new_place[None], old_place[None], expert_ids.T, replica.T)
    block = jax.ShapeDtypeStruct((CAP * (2 if split else 1), width), jnp.bfloat16)
    blocks = call(
        functools.partial(dispatch_kernel, shards),
        [block] * (devices // 2 // repeats),
        (*routing, tokens),
        2 * SLOTS * CAP * rows * width,
    )
    distances = range(0, devices, 2)
    received = [swap(blocks[c // repeats], d) for c, d in enumerate(distances)]
    weight = call(
        functools.partial(combine_kernel, shards),
        jax.ShapeDtypeStruct((2 * rows, SLOTS * CAP), jnp.bfloat16),
        (*routing, combine.T),
    )
    pieces = call(
        functools.partial(expert_kernel, split),
        [block] * len(distances),
        (w_in, w_down, twin_in, twin_down, *received),
        12 * len(distances) * block.shape[0] * hidden * width,
    )
    returned = [swap(piece, d) for piece, d in zip(pieces, distances)]
    return call(
        functools.partial(mix_kernel, repeats),
        jax.ShapeDtypeStruct((rows, width), jnp.bfloat16),
        (weight, *returned),
        4 * SLOTS * CAP * rows * width,
    )


def solution(mesh):
    placed = (
        P(("group", "expert"), None),
        P(None, None, ("group", "expert")),
        P(("group", "expert"), None),
        P("group"),
        P("group"),
        P(("group", "expert"), None),
        P(("group", "expert"), None),
        P(("group", "expert"), None),
    )
    return jax.shard_map(
        body, mesh=mesh, in_specs=placed, out_specs=P(("group", "expert"), None), check_vma=False
    )
```

```python
import functools

import jax
import jax.numpy as jnp
from jax import lax
from jax.experimental import pallas as pl
from jax.experimental.pallas import tpu as pltpu
from jax.sharding import PartitionSpec as P

SLOTS = 8
CAP = 4
CHIP_STEPS = ((0, 3, 1, 2), (0, 3, 2, 1))

VMEM = pl.BlockSpec(memory_space=pltpu.VMEM)
HBM = pl.BlockSpec(memory_space=pltpu.HBM)


def targets(shards, new, old, ids, replica):
    slots, rows = new.shape[1], ids.shape[1]
    device = lax.axis_index("expert")
    down = lax.broadcasted_iota(jnp.int32, (slots, slots), 0)
    across = lax.broadcasted_iota(jnp.int32, (slots, slots), 1)
    new_full = jnp.broadcast_to(new, (slots, slots)).astype(jnp.float32)
    away = jnp.where(new == old, across, across ^ 1) ^ (device // shards)
    if shards == 1:
        odd = device & 1
        chip = away >> 1
        step = sum(
            jnp.where(chip == jnp.where(odd == 1, c_odd, c_even), k, 0)
            for k, (c_even, c_odd) in enumerate(zip(*CHIP_STEPS))
        )
        away = (away & 1) | (step << 1)
    base = (CAP * away).astype(jnp.float32)
    diagonal = down == across
    mine = jnp.sum(jnp.where(diagonal, new_full, 0.0), axis=1, keepdims=True)
    line = jnp.sum(jnp.where(diagonal, base, 0.0), axis=1, keepdims=True)
    same = jnp.where(mine == new_full, 1.0, 0.0)
    count = jnp.sum(same, axis=1, keepdims=True).astype(jnp.int32)
    rank = jnp.sum(jnp.where(across < down, same, 0.0), axis=1, keepdims=True).astype(jnp.int32)
    expert = mine.astype(jnp.int32)
    chosen = []
    for k in range(ids.shape[0]):
        wanted = replica[k : k + 1] & (count - 1)
        hit = (ids[k : k + 1] == expert) & (rank == wanted)
        chosen.append(jnp.where(hit, 1.0, 0.0))
    earlier = lax.broadcasted_iota(jnp.int32, (rows, rows), 0) < lax.broadcasted_iota(
        jnp.int32, (rows, rows), 1
    )
    any_choice = functools.reduce(jnp.add, chosen)
    position = jnp.dot(
        any_choice.astype(jnp.bfloat16),
        jnp.where(earlier, 1.0, 0.0).astype(jnp.bfloat16),
        preferred_element_type=jnp.float32,
    )
    found = []
    for hit in chosen:
        place = jnp.where(position < CAP, line + position + 1.0, 0.0)
        found.append((jnp.sum(hit * place, axis=0, keepdims=True) - 1.0).astype(jnp.int32))
        position = position + hit
    return found


def start_copies(sources, buffers, sems):
    copies = [pltpu.make_async_copy(*pair, sems.at[i]) for i, pair in enumerate(zip(sources, buffers))]
    for copy in copies:
        copy.start()
    return copies


def dispatch_kernel(shards, *refs):
    sources, refs = refs[:5], refs[5:]
    found_ref, *block_refs = refs[:-6]
    buffers, sems = refs[-6:-1], refs[-1]
    copies = start_copies(sources, buffers, sems)
    for copy in copies[:-1]:
        copy.wait()
    found = targets(shards, *[ref[...] for ref in buffers[:-1]])
    found_ref[...] = jnp.concatenate(found, axis=0)
    tokens_ref = buffers[-1]
    size = block_refs[0].shape[0]
    line = lax.broadcasted_iota(jnp.int32, (size * len(block_refs), tokens_ref.shape[0]), 0)
    picked = functools.reduce(jnp.logical_or, [line == target for target in found])
    selector = jnp.where(picked, 1.0, 0.0).astype(jnp.bfloat16)
    copies[-1].wait()
    buffer = jnp.dot(selector, tokens_ref[...], preferred_element_type=jnp.float32)
    for b, block_ref in enumerate(block_refs):
        block_ref[...] = buffer[size * b : size * (b + 1)].astype(jnp.bfloat16)


def prepare_kernel(
    found_ref, combine_hbm, in_hbm, down_hbm, in_ref, down_ref, weight_ref, combine_ref, sems
):
    copies = start_copies(
        (combine_hbm, in_hbm, down_hbm), (combine_ref, in_ref, down_ref), sems
    )
    copies[0].wait()
    line = lax.broadcasted_iota(jnp.int32, (weight_ref.shape[1], combine_ref.shape[1]), 0)
    weight = functools.reduce(
        jnp.add,
        [
            jnp.where(line == found_ref[k : k + 1], combine_ref[k : k + 1], 0.0)
            for k in range(found_ref.shape[0])
        ],
    ).T
    high = weight.astype(jnp.bfloat16)
    low = (weight - high.astype(jnp.float32)).astype(jnp.bfloat16)
    weight_ref[...] = jnp.concatenate([high, low], axis=0)
    for copy in copies[1:]:
        copy.wait()


def stack(refs):
    return jnp.concatenate([ref[...].astype(jnp.float32) for ref in refs], axis=0)


def expert_kernel(split, in_ref, down_ref, twin_in_ref, twin_down_ref, *refs):
    count = len(refs) // 2
    rows = stack(refs[:count]).astype(jnp.bfloat16)
    size = refs[0].shape[0]
    hidden = []
    for half, ref in enumerate((in_ref, twin_in_ref)):
        gate = jnp.dot(rows, ref[0], preferred_element_type=jnp.float32)
        up = jnp.dot(rows, ref[1], preferred_element_type=jnp.float32)
        value = jax.nn.silu(gate) * up
        if split:
            place = lax.broadcasted_iota(jnp.int32, value.shape, 0) & (size - 1)
            value = jnp.where((place >= size // 2) == bool(half), value, 0.0)
        hidden.append(value.astype(jnp.bfloat16))
    piece = jnp.dot(
        jnp.concatenate(hidden, axis=1),
        jnp.concatenate([down_ref[...], twin_down_ref[...]], axis=0),
        preferred_element_type=jnp.float32,
    )
    for b, out_ref in enumerate(refs[count:]):
        out_ref[...] = piece[size * b : size * (b + 1)].astype(jnp.bfloat16)


def mix_kernel(repeats, weight_ref, *refs):
    out_hbm, out_ref, sems = refs[-3:]
    refs = refs[:-3]
    rows, width = out_ref.shape
    parts = sems.shape[0]
    step = width // parts
    copies = []
    for part in range(parts):
        columns = slice(part * step, (part + 1) * step)
        total = functools.reduce(
            jnp.add,
            [stack([ref.at[:, columns] for ref in refs[j::repeats]]) for j in range(repeats)],
        )
        high = total.astype(jnp.bfloat16)
        mixed = jnp.dot(weight_ref[...], high, preferred_element_type=jnp.float32)
        if repeats > 1:
            low = (total - high.astype(jnp.float32)).astype(jnp.bfloat16)
            mixed += jnp.dot(weight_ref[...], low, preferred_element_type=jnp.float32)
        out_ref[:, columns] = (mixed[:rows] + mixed[rows:]).astype(jnp.bfloat16)
        copies.append(
            pltpu.make_async_copy(out_ref.at[:, columns], out_hbm.at[:, columns], sems.at[part])
        )
        copies[-1].start()
    for copy in copies:
        copy.wait()


def call(kernel, outs, args, flops, arg_specs=None, out_specs=None, scratch=()):
    arg_specs = arg_specs or [VMEM] * len(args)
    nbytes = sum(x.size * x.dtype.itemsize for x in jax.tree.leaves((outs, args)))
    return pl.pallas_call(
        kernel,
        out_shape=outs,
        in_specs=arg_specs,
        out_specs=out_specs or jax.tree.map(lambda _: VMEM, outs),
        scratch_shapes=scratch,
        compiler_params=pltpu.CompilerParams(vmem_limit_bytes=16 << 20),
        cost_estimate=pl.CostEstimate(flops=flops, bytes_accessed=nbytes, transcendentals=0),
    )(*[pltpu.with_memory_space_constraint(x, s.memory_space) for x, s in zip(args, arg_specs)])


def shape_of(array):
    return jax.ShapeDtypeStruct(array.shape, array.dtype)


def scratch_for(*arrays):
    return [pltpu.VMEM(x.shape, x.dtype) for x in arrays] + [pltpu.SemaphoreType.DMA((len(arrays),))]


def swap(block, distance, odd_distance=None):
    if distance == 0:
        return block
    apart = (distance, distance if odd_distance is None else odd_distance)
    pairs = [(i, i ^ apart[i & 1]) for i in range(lax.axis_size("expert"))]
    return lax.ppermute(block, "expert", pairs)


def exchange(blocks, split):
    even, odd = CHIP_STEPS if split else (range(len(blocks)),) * 2
    return [swap(block, 2 * even[k], 2 * odd[k]) for k, block in enumerate(blocks)]


def body(tokens, w_in, w_down, old_place, new_place, expert_ids, replica, combine):
    devices = lax.axis_size("expert")
    shards = devices // SLOTS
    split = shards == 1
    repeats = max(shards // 2, 1)
    chips = devices // 2
    rows, width = tokens.shape
    hidden = w_down.shape[0]
    twin_in, twin_down = swap(w_in, 1), swap(w_down, 1)
    operands = (new_place[None], old_place[None], expert_ids.T, replica.T, tokens)
    combine = combine.T
    block = jax.ShapeDtypeStruct((CAP * (2 if split else 1), width), jnp.bfloat16)
    found, *blocks = call(
        functools.partial(dispatch_kernel, shards),
        [shape_of(operands[2])] + [block] * (chips // repeats),
        operands,
        2 * SLOTS * CAP * rows * width,
        [HBM] * len(operands),
        scratch=scratch_for(*operands),
    )
    received = exchange([blocks[c // repeats] for c in range(chips)], split)
    own_in, own_down, weight = call(
        prepare_kernel,
        [
            shape_of(w_in),
            shape_of(w_down),
            jax.ShapeDtypeStruct((2 * rows, SLOTS * CAP), jnp.bfloat16),
        ],
        (found, combine, w_in, w_down),
        0,
        [VMEM, HBM, HBM, HBM],
        scratch=[pltpu.VMEM(combine.shape, combine.dtype), pltpu.SemaphoreType.DMA((3,))],
    )
    pieces = call(
        functools.partial(expert_kernel, split),
        [block] * chips,
        (own_in, own_down, twin_in, twin_down, *received),
        12 * chips * block.shape[0] * hidden * width,
    )
    returned = exchange(pieces, split)
    parts = 4 if width % 512 == 0 else 1
    return call(
        functools.partial(mix_kernel, repeats),
        shape_of(tokens),
        (weight, *returned),
        4 * SLOTS * CAP * rows * width,
        out_specs=HBM,
        scratch=[pltpu.VMEM(tokens.shape, tokens.dtype), pltpu.SemaphoreType.DMA((parts,))],
    )


def solution(mesh):
    placed = (
        P(("group", "expert"), None),
        P(None, None, ("group", "expert")),
        P(("group", "expert"), None),
        P("group"),
        P("group"),
        P(("group", "expert"), None),
        P(("group", "expert"), None),
        P(("group", "expert"), None),
    )
    return jax.shard_map(
        body, mesh=mesh, in_specs=placed, out_specs=P(("group", "expert"), None), check_vma=False
    )
```

```python
import functools

import jax
import jax.numpy as jnp
from jax import lax
from jax.experimental import pallas as pl
from jax.experimental.pallas import tpu as pltpu
from jax.sharding import PartitionSpec as P

SLOTS = 8
CAP = 4
CHIP_STEPS = ((0, 3, 1, 2), (0, 3, 2, 1))

VMEM = pl.BlockSpec(memory_space=pltpu.VMEM)
HBM = pl.BlockSpec(memory_space=pltpu.HBM)


def targets(shards, new, old, ids, replica):
    slots, rows = new.shape[1], ids.shape[1]
    device = lax.axis_index("expert")
    down = lax.broadcasted_iota(jnp.int32, (slots, slots), 0)
    across = lax.broadcasted_iota(jnp.int32, (slots, slots), 1)
    new_full = jnp.broadcast_to(new, (slots, slots)).astype(jnp.float32)
    source = jnp.where(new == old, across, across ^ 1)
    away = source ^ (device // shards)
    if shards == 1:
        odd = device & 1
        chip = away >> 1
        step = sum(
            jnp.where(chip == jnp.where(odd == 1, c_odd, c_even), k, 0)
            for k, (c_even, c_odd) in enumerate(zip(*CHIP_STEPS))
        )
        away = (source & 1) | (step << 1)
    base = (CAP * away).astype(jnp.float32)
    diagonal = down == across
    mine = jnp.sum(jnp.where(diagonal, new_full, 0.0), axis=1, keepdims=True)
    line = jnp.sum(jnp.where(diagonal, base, 0.0), axis=1, keepdims=True)
    same = jnp.where(mine == new_full, 1.0, 0.0)
    count = jnp.sum(same, axis=1, keepdims=True).astype(jnp.int32)
    rank = jnp.sum(jnp.where(across < down, same, 0.0), axis=1, keepdims=True).astype(jnp.int32)
    expert = mine.astype(jnp.int32)
    chosen = []
    for k in range(ids.shape[0]):
        wanted = replica[k : k + 1] & (count - 1)
        hit = (ids[k : k + 1] == expert) & (rank == wanted)
        chosen.append(jnp.where(hit, 1.0, 0.0))
    earlier = lax.broadcasted_iota(jnp.int32, (rows, rows), 0) < lax.broadcasted_iota(
        jnp.int32, (rows, rows), 1
    )
    any_choice = functools.reduce(jnp.add, chosen)
    position = jnp.dot(
        any_choice.astype(jnp.bfloat16),
        jnp.where(earlier, 1.0, 0.0).astype(jnp.bfloat16),
        preferred_element_type=jnp.float32,
    )
    found = []
    for hit in chosen:
        place = jnp.where(position < CAP, line + position + 1.0, 0.0)
        found.append((jnp.sum(hit * place, axis=0, keepdims=True) - 1.0).astype(jnp.int32))
        position = position + hit
    return found


def start_copies(sources, buffers, sems):
    copies = [pltpu.make_async_copy(*pair, sems.at[i]) for i, pair in enumerate(zip(sources, buffers))]
    for copy in copies:
        copy.start()
    return copies


def dispatch_kernel(shards, *refs):
    sources, refs = refs[:5], refs[5:]
    found_ref, *block_refs = refs[:-6]
    buffers, sems = refs[-6:-1], refs[-1]
    copies = start_copies(sources, buffers, sems)
    for copy in copies[:-1]:
        copy.wait()
    found = targets(shards, *[ref[...] for ref in buffers[:-1]])
    found_ref[...] = jnp.concatenate(found, axis=0)
    tokens_ref = buffers[-1]
    size = block_refs[0].shape[0]
    line = lax.broadcasted_iota(jnp.int32, (size * len(block_refs), tokens_ref.shape[0]), 0)
    picked = functools.reduce(jnp.logical_or, [line == target for target in found])
    selector = jnp.where(picked, 1.0, 0.0).astype(jnp.bfloat16)
    copies[-1].wait()
    buffer = jnp.dot(selector, tokens_ref[...], preferred_element_type=jnp.float32)
    for b, block_ref in enumerate(block_refs):
        block_ref[...] = buffer[size * b : size * (b + 1)].astype(jnp.bfloat16)


def prepare_kernel(
    found_ref, combine_hbm, in_hbm, down_hbm, in_ref, down_ref, weight_ref, combine_ref, sems
):
    copies = start_copies(
        (combine_hbm, in_hbm, down_hbm), (combine_ref, in_ref, down_ref), sems
    )
    copies[0].wait()
    line = lax.broadcasted_iota(jnp.int32, (weight_ref.shape[1], combine_ref.shape[1]), 0)
    weight = functools.reduce(
        jnp.add,
        [
            jnp.where(line == found_ref[k : k + 1], combine_ref[k : k + 1], 0.0)
            for k in range(found_ref.shape[0])
        ],
    ).T
    high = weight.astype(jnp.bfloat16)
    low = (weight - high.astype(jnp.float32)).astype(jnp.bfloat16)
    weight_ref[...] = jnp.concatenate([high, low], axis=0)
    for copy in copies[1:]:
        copy.wait()


def stack(refs):
    return jnp.concatenate([ref[...].astype(jnp.float32) for ref in refs], axis=0)


def expert_kernel(split, in_ref, down_ref, twin_in_ref, twin_down_ref, *refs):
    odd = lax.axis_index("expert") & 1
    count = len(refs) // 2
    rows = stack(refs[:count]).astype(jnp.bfloat16)
    size = refs[0].shape[0]
    hidden = []
    for half, ref in enumerate((in_ref, twin_in_ref)):
        gate = jnp.dot(rows, ref[0], preferred_element_type=jnp.float32)
        up = jnp.dot(rows, ref[1], preferred_element_type=jnp.float32)
        value = jax.nn.silu(gate) * up
        if split:
            place = lax.broadcasted_iota(jnp.int32, value.shape, 0) // (size // 2)
            value = jnp.where((place & 1) == (odd ^ half), value, 0.0)
        hidden.append(value.astype(jnp.bfloat16))
    piece = jnp.dot(
        jnp.concatenate(hidden, axis=1),
        jnp.concatenate([down_ref[...], twin_down_ref[...]], axis=0),
        preferred_element_type=jnp.float32,
    )
    for b, out_ref in enumerate(refs[count:]):
        out_ref[...] = piece[size * b : size * (b + 1)].astype(jnp.bfloat16)


def mix_kernel(repeats, weight_ref, *refs):
    out_hbm, out_ref, sems = refs[-3:]
    refs = refs[:-3]
    rows, width = out_ref.shape
    parts = sems.shape[0]
    step = width // parts
    copies = []
    for part in range(parts):
        columns = slice(part * step, (part + 1) * step)
        total = functools.reduce(
            jnp.add,
            [stack([ref.at[:, columns] for ref in refs[j::repeats]]) for j in range(repeats)],
        )
        high = total.astype(jnp.bfloat16)
        mixed = jnp.dot(weight_ref[...], high, preferred_element_type=jnp.float32)
        if repeats > 1:
            low = (total - high.astype(jnp.float32)).astype(jnp.bfloat16)
            mixed += jnp.dot(weight_ref[...], low, preferred_element_type=jnp.float32)
        out_ref[:, columns] = (mixed[:rows] + mixed[rows:]).astype(jnp.bfloat16)
        copies.append(
            pltpu.make_async_copy(out_ref.at[:, columns], out_hbm.at[:, columns], sems.at[part])
        )
        copies[-1].start()
    for copy in copies:
        copy.wait()


def call(kernel, outs, args, flops, arg_specs=None, out_specs=None, scratch=()):
    arg_specs = arg_specs or [VMEM] * len(args)
    nbytes = sum(x.size * x.dtype.itemsize for x in jax.tree.leaves((outs, args)))
    return pl.pallas_call(
        kernel,
        out_shape=outs,
        in_specs=arg_specs,
        out_specs=out_specs or jax.tree.map(lambda _: VMEM, outs),
        scratch_shapes=scratch,
        compiler_params=pltpu.CompilerParams(vmem_limit_bytes=16 << 20),
        cost_estimate=pl.CostEstimate(flops=flops, bytes_accessed=nbytes, transcendentals=0),
    )(*[pltpu.with_memory_space_constraint(x, s.memory_space) for x, s in zip(args, arg_specs)])


def shape_of(array):
    return jax.ShapeDtypeStruct(array.shape, array.dtype)


def scratch_for(*arrays):
    return [pltpu.VMEM(x.shape, x.dtype) for x in arrays] + [pltpu.SemaphoreType.DMA((len(arrays),))]


def exchange(blocks, split, back=False):
    devices = lax.axis_size("expert")
    result = list(blocks)
    for k in range(1, len(blocks)):
        if split:
            pairs = [(i, i ^ 1 ^ 2 * CHIP_STEPS[i & 1][k]) for i in range(devices)]
        else:
            pairs = [(i, i ^ 2 * k) for i in range(devices)]
        if back:
            pairs = [(target, source) for source, target in pairs]
        result[k] = lax.ppermute(blocks[k], "expert", pairs)
    return result


def from_twin(array):
    pairs = [(i, i ^ 1) for i in range(lax.axis_size("expert"))]
    return lax.ppermute(array, "expert", pairs)


def body(tokens, w_in, w_down, old_place, new_place, expert_ids, replica, combine):
    devices = lax.axis_size("expert")
    shards = devices // SLOTS
    split = shards == 1
    repeats = max(shards // 2, 1)
    chips = devices // 2
    rows, width = tokens.shape
    hidden = w_down.shape[0]
    twin_in, twin_down = from_twin(w_in), from_twin(w_down)
    operands = (new_place[None], old_place[None], expert_ids.T, replica.T, tokens)
    combine = combine.T
    block = jax.ShapeDtypeStruct((CAP * (2 if split else 1), width), jnp.bfloat16)
    found, *blocks = call(
        functools.partial(dispatch_kernel, shards),
        [shape_of(operands[2])] + [block] * (chips // repeats),
        operands,
        2 * SLOTS * CAP * rows * width,
        [HBM] * len(operands),
        scratch=scratch_for(*operands),
    )
    received = exchange([blocks[c // repeats] for c in range(chips)], split)
    own_in, own_down, weight = call(
        prepare_kernel,
        [
            shape_of(w_in),
            shape_of(w_down),
            jax.ShapeDtypeStruct((2 * rows, SLOTS * CAP), jnp.bfloat16),
        ],
        (found, combine, w_in, w_down),
        0,
        [VMEM, HBM, HBM, HBM],
        scratch=[pltpu.VMEM(combine.shape, combine.dtype), pltpu.SemaphoreType.DMA((3,))],
    )
    pieces = call(
        functools.partial(expert_kernel, split),
        [block] * chips,
        (own_in, own_down, twin_in, twin_down, *received),
        12 * chips * block.shape[0] * hidden * width,
    )
    returned = exchange(pieces, split, back=True)
    parts = 4 if width % 512 == 0 else 1
    return call(
        functools.partial(mix_kernel, repeats),
        shape_of(tokens),
        (weight, *returned),
        4 * SLOTS * CAP * rows * width,
        out_specs=HBM,
        scratch=[pltpu.VMEM(tokens.shape, tokens.dtype), pltpu.SemaphoreType.DMA((parts,))],
    )


def solution(mesh):
    placed = (
        P(("group", "expert"), None),
        P(None, None, ("group", "expert")),
        P(("group", "expert"), None),
        P("group"),
        P("group"),
        P(("group", "expert"), None),
        P(("group", "expert"), None),
        P(("group", "expert"), None),
    )
    return jax.shard_map(
        body, mesh=mesh, in_specs=placed, out_specs=P(("group", "expert"), None), check_vma=False
    )
```

```python
import functools

import jax
import jax.numpy as jnp
from jax import lax
from jax.experimental import pallas as pl
from jax.experimental.pallas import tpu as pltpu
from jax.sharding import PartitionSpec as P

SLOTS = 8
CAP = 4

VMEM = pl.BlockSpec(memory_space=pltpu.VMEM)
HBM = pl.BlockSpec(memory_space=pltpu.HBM)


def targets(new, old, ids, replica):
    slots, rows = new.shape[1], ids.shape[1]
    down = lax.broadcasted_iota(jnp.int32, (slots, slots), 0)
    across = lax.broadcasted_iota(jnp.int32, (slots, slots), 1)
    new_full = jnp.broadcast_to(new, (slots, slots)).astype(jnp.float32)
    source = jnp.where(new == old, across, across ^ 1)
    base = (CAP * source).astype(jnp.float32)
    diagonal = down == across
    mine = jnp.sum(jnp.where(diagonal, new_full, 0.0), axis=1, keepdims=True)
    line = jnp.sum(jnp.where(diagonal, base, 0.0), axis=1, keepdims=True)
    same = jnp.where(mine == new_full, 1.0, 0.0)
    count = jnp.sum(same, axis=1, keepdims=True).astype(jnp.int32)
    rank = jnp.sum(jnp.where(across < down, same, 0.0), axis=1, keepdims=True).astype(jnp.int32)
    expert = mine.astype(jnp.int32)
    chosen = []
    for k in range(ids.shape[0]):
        wanted = replica[k : k + 1] & (count - 1)
        hit = (ids[k : k + 1] == expert) & (rank == wanted)
        chosen.append(jnp.where(hit, 1.0, 0.0))
    earlier = lax.broadcasted_iota(jnp.int32, (rows, rows), 0) < lax.broadcasted_iota(
        jnp.int32, (rows, rows), 1
    )
    any_choice = functools.reduce(jnp.add, chosen)
    position = jnp.dot(
        any_choice.astype(jnp.bfloat16),
        jnp.where(earlier, 1.0, 0.0).astype(jnp.bfloat16),
        preferred_element_type=jnp.float32,
    )
    found = []
    for hit in chosen:
        place = jnp.where(position < CAP, line + position + 1.0, 0.0)
        found.append((jnp.sum(hit * place, axis=0, keepdims=True) - 1.0).astype(jnp.int32))
        position = position + hit
    return found


def start_copies(sources, buffers, sems):
    copies = [pltpu.make_async_copy(*pair, sems.at[i]) for i, pair in enumerate(zip(sources, buffers))]
    for copy in copies:
        copy.start()
    return copies


def dispatch_kernel(*refs):
    sources, (found_ref, lines_ref), buffers, sems = refs[:5], refs[5:7], refs[7:-1], refs[-1]
    copies = start_copies(sources, buffers, sems)
    for copy in copies[:-1]:
        copy.wait()
    found = targets(*[ref[...] for ref in buffers[:-1]])
    found_ref[...] = jnp.concatenate(found, axis=0)
    tokens_ref = buffers[-1]
    line = lax.broadcasted_iota(jnp.int32, (lines_ref.shape[0], tokens_ref.shape[0]), 0)
    picked = functools.reduce(jnp.logical_or, [line == target for target in found])
    selector = jnp.where(picked, 1.0, 0.0).astype(jnp.bfloat16)
    copies[-1].wait()
    lines = jnp.dot(selector, tokens_ref[...], preferred_element_type=jnp.float32)
    lines_ref[...] = lines.astype(jnp.bfloat16)


def prepare_kernel(
    found_ref, combine_hbm, in_hbm, down_hbm, in_ref, down_ref, weight_ref, combine_ref, sems
):
    copies = start_copies(
        (combine_hbm, in_hbm, down_hbm), (combine_ref, in_ref, down_ref), sems
    )
    copies[0].wait()
    line = lax.broadcasted_iota(jnp.int32, (weight_ref.shape[1], combine_ref.shape[1]), 0)
    weight = functools.reduce(
        jnp.add,
        [
            jnp.where(line == found_ref[k : k + 1], combine_ref[k : k + 1], 0.0)
            for k in range(found_ref.shape[0])
        ],
    ).T
    high = weight.astype(jnp.bfloat16)
    low = (weight - high.astype(jnp.float32)).astype(jnp.bfloat16)
    weight_ref[...] = jnp.concatenate([high, low], axis=0)
    for copy in copies[1:]:
        copy.wait()


def expert_kernel(size, in_ref, down_ref, twin_in_ref, twin_down_ref, rows_ref, out_ref):
    odd = lax.axis_index("expert") & 1
    rows = rows_ref[...]
    hidden = []
    for half, ref in enumerate((in_ref, twin_in_ref)):
        gate = jnp.dot(rows, ref[0], preferred_element_type=jnp.float32)
        up = jnp.dot(rows, ref[1], preferred_element_type=jnp.float32)
        value = jax.nn.silu(gate) * up
        if size:
            place = lax.broadcasted_iota(jnp.int32, value.shape, 0) // size
            value = jnp.where((place & 1) == (odd ^ half), value, 0.0)
        hidden.append(value.astype(jnp.bfloat16))
    piece = jnp.dot(
        jnp.concatenate(hidden, axis=1),
        jnp.concatenate([down_ref[...], twin_down_ref[...]], axis=0),
        preferred_element_type=jnp.float32,
    )
    out_ref[...] = piece.astype(jnp.bfloat16)


def mix_kernel(weight_ref, pieces_ref, out_hbm, out_ref, sems):
    rows, width = out_ref.shape
    lines = weight_ref.shape[1]
    repeats = pieces_ref.shape[0] // lines
    parts = sems.shape[0]
    step = width // parts
    copies = []
    for part in range(parts):
        columns = slice(part * step, (part + 1) * step)
        total = pieces_ref[:, columns]
        if repeats > 1:
            total = total.astype(jnp.float32).reshape(lines // CAP, repeats, CAP, step)
            total = jnp.sum(total, axis=1).reshape(lines, step)
        high = total.astype(jnp.bfloat16)
        mixed = jnp.dot(weight_ref[...], high, preferred_element_type=jnp.float32)
        if repeats > 1:
            low = (total - high.astype(jnp.float32)).astype(jnp.bfloat16)
            mixed += jnp.dot(weight_ref[...], low, preferred_element_type=jnp.float32)
        out_ref[:, columns] = (mixed[:rows] + mixed[rows:]).astype(jnp.bfloat16)
        copies.append(
            pltpu.make_async_copy(out_ref.at[:, columns], out_hbm.at[:, columns], sems.at[part])
        )
        copies[-1].start()
    for copy in copies:
        copy.wait()


def call(kernel, outs, args, flops, arg_specs=None, out_specs=None, scratch=()):
    arg_specs = arg_specs or [VMEM] * len(args)
    nbytes = sum(x.size * x.dtype.itemsize for x in jax.tree.leaves((outs, args)))
    return pl.pallas_call(
        kernel,
        out_shape=outs,
        in_specs=arg_specs,
        out_specs=out_specs or jax.tree.map(lambda _: VMEM, outs),
        scratch_shapes=scratch,
        compiler_params=pltpu.CompilerParams(vmem_limit_bytes=16 << 20),
        cost_estimate=pl.CostEstimate(flops=flops, bytes_accessed=nbytes, transcendentals=0),
    )(*[pltpu.with_memory_space_constraint(x, s.memory_space) for x, s in zip(args, arg_specs)])


def shape_of(array):
    return jax.ShapeDtypeStruct(array.shape, array.dtype)


def scratch_for(*arrays):
    return [pltpu.VMEM(x.shape, x.dtype) for x in arrays] + [pltpu.SemaphoreType.DMA((len(arrays),))]


def exchange(lines):
    devices = lax.axis_size("expert")
    groups = [list(range(core, devices, 2)) for core in range(2)]
    return lax.all_to_all(
        lines, "expert", split_axis=0, concat_axis=0, axis_index_groups=groups, tiled=True
    )


def from_twin(array):
    pairs = [(i, i ^ 1) for i in range(lax.axis_size("expert"))]
    return lax.ppermute(array, "expert", pairs)


def body(tokens, w_in, w_down, old_place, new_place, expert_ids, replica, combine):
    devices = lax.axis_size("expert")
    shards = devices // SLOTS
    chips = devices // 2
    rows, width = tokens.shape
    hidden = w_down.shape[0]
    twin_in, twin_down = from_twin(w_in), from_twin(w_down)
    operands = (new_place[None], old_place[None], expert_ids.T, replica.T, tokens)
    combine = combine.T
    found, lines = call(
        dispatch_kernel,
        [shape_of(operands[2]), jax.ShapeDtypeStruct((SLOTS * CAP, width), jnp.bfloat16)],
        operands,
        2 * SLOTS * CAP * rows * width,
        [HBM] * len(operands),
        scratch=scratch_for(*operands),
    )
    if shards > 1:
        lines = jnp.repeat(lines.reshape(SLOTS, CAP, width), shards // 2, axis=0)
        lines = lines.reshape(chips * CAP, width)
    received = exchange(lines)
    own_in, own_down, weight = call(
        prepare_kernel,
        [
            shape_of(w_in),
            shape_of(w_down),
            jax.ShapeDtypeStruct((2 * rows, SLOTS * CAP), jnp.bfloat16),
        ],
        (found, combine, w_in, w_down),
        0,
        [VMEM, HBM, HBM, HBM],
        scratch=[pltpu.VMEM(combine.shape, combine.dtype), pltpu.SemaphoreType.DMA((3,))],
    )
    pieces = call(
        functools.partial(expert_kernel, CAP if shards == 1 else 0),
        shape_of(received),
        (own_in, own_down, twin_in, twin_down, received),
        12 * received.shape[0] * hidden * width,
    )
    returned = exchange(pieces)
    parts = 4 if width % 512 == 0 else 1
    return call(
        mix_kernel,
        shape_of(tokens),
        (weight, returned),
        4 * SLOTS * CAP * rows * width,
        out_specs=HBM,
        scratch=[pltpu.VMEM(tokens.shape, tokens.dtype), pltpu.SemaphoreType.DMA((parts,))],
    )


def solution(mesh):
    placed = (
        P(("group", "expert"), None),
        P(None, None, ("group", "expert")),
        P(("group", "expert"), None),
        P("group"),
        P("group"),
        P(("group", "expert"), None),
        P(("group", "expert"), None),
        P(("group", "expert"), None),
    )
    return jax.shard_map(
        body, mesh=mesh, in_specs=placed, out_specs=P(("group", "expert"), None), check_vma=False
    )
```

```python
import functools

import jax
import jax.numpy as jnp
from jax import lax
from jax.experimental import pallas as pl
from jax.experimental.pallas import tpu as pltpu
from jax.sharding import PartitionSpec as P

SLOTS = 8
CAP = 4

VMEM = pl.BlockSpec(memory_space=pltpu.VMEM)
HBM = pl.BlockSpec(memory_space=pltpu.HBM)


def targets(shards, new, old, ids, replica):
    slots, rows = new.shape[1], ids.shape[1]
    device = lax.axis_index("expert")
    down = lax.broadcasted_iota(jnp.int32, (slots, slots), 0)
    across = lax.broadcasted_iota(jnp.int32, (slots, slots), 1)
    new_full = jnp.broadcast_to(new, (slots, slots)).astype(jnp.float32)
    source = jnp.where(new == old, across, across ^ 1)
    away = source ^ (device // shards)
    if shards == 1:
        away = (away & -2) | (source & 1)
    base = (CAP * away).astype(jnp.float32)
    diagonal = down == across
    mine = jnp.sum(jnp.where(diagonal, new_full, 0.0), axis=1, keepdims=True)
    line = jnp.sum(jnp.where(diagonal, base, 0.0), axis=1, keepdims=True)
    same = jnp.where(mine == new_full, 1.0, 0.0)
    count = jnp.sum(same, axis=1, keepdims=True).astype(jnp.int32)
    rank = jnp.sum(jnp.where(across < down, same, 0.0), axis=1, keepdims=True).astype(jnp.int32)
    expert = mine.astype(jnp.int32)
    chosen = []
    for k in range(ids.shape[0]):
        wanted = replica[k : k + 1] & (count - 1)
        hit = (ids[k : k + 1] == expert) & (rank == wanted)
        chosen.append(jnp.where(hit, 1.0, 0.0))
    earlier = lax.broadcasted_iota(jnp.int32, (rows, rows), 0) < lax.broadcasted_iota(
        jnp.int32, (rows, rows), 1
    )
    any_choice = functools.reduce(jnp.add, chosen)
    position = jnp.dot(
        any_choice.astype(jnp.bfloat16),
        jnp.where(earlier, 1.0, 0.0).astype(jnp.bfloat16),
        preferred_element_type=jnp.float32,
    )
    found = []
    for hit in chosen:
        place = jnp.where(position < CAP, line + position + 1.0, 0.0)
        found.append((jnp.sum(hit * place, axis=0, keepdims=True) - 1.0).astype(jnp.int32))
        position = position + hit
    return found


def start_copies(sources, buffers, sems):
    copies = [pltpu.make_async_copy(*pair, sems.at[i]) for i, pair in enumerate(zip(sources, buffers))]
    for copy in copies:
        copy.start()
    return copies


def dispatch_kernel(shards, *refs):
    sources, refs = refs[:5], refs[5:]
    found_ref, *block_refs = refs[:-6]
    buffers, sems = refs[-6:-1], refs[-1]
    copies = start_copies(sources, buffers, sems)
    for copy in copies[:-1]:
        copy.wait()
    found = targets(shards, *[ref[...] for ref in buffers[:-1]])
    found_ref[...] = jnp.concatenate(found, axis=0)
    tokens_ref = buffers[-1]
    size = block_refs[0].shape[0]
    line = lax.broadcasted_iota(jnp.int32, (size * len(block_refs), tokens_ref.shape[0]), 0)
    picked = functools.reduce(jnp.logical_or, [line == target for target in found])
    selector = jnp.where(picked, 1.0, 0.0).astype(jnp.bfloat16)
    copies[-1].wait()
    buffer = jnp.dot(selector, tokens_ref[...], preferred_element_type=jnp.float32)
    for b, block_ref in enumerate(block_refs):
        block_ref[...] = buffer[size * b : size * (b + 1)].astype(jnp.bfloat16)


def prepare_kernel(
    found_ref, combine_hbm, in_hbm, down_hbm, in_ref, down_ref, weight_ref, combine_ref, sems
):
    copies = start_copies(
        (combine_hbm, in_hbm, down_hbm), (combine_ref, in_ref, down_ref), sems
    )
    copies[0].wait()
    line = lax.broadcasted_iota(jnp.int32, (weight_ref.shape[1], combine_ref.shape[1]), 0)
    weight = functools.reduce(
        jnp.add,
        [
            jnp.where(line == found_ref[k : k + 1], combine_ref[k : k + 1], 0.0)
            for k in range(found_ref.shape[0])
        ],
    ).T
    high = weight.astype(jnp.bfloat16)
    low = (weight - high.astype(jnp.float32)).astype(jnp.bfloat16)
    weight_ref[...] = jnp.concatenate([high, low], axis=0)
    for copy in copies[1:]:
        copy.wait()


def arrived(split, refs, columns=slice(None)):
    blocks = [ref[:, columns].astype(jnp.float32) for ref in refs]
    if split:
        near = len(blocks) // 2 - 1
        own, to_odd, far, to_even = blocks[0], blocks[1:-near - 1], blocks[-near - 1], blocks[-near:]
        odd = (lax.axis_index("expert") & 1) == 1
        blocks = [own, *[jnp.where(odd, *pair) for pair in zip(to_odd, to_even)], far]
    return blocks


def expert_kernel(split, count, in_ref, down_ref, twin_in_ref, twin_down_ref, *refs):
    odd = lax.axis_index("expert") & 1
    outs = refs[count:]
    rows = jnp.concatenate(arrived(split, refs[:count]), axis=0).astype(jnp.bfloat16)
    size = outs[0].shape[0]
    hidden = []
    for half, ref in enumerate((in_ref, twin_in_ref)):
        gate = jnp.dot(rows, ref[0], preferred_element_type=jnp.float32)
        up = jnp.dot(rows, ref[1], preferred_element_type=jnp.float32)
        value = jax.nn.silu(gate) * up
        if split:
            place = lax.broadcasted_iota(jnp.int32, value.shape, 0) // (size // 2)
            value = jnp.where((place & 1) == (odd ^ half), value, 0.0)
        hidden.append(value.astype(jnp.bfloat16))
    piece = jnp.dot(
        jnp.concatenate(hidden, axis=1),
        jnp.concatenate([down_ref[...], twin_down_ref[...]], axis=0),
        preferred_element_type=jnp.float32,
    )
    for b, out_ref in enumerate(outs):
        out_ref[...] = piece[size * b : size * (b + 1)].astype(jnp.bfloat16)


def mix_kernel(split, repeats, weight_ref, *refs):
    out_hbm, out_ref, sems = refs[-3:]
    refs = refs[:-3]
    rows, width = out_ref.shape
    parts = sems.shape[0]
    step = width // parts
    copies = []
    for part in range(parts):
        columns = slice(part * step, (part + 1) * step)
        total = functools.reduce(
            jnp.add,
            [
                jnp.concatenate(arrived(split, refs[j::repeats], columns), axis=0)
                for j in range(repeats)
            ],
        )
        high = total.astype(jnp.bfloat16)
        mixed = jnp.dot(weight_ref[...], high, preferred_element_type=jnp.float32)
        if repeats > 1:
            low = (total - high.astype(jnp.float32)).astype(jnp.bfloat16)
            mixed += jnp.dot(weight_ref[...], low, preferred_element_type=jnp.float32)
        out_ref[:, columns] = (mixed[:rows] + mixed[rows:]).astype(jnp.bfloat16)
        copies.append(
            pltpu.make_async_copy(out_ref.at[:, columns], out_hbm.at[:, columns], sems.at[part])
        )
        copies[-1].start()
    for copy in copies:
        copy.wait()


def call(kernel, outs, args, flops, arg_specs=None, out_specs=None, scratch=()):
    arg_specs = arg_specs or [VMEM] * len(args)
    nbytes = sum(x.size * x.dtype.itemsize for x in jax.tree.leaves((outs, args)))
    return pl.pallas_call(
        kernel,
        out_shape=outs,
        in_specs=arg_specs,
        out_specs=out_specs or jax.tree.map(lambda _: VMEM, outs),
        scratch_shapes=scratch,
        compiler_params=pltpu.CompilerParams(vmem_limit_bytes=16 << 20),
        cost_estimate=pl.CostEstimate(flops=flops, bytes_accessed=nbytes, transcendentals=0),
    )(*[pltpu.with_memory_space_constraint(x, s.memory_space) for x, s in zip(args, arg_specs)])


def shape_of(array):
    return jax.ShapeDtypeStruct(array.shape, array.dtype)


def scratch_for(*arrays):
    return [pltpu.VMEM(x.shape, x.dtype) for x in arrays] + [pltpu.SemaphoreType.DMA((len(arrays),))]


def exchange(blocks, split, ready=(0, 0)):
    devices = lax.axis_size("expert")

    def move(block, distance, cores=(0, 1)):
        pairs = [(i, i ^ distance) for i in range(devices) if i & 1 in cores]
        return lax.ppermute(block, "expert", pairs)

    if not split:
        return [blocks[0]] + [move(block, 2 * c) for c, block in enumerate(blocks) if c > 0]
    far = len(blocks) - 1
    near = [c for c in range(1, far)]
    from_even = [move(blocks[c], 2 * c + 1, (0,)) for c in near]
    from_far = move(blocks[far], 2 * far + 1)
    from_odd = [
        move(lax.optimization_barrier((blocks[c], first))[0], 2 * c + 1, (1,))
        for c, first in zip(near, ready)
    ]
    return [blocks[0], *from_even, from_far, *from_odd]


def from_twin(array):
    pairs = [(i, i ^ 1) for i in range(lax.axis_size("expert"))]
    return lax.ppermute(array, "expert", pairs)


def body(tokens, w_in, w_down, old_place, new_place, expert_ids, replica, combine):
    devices = lax.axis_size("expert")
    shards = devices // SLOTS
    split = shards == 1
    repeats = max(shards // 2, 1)
    chips = devices // 2
    rows, width = tokens.shape
    hidden = w_down.shape[0]
    twin_in, twin_down = from_twin(w_in), from_twin(w_down)
    operands = (new_place[None], old_place[None], expert_ids.T, replica.T, tokens)
    combine = combine.T
    block = jax.ShapeDtypeStruct((CAP * (2 if split else 1), width), jnp.bfloat16)
    found, *blocks = call(
        functools.partial(dispatch_kernel, shards),
        [shape_of(operands[2])] + [block] * (chips // repeats),
        operands,
        2 * SLOTS * CAP * rows * width,
        [HBM] * len(operands),
        scratch=scratch_for(*operands),
    )
    received = exchange([blocks[c // repeats] for c in range(chips)], split, (twin_in, twin_down))
    own_in, own_down, weight = call(
        prepare_kernel,
        [
            shape_of(w_in),
            shape_of(w_down),
            jax.ShapeDtypeStruct((2 * rows, SLOTS * CAP), jnp.bfloat16),
        ],
        (found, combine, w_in, w_down),
        0,
        [VMEM, HBM, HBM, HBM],
        scratch=[pltpu.VMEM(combine.shape, combine.dtype), pltpu.SemaphoreType.DMA((3,))],
    )
    pieces = call(
        functools.partial(expert_kernel, split, len(received)),
        [block] * chips,
        (own_in, own_down, twin_in, twin_down, *received),
        12 * chips * block.shape[0] * hidden * width,
    )
    returned = exchange(pieces, split)
    parts = 4 if width % 512 == 0 else 1
    return call(
        functools.partial(mix_kernel, split, repeats),
        shape_of(tokens),
        (weight, *returned),
        4 * SLOTS * CAP * rows * width,
        out_specs=HBM,
        scratch=[pltpu.VMEM(tokens.shape, tokens.dtype), pltpu.SemaphoreType.DMA((parts,))],
    )


def solution(mesh):
    placed = (
        P(("group", "expert"), None),
        P(None, None, ("group", "expert")),
        P(("group", "expert"), None),
        P("group"),
        P("group"),
        P(("group", "expert"), None),
        P(("group", "expert"), None),
        P(("group", "expert"), None),
    )
    return jax.shard_map(
        body, mesh=mesh, in_specs=placed, out_specs=P(("group", "expert"), None), check_vma=False
    )
```

```python
import functools

import jax
import jax.numpy as jnp
from jax import lax
from jax.experimental import pallas as pl
from jax.experimental.pallas import tpu as pltpu
from jax.sharding import PartitionSpec as P

SLOTS = 8
CAP = 4
CHIP_STEPS = ((0, 3, 1, 2), (0, 3, 2, 1))

VMEM = pl.BlockSpec(memory_space=pltpu.VMEM)
HBM = pl.BlockSpec(memory_space=pltpu.HBM)


def targets(shards, new_ref, old_ref, ids, replica):
    slots, rows = new_ref.shape[0], ids.shape[1]
    device = lax.axis_index("expert")
    down = lax.broadcasted_iota(jnp.int32, (slots, rows), 0)
    expert = jnp.zeros((slots, rows), jnp.int32)
    line = jnp.zeros((slots, rows), jnp.int32)
    for slot in range(slots):
        source = jnp.where(new_ref[slot] == old_ref[slot], slot, slot ^ 1)
        away = source ^ (device // shards)
        if shards == 1:
            chip = away >> 1
            even, odd = [
                sum(jnp.where(chip == c, k, 0) for k, c in enumerate(steps)) for steps in CHIP_STEPS
            ]
            away = (source & 1) | (jnp.where((device & 1) == 1, odd, even) << 1)
        expert = jnp.where(down == slot, new_ref[slot], expert)
        line = jnp.where(down == slot, CAP * away, line)
    count = jnp.zeros((slots, rows), jnp.int32)
    rank = jnp.zeros((slots, rows), jnp.int32)
    for slot in range(slots):
        same = expert == new_ref[slot]
        count += jnp.where(same, 1, 0)
        rank += jnp.where(same & (down > slot), 1, 0)
    chosen = []
    for k in range(ids.shape[0]):
        hit = (ids[k : k + 1] == expert) & (rank == (replica[k : k + 1] & (count - 1)))
        chosen.append(jnp.where(hit, 1.0, 0.0))
    earlier = lax.broadcasted_iota(jnp.int32, (rows, rows), 0) < lax.broadcasted_iota(
        jnp.int32, (rows, rows), 1
    )
    any_choice = functools.reduce(jnp.add, chosen)
    position = jnp.dot(
        any_choice.astype(jnp.bfloat16),
        jnp.where(earlier, 1.0, 0.0).astype(jnp.bfloat16),
        preferred_element_type=jnp.float32,
    )
    line = line.astype(jnp.float32)
    found = []
    for hit in chosen:
        place = jnp.where(position < CAP, line + position + 1.0, 0.0)
        found.append((jnp.sum(hit * place, axis=0, keepdims=True) - 1.0).astype(jnp.int32))
        position = position + hit
    return found


def start_copies(sources, buffers, sems):
    copies = [pltpu.make_async_copy(*pair, sems.at[i]) for i, pair in enumerate(zip(sources, buffers))]
    for copy in copies:
        copy.start()
    return copies


def dispatch_kernel(shards, *refs):
    sources, refs = refs[:5], refs[5:]
    found_ref, *block_refs = refs[:-6]
    buffers, sems = refs[-6:-1], refs[-1]
    copies = start_copies(sources, buffers, sems)
    for copy in copies[:-1]:
        copy.wait()
    found = targets(shards, *buffers[:2], *[ref[...] for ref in buffers[2:-1]])
    found_ref[...] = jnp.concatenate(found, axis=0)
    tokens_ref = buffers[-1]
    size = block_refs[0].shape[0]
    line = lax.broadcasted_iota(jnp.int32, (size * len(block_refs), tokens_ref.shape[0]), 0)
    picked = functools.reduce(jnp.logical_or, [line == target for target in found])
    selector = jnp.where(picked, 1.0, 0.0).astype(jnp.bfloat16)
    copies[-1].wait()
    buffer = jnp.dot(selector, tokens_ref[...], preferred_element_type=jnp.float32)
    for b, block_ref in enumerate(block_refs):
        block_ref[...] = buffer[size * b : size * (b + 1)].astype(jnp.bfloat16)


def prepare_kernel(
    found_ref, combine_hbm, in_hbm, down_hbm, in_ref, down_ref, weight_ref, combine_ref, sems
):
    copies = start_copies(
        (combine_hbm, in_hbm, down_hbm), (combine_ref, in_ref, down_ref), sems
    )
    copies[0].wait()
    line = lax.broadcasted_iota(jnp.int32, (weight_ref.shape[1], combine_ref.shape[1]), 0)
    weight = functools.reduce(
        jnp.add,
        [
            jnp.where(line == found_ref[k : k + 1], combine_ref[k : k + 1], 0.0)
            for k in range(found_ref.shape[0])
        ],
    ).T
    high = weight.astype(jnp.bfloat16)
    low = (weight - high.astype(jnp.float32)).astype(jnp.bfloat16)
    weight_ref[...] = jnp.concatenate([high, low], axis=0)
    for copy in copies[1:]:
        copy.wait()


def stack(refs):
    return jnp.concatenate([ref[...].astype(jnp.float32) for ref in refs], axis=0)


def expert_kernel(split, in_ref, down_ref, twin_in_ref, twin_down_ref, *refs):
    odd = lax.axis_index("expert") & 1
    count = len(refs) // 2
    rows = stack(refs[:count]).astype(jnp.bfloat16)
    size = refs[0].shape[0]
    hidden = []
    for half, ref in enumerate((in_ref, twin_in_ref)):
        both = jnp.concatenate([ref[0], ref[1]], axis=1)
        both = jnp.dot(rows, both, preferred_element_type=jnp.float32)
        gate, up = both[:, : ref.shape[2]], both[:, ref.shape[2] :]
        value = jax.nn.silu(gate) * up
        if split:
            place = lax.broadcasted_iota(jnp.int32, value.shape, 0) // (size // 2)
            value = jnp.where((place & 1) == (odd ^ half), value, 0.0)
        hidden.append(value.astype(jnp.bfloat16))
    piece = jnp.dot(
        jnp.concatenate(hidden, axis=1),
        jnp.concatenate([down_ref[...], twin_down_ref[...]], axis=0),
        preferred_element_type=jnp.float32,
    )
    for b, out_ref in enumerate(refs[count:]):
        out_ref[...] = piece[size * b : size * (b + 1)].astype(jnp.bfloat16)


def mix_kernel(repeats, weight_ref, *refs):
    out_hbm, out_ref, sems = refs[-3:]
    refs = refs[:-3]
    rows, width = out_ref.shape
    parts = sems.shape[0]
    step = width // parts
    copies = []
    for part in range(parts):
        columns = slice(part * step, (part + 1) * step)
        total = functools.reduce(
            jnp.add,
            [stack([ref.at[:, columns] for ref in refs[j::repeats]]) for j in range(repeats)],
        )
        high = total.astype(jnp.bfloat16)
        mixed = jnp.dot(weight_ref[...], high, preferred_element_type=jnp.float32)
        if repeats > 1:
            low = (total - high.astype(jnp.float32)).astype(jnp.bfloat16)
            mixed += jnp.dot(weight_ref[...], low, preferred_element_type=jnp.float32)
        out_ref[:, columns] = (mixed[:rows] + mixed[rows:]).astype(jnp.bfloat16)
        copies.append(
            pltpu.make_async_copy(out_ref.at[:, columns], out_hbm.at[:, columns], sems.at[part])
        )
        copies[-1].start()
    for copy in copies:
        copy.wait()


def call(kernel, outs, args, flops, arg_specs=None, out_specs=None, scratch=()):
    arg_specs = arg_specs or [VMEM] * len(args)
    nbytes = sum(x.size * x.dtype.itemsize for x in jax.tree.leaves((outs, args)))
    return pl.pallas_call(
        kernel,
        out_shape=outs,
        in_specs=arg_specs,
        out_specs=out_specs or jax.tree.map(lambda _: VMEM, outs),
        scratch_shapes=scratch,
        compiler_params=pltpu.CompilerParams(vmem_limit_bytes=16 << 20),
        cost_estimate=pl.CostEstimate(flops=flops, bytes_accessed=nbytes, transcendentals=0),
    )(*[pltpu.with_memory_space_constraint(x, s.memory_space) for x, s in zip(args, arg_specs)])


def shape_of(array):
    return jax.ShapeDtypeStruct(array.shape, array.dtype)


def scratch_for(scalars, arrays):
    return [
        *[pltpu.SMEM(x.shape, x.dtype) for x in scalars],
        *[pltpu.VMEM(x.shape, x.dtype) for x in arrays],
        pltpu.SemaphoreType.DMA((len(scalars) + len(arrays),)),
    ]


def exchange(blocks, split, back=False):
    devices = lax.axis_size("expert")
    result = list(blocks)
    for k in range(1, len(blocks)):
        if split:
            pairs = [(i, i ^ 1 ^ 2 * CHIP_STEPS[i & 1][k]) for i in range(devices)]
        else:
            pairs = [(i, i ^ 2 * k) for i in range(devices)]
        if back:
            pairs = [(target, source) for source, target in pairs]
        result[k] = lax.ppermute(blocks[k], "expert", pairs)
    return result


def from_twin(array):
    pairs = [(i, i ^ 1) for i in range(lax.axis_size("expert"))]
    return lax.ppermute(array, "expert", pairs)


def body(tokens, w_in, w_down, old_place, new_place, expert_ids, replica, combine):
    devices = lax.axis_size("expert")
    shards = devices // SLOTS
    split = shards == 1
    repeats = max(shards // 2, 1)
    chips = devices // 2
    rows, width = tokens.shape
    hidden = w_down.shape[0]
    twin_in, twin_down = from_twin(w_in), from_twin(w_down)
    operands = (new_place, old_place, expert_ids.T, replica.T, tokens)
    combine = combine.T
    block = jax.ShapeDtypeStruct((CAP * (2 if split else 1), width), jnp.bfloat16)
    found, *blocks = call(
        functools.partial(dispatch_kernel, shards),
        [shape_of(operands[2])] + [block] * (chips // repeats),
        operands,
        2 * SLOTS * CAP * rows * width,
        [HBM] * len(operands),
        scratch=scratch_for(operands[:2], operands[2:]),
    )
    received = exchange([blocks[c // repeats] for c in range(chips)], split)
    own_in, own_down, weight = call(
        prepare_kernel,
        [
            shape_of(w_in),
            shape_of(w_down),
            jax.ShapeDtypeStruct((2 * rows, SLOTS * CAP), jnp.bfloat16),
        ],
        (found, combine, w_in, w_down),
        0,
        [VMEM, HBM, HBM, HBM],
        scratch=[pltpu.VMEM(combine.shape, combine.dtype), pltpu.SemaphoreType.DMA((3,))],
    )
    pieces = call(
        functools.partial(expert_kernel, split),
        [block] * chips,
        (own_in, own_down, twin_in, twin_down, *received),
        12 * chips * block.shape[0] * hidden * width,
    )
    returned = exchange(pieces, split, back=True)
    parts = 4 if width % 512 == 0 else 1
    return call(
        functools.partial(mix_kernel, repeats),
        shape_of(tokens),
        (weight, *returned),
        4 * SLOTS * CAP * rows * width,
        out_specs=HBM,
        scratch=[pltpu.VMEM(tokens.shape, tokens.dtype), pltpu.SemaphoreType.DMA((parts,))],
    )


def solution(mesh):
    placed = (
        P(("group", "expert"), None),
        P(None, None, ("group", "expert")),
        P(("group", "expert"), None),
        P("group"),
        P("group"),
        P(("group", "expert"), None),
        P(("group", "expert"), None),
        P(("group", "expert"), None),
    )
    return jax.shard_map(
        body, mesh=mesh, in_specs=placed, out_specs=P(("group", "expert"), None), check_vma=False
    )
```

```python
import functools

import jax
import jax.numpy as jnp
from jax import lax
from jax.experimental import pallas as pl
from jax.experimental.pallas import tpu as pltpu
from jax.sharding import PartitionSpec as P

SLOTS = 8
CAP = 4
CHIP_STEPS = ((0, 3, 1, 2), (0, 3, 2, 1))

VMEM = pl.BlockSpec(memory_space=pltpu.VMEM)
HBM = pl.BlockSpec(memory_space=pltpu.HBM)


def targets(shards, new_ref, old_ref, ids, replica):
    slots, rows = new_ref.shape[0], ids.shape[1]
    device = lax.axis_index("expert")
    down = lax.broadcasted_iota(jnp.int32, (slots, rows), 0)
    expert = jnp.zeros((slots, rows), jnp.int32)
    line = jnp.zeros((slots, rows), jnp.int32)
    for slot in range(slots):
        source = jnp.where(new_ref[slot] == old_ref[slot], slot, slot ^ 1)
        away = source ^ (device // shards)
        if shards == 1:
            chip = away >> 1
            even, odd = [
                sum(jnp.where(chip == c, k, 0) for k, c in enumerate(steps)) for steps in CHIP_STEPS
            ]
            away = (source & 1) | (jnp.where((device & 1) == 1, odd, even) << 1)
        expert = jnp.where(down == slot, new_ref[slot], expert)
        line = jnp.where(down == slot, CAP * away, line)
    count = jnp.zeros((slots, rows), jnp.int32)
    rank = jnp.zeros((slots, rows), jnp.int32)
    for slot in range(slots):
        same = expert == new_ref[slot]
        count += jnp.where(same, 1, 0)
        rank += jnp.where(same & (down > slot), 1, 0)
    chosen = []
    for k in range(ids.shape[0]):
        hit = (ids[k : k + 1] == expert) & (rank == (replica[k : k + 1] & (count - 1)))
        chosen.append(jnp.where(hit, 1.0, 0.0))
    earlier = lax.broadcasted_iota(jnp.int32, (rows, rows), 0) < lax.broadcasted_iota(
        jnp.int32, (rows, rows), 1
    )
    any_choice = functools.reduce(jnp.add, chosen)
    position = jnp.dot(
        any_choice.astype(jnp.bfloat16),
        jnp.where(earlier, 1.0, 0.0).astype(jnp.bfloat16),
        preferred_element_type=jnp.float32,
    )
    line = line.astype(jnp.float32)
    found = []
    for hit in chosen:
        place = jnp.where(position < CAP, line + position + 1.0, 0.0)
        found.append((jnp.sum(hit * place, axis=0, keepdims=True) - 1.0).astype(jnp.int32))
        position = position + hit
    return found


def start_copies(sources, buffers, sems):
    copies = [pltpu.make_async_copy(*pair, sems.at[i]) for i, pair in enumerate(zip(sources, buffers))]
    for copy in copies:
        copy.start()
    return copies


def dispatch_kernel(shards, *refs):
    sources, refs = refs[:5], refs[5:]
    found_ref, *block_refs = refs[:-6]
    buffers, sems = refs[-6:-1], refs[-1]
    copies = start_copies(sources, buffers, sems)
    for copy in copies[:-1]:
        copy.wait()
    found = targets(shards, *buffers[:2], *[ref[...] for ref in buffers[2:-1]])
    found_ref[...] = jnp.concatenate(found, axis=0)
    tokens_ref = buffers[-1]
    size = block_refs[0].shape[0]
    line = lax.broadcasted_iota(jnp.int32, (size * len(block_refs), tokens_ref.shape[0]), 0)
    picked = functools.reduce(jnp.logical_or, [line == target for target in found])
    selector = jnp.where(picked, 1.0, 0.0).astype(jnp.bfloat16)
    copies[-1].wait()
    buffer = jnp.dot(selector, tokens_ref[...], preferred_element_type=jnp.float32)
    for b, block_ref in enumerate(block_refs):
        block_ref[...] = buffer[size * b : size * (b + 1)].astype(jnp.bfloat16)


def prepare_kernel(
    found_ref, combine_hbm, in_hbm, down_hbm, in_ref, down_ref, weight_ref, combine_ref, sems
):
    copies = start_copies(
        (combine_hbm, in_hbm, down_hbm), (combine_ref, in_ref, down_ref), sems
    )
    copies[0].wait()
    line = lax.broadcasted_iota(jnp.int32, (weight_ref.shape[1], combine_ref.shape[1]), 0)
    weight = functools.reduce(
        jnp.add,
        [
            jnp.where(line == found_ref[k : k + 1], combine_ref[k : k + 1], 0.0)
            for k in range(found_ref.shape[0])
        ],
    ).T
    high = weight.astype(jnp.bfloat16)
    low = (weight - high.astype(jnp.float32)).astype(jnp.bfloat16)
    weight_ref[...] = jnp.concatenate([high, low], axis=0)
    for copy in copies[1:]:
        copy.wait()


def stack(refs):
    return jnp.concatenate([ref[...].astype(jnp.float32) for ref in refs], axis=0)


def expert_kernel(split, in_ref, down_ref, *refs):
    count = len(refs) // 2
    rows = stack(refs[:count]).astype(jnp.bfloat16)
    size = refs[0].shape[0]
    hidden = []
    for half in range(2):
        gate = jnp.dot(rows, in_ref[half, 0], preferred_element_type=jnp.float32)
        up = jnp.dot(rows, in_ref[half, 1], preferred_element_type=jnp.float32)
        value = jax.nn.silu(gate) * up
        if split:
            place = lax.broadcasted_iota(jnp.int32, value.shape, 0) // (size // 2)
            value = jnp.where((place & 1) == half, value, 0.0)
        hidden.append(value.astype(jnp.bfloat16))
    piece = jnp.dot(
        jnp.concatenate(hidden, axis=1),
        down_ref[...].reshape(-1, down_ref.shape[2]),
        preferred_element_type=jnp.float32,
    )
    for b, out_ref in enumerate(refs[count:]):
        out_ref[...] = piece[size * b : size * (b + 1)].astype(jnp.bfloat16)


def mix_kernel(repeats, weight_ref, *refs):
    out_hbm, out_ref, sems = refs[-3:]
    refs = refs[:-3]
    rows, width = out_ref.shape
    parts = sems.shape[0]
    step = width // parts
    copies = []
    for part in range(parts):
        columns = slice(part * step, (part + 1) * step)
        total = functools.reduce(
            jnp.add,
            [stack([ref.at[:, columns] for ref in refs[j::repeats]]) for j in range(repeats)],
        )
        high = total.astype(jnp.bfloat16)
        mixed = jnp.dot(weight_ref[...], high, preferred_element_type=jnp.float32)
        if repeats > 1:
            low = (total - high.astype(jnp.float32)).astype(jnp.bfloat16)
            mixed += jnp.dot(weight_ref[...], low, preferred_element_type=jnp.float32)
        out_ref[:, columns] = (mixed[:rows] + mixed[rows:]).astype(jnp.bfloat16)
        copies.append(
            pltpu.make_async_copy(out_ref.at[:, columns], out_hbm.at[:, columns], sems.at[part])
        )
        copies[-1].start()
    for copy in copies:
        copy.wait()


def call(kernel, outs, args, flops, arg_specs=None, out_specs=None, scratch=()):
    arg_specs = arg_specs or [VMEM] * len(args)
    nbytes = sum(x.size * x.dtype.itemsize for x in jax.tree.leaves((outs, args)))
    return pl.pallas_call(
        kernel,
        out_shape=outs,
        in_specs=arg_specs,
        out_specs=out_specs or jax.tree.map(lambda _: VMEM, outs),
        scratch_shapes=scratch,
        compiler_params=pltpu.CompilerParams(vmem_limit_bytes=16 << 20),
        cost_estimate=pl.CostEstimate(flops=flops, bytes_accessed=nbytes, transcendentals=0),
    )(*[pltpu.with_memory_space_constraint(x, s.memory_space) for x, s in zip(args, arg_specs)])


def shape_of(array):
    return jax.ShapeDtypeStruct(array.shape, array.dtype)


def scratch_for(scalars, arrays):
    return [
        *[pltpu.SMEM(x.shape, x.dtype) for x in scalars],
        *[pltpu.VMEM(x.shape, x.dtype) for x in arrays],
        pltpu.SemaphoreType.DMA((len(scalars) + len(arrays),)),
    ]


def exchange(blocks, split, back=False):
    devices = lax.axis_size("expert")
    result = list(blocks)
    for k in range(1, len(blocks)):
        if split:
            pairs = [(i, i ^ 1 ^ 2 * CHIP_STEPS[i & 1][k]) for i in range(devices)]
        else:
            pairs = [(i, i ^ 2 * k) for i in range(devices)]
        if back:
            pairs = [(target, source) for source, target in pairs]
        result[k] = lax.ppermute(blocks[k], "expert", pairs)
    return result


def of_chip(array):
    pairs = [[i, i + 1] for i in range(0, lax.axis_size("expert"), 2)]
    return lax.all_gather(array, "expert", axis_index_groups=pairs)


def body(tokens, w_in, w_down, old_place, new_place, expert_ids, replica, combine):
    devices = lax.axis_size("expert")
    shards = devices // SLOTS
    split = shards == 1
    repeats = max(shards // 2, 1)
    chips = devices // 2
    rows, width = tokens.shape
    hidden = w_down.shape[0]
    chip_in, chip_down = of_chip(w_in), of_chip(w_down)
    operands = (new_place, old_place, expert_ids.T, replica.T, tokens)
    combine = combine.T
    block = jax.ShapeDtypeStruct((CAP * (2 if split else 1), width), jnp.bfloat16)
    found, *blocks = call(
        functools.partial(dispatch_kernel, shards),
        [shape_of(operands[2])] + [block] * (chips // repeats),
        operands,
        2 * SLOTS * CAP * rows * width,
        [HBM] * len(operands),
        scratch=scratch_for(operands[:2], operands[2:]),
    )
    received = exchange([blocks[c // repeats] for c in range(chips)], split)
    both_in, both_down, weight = call(
        prepare_kernel,
        [
            shape_of(chip_in),
            shape_of(chip_down),
            jax.ShapeDtypeStruct((2 * rows, SLOTS * CAP), jnp.bfloat16),
        ],
        (found, combine, chip_in, chip_down),
        0,
        [VMEM, HBM, HBM, HBM],
        scratch=[pltpu.VMEM(combine.shape, combine.dtype), pltpu.SemaphoreType.DMA((3,))],
    )
    pieces = call(
        functools.partial(expert_kernel, split),
        [block] * chips,
        (both_in, both_down, *received),
        12 * chips * block.shape[0] * hidden * width,
    )
    returned = exchange(pieces, split, back=True)
    parts = 4 if width % 512 == 0 else 1
    return call(
        functools.partial(mix_kernel, repeats),
        shape_of(tokens),
        (weight, *returned),
        4 * SLOTS * CAP * rows * width,
        out_specs=HBM,
        scratch=[pltpu.VMEM(tokens.shape, tokens.dtype), pltpu.SemaphoreType.DMA((parts,))],
    )


def solution(mesh):
    placed = (
        P(("group", "expert"), None),
        P(None, None, ("group", "expert")),
        P(("group", "expert"), None),
        P("group"),
        P("group"),
        P(("group", "expert"), None),
        P(("group", "expert"), None),
        P(("group", "expert"), None),
    )
    return jax.shard_map(
        body, mesh=mesh, in_specs=placed, out_specs=P(("group", "expert"), None), check_vma=False
    )
```

```python
import functools

import jax
import jax.numpy as jnp
from jax import lax
from jax.experimental import pallas as pl
from jax.experimental.pallas import tpu as pltpu
from jax.sharding import PartitionSpec as P

SLOTS = 8
CAP = 4
CHIP_STEPS = ((0, 3, 1, 2), (0, 3, 2, 1))

VMEM = pl.BlockSpec(memory_space=pltpu.VMEM)
HBM = pl.BlockSpec(memory_space=pltpu.HBM)


def targets(shards, new_ref, old_ref, ids, replica):
    slots, rows = new_ref.shape[0], ids.shape[1]
    device = lax.axis_index("expert")
    down = lax.broadcasted_iota(jnp.int32, (slots, rows), 0)
    expert = jnp.zeros((slots, rows), jnp.int32)
    line = jnp.zeros((slots, rows), jnp.int32)
    for slot in range(slots):
        source = jnp.where(new_ref[slot] == old_ref[slot], slot, slot ^ 1)
        away = source ^ (device // shards)
        if shards == 1:
            chip = away >> 1
            even, odd = [
                sum(jnp.where(chip == c, k, 0) for k, c in enumerate(steps)) for steps in CHIP_STEPS
            ]
            away = (source & 1) | (jnp.where((device & 1) == 1, odd, even) << 1)
        expert = jnp.where(down == slot, new_ref[slot], expert)
        line = jnp.where(down == slot, CAP * away, line)
    count = jnp.zeros((slots, rows), jnp.int32)
    rank = jnp.zeros((slots, rows), jnp.int32)
    for slot in range(slots):
        same = expert == new_ref[slot]
        count += jnp.where(same, 1, 0)
        rank += jnp.where(same & (down > slot), 1, 0)
    chosen = []
    for k in range(ids.shape[0]):
        hit = (ids[k : k + 1] == expert) & (rank == (replica[k : k + 1] & (count - 1)))
        chosen.append(jnp.where(hit, 1.0, 0.0))
    earlier = lax.broadcasted_iota(jnp.int32, (rows, rows), 0) < lax.broadcasted_iota(
        jnp.int32, (rows, rows), 1
    )
    any_choice = functools.reduce(jnp.add, chosen)
    position = jnp.dot(
        any_choice.astype(jnp.bfloat16),
        jnp.where(earlier, 1.0, 0.0).astype(jnp.bfloat16),
        preferred_element_type=jnp.float32,
    )
    line = line.astype(jnp.float32)
    found = []
    for hit in chosen:
        place = jnp.where(position < CAP, line + position + 1.0, 0.0)
        found.append((jnp.sum(hit * place, axis=0, keepdims=True) - 1.0).astype(jnp.int32))
        position = position + hit
    return found


def start_copies(sources, buffers, sems):
    copies = [pltpu.make_async_copy(*pair, sems.at[i]) for i, pair in enumerate(zip(sources, buffers))]
    for copy in copies:
        copy.start()
    return copies


def dispatch_kernel(shards, *refs):
    sources, refs = refs[:5], refs[5:]
    found_ref, *block_refs = refs[:-6]
    buffers, sems = refs[-6:-1], refs[-1]
    copies = start_copies(sources, buffers, sems)
    for copy in copies[:-1]:
        copy.wait()
    found = targets(shards, *buffers[:2], *[ref[...] for ref in buffers[2:-1]])
    found_ref[...] = jnp.concatenate(found, axis=0)
    tokens_ref = buffers[-1]
    size = block_refs[0].shape[0]
    line = lax.broadcasted_iota(jnp.int32, (size * len(block_refs), tokens_ref.shape[0]), 0)
    picked = functools.reduce(jnp.logical_or, [line == target for target in found])
    selector = jnp.where(picked, 1.0, 0.0).astype(jnp.bfloat16)
    copies[-1].wait()
    buffer = jnp.dot(selector, tokens_ref[...], preferred_element_type=jnp.float32)
    for b, block_ref in enumerate(block_refs):
        block_ref[...] = buffer[size * b : size * (b + 1)].astype(jnp.bfloat16)


def prepare_kernel(
    found_ref, combine_hbm, in_hbm, down_hbm, in_ref, down_ref, weight_ref, combine_ref, sems
):
    copies = start_copies(
        (combine_hbm, in_hbm, down_hbm), (combine_ref, in_ref, down_ref), sems
    )
    copies[0].wait()
    line = lax.broadcasted_iota(jnp.int32, (weight_ref.shape[1], combine_ref.shape[1]), 0)
    weight = functools.reduce(
        jnp.add,
        [
            jnp.where(line == found_ref[k : k + 1], combine_ref[k : k + 1], 0.0)
            for k in range(found_ref.shape[0])
        ],
    ).T
    high = weight.astype(jnp.bfloat16)
    low = (weight - high.astype(jnp.float32)).astype(jnp.bfloat16)
    weight_ref[...] = jnp.concatenate([high, low], axis=0)
    for copy in copies[1:]:
        copy.wait()


def stack(refs):
    return jnp.concatenate([ref[...].astype(jnp.float32) for ref in refs], axis=0)


def chunks(width, size=256):
    step = size if width % size == 0 else width
    return [slice(start, start + step) for start in range(0, width, step)]


def expert_kernel(split, in_ref, down_ref, twin_in_ref, twin_down_ref, *refs):
    odd = lax.axis_index("expert") & 1
    count = len(refs) // 2
    rows = stack(refs[:count]).astype(jnp.bfloat16)
    size = refs[0].shape[0]
    width, units = in_ref.shape[1:]
    hidden = []
    for half, ref in enumerate((in_ref, twin_in_ref)):
        both = jnp.zeros((rows.shape[0], 2 * units), jnp.float32)
        for chunk in chunks(width):
            part = jnp.concatenate([ref[0, chunk], ref[1, chunk]], axis=1)
            both += jnp.dot(rows[:, chunk], part, preferred_element_type=jnp.float32)
        value = jax.nn.silu(both[:, :units]) * both[:, units:]
        if split:
            place = lax.broadcasted_iota(jnp.int32, value.shape, 0) // (size // 2)
            value = jnp.where((place & 1) == (odd ^ half), value, 0.0)
        hidden.append(value.astype(jnp.bfloat16))
    hidden = jnp.concatenate(hidden, axis=1)
    for chunk in chunks(width):
        part = jnp.concatenate([down_ref[:, chunk], twin_down_ref[:, chunk]], axis=0)
        piece = jnp.dot(hidden, part, preferred_element_type=jnp.float32)
        for b, out_ref in enumerate(refs[count:]):
            out_ref[:, chunk] = piece[size * b : size * (b + 1)].astype(jnp.bfloat16)


def mix_kernel(repeats, weight_ref, *refs):
    out_hbm, out_ref, sems = refs[-3:]
    refs = refs[:-3]
    rows, width = out_ref.shape
    parts = sems.shape[0]
    step = width // parts
    copies = []
    for part in range(parts):
        columns = slice(part * step, (part + 1) * step)
        total = functools.reduce(
            jnp.add,
            [stack([ref.at[:, columns] for ref in refs[j::repeats]]) for j in range(repeats)],
        )
        high = total.astype(jnp.bfloat16)
        mixed = jnp.dot(weight_ref[...], high, preferred_element_type=jnp.float32)
        if repeats > 1:
            low = (total - high.astype(jnp.float32)).astype(jnp.bfloat16)
            mixed += jnp.dot(weight_ref[...], low, preferred_element_type=jnp.float32)
        out_ref[:, columns] = (mixed[:rows] + mixed[rows:]).astype(jnp.bfloat16)
        copies.append(
            pltpu.make_async_copy(out_ref.at[:, columns], out_hbm.at[:, columns], sems.at[part])
        )
        copies[-1].start()
    for copy in copies:
        copy.wait()


def call(kernel, outs, args, flops, arg_specs=None, out_specs=None, scratch=()):
    arg_specs = arg_specs or [VMEM] * len(args)
    nbytes = sum(x.size * x.dtype.itemsize for x in jax.tree.leaves((outs, args)))
    return pl.pallas_call(
        kernel,
        out_shape=outs,
        in_specs=arg_specs,
        out_specs=out_specs or jax.tree.map(lambda _: VMEM, outs),
        scratch_shapes=scratch,
        compiler_params=pltpu.CompilerParams(vmem_limit_bytes=16 << 20),
        cost_estimate=pl.CostEstimate(flops=flops, bytes_accessed=nbytes, transcendentals=0),
    )(*[pltpu.with_memory_space_constraint(x, s.memory_space) for x, s in zip(args, arg_specs)])


def shape_of(array):
    return jax.ShapeDtypeStruct(array.shape, array.dtype)


def scratch_for(scalars, arrays):
    return [
        *[pltpu.SMEM(x.shape, x.dtype) for x in scalars],
        *[pltpu.VMEM(x.shape, x.dtype) for x in arrays],
        pltpu.SemaphoreType.DMA((len(scalars) + len(arrays),)),
    ]


def exchange(blocks, split, back=False):
    devices = lax.axis_size("expert")
    result = list(blocks)
    for k in range(1, len(blocks)):
        if split:
            pairs = [(i, i ^ 1 ^ 2 * CHIP_STEPS[i & 1][k]) for i in range(devices)]
        else:
            pairs = [(i, i ^ 2 * k) for i in range(devices)]
        if back:
            pairs = [(target, source) for source, target in pairs]
        result[k] = lax.ppermute(blocks[k], "expert", pairs)
    return result


def from_twin(array):
    pairs = [(i, i ^ 1) for i in range(lax.axis_size("expert"))]
    return lax.ppermute(array, "expert", pairs)


def body(tokens, w_in, w_down, old_place, new_place, expert_ids, replica, combine):
    devices = lax.axis_size("expert")
    shards = devices // SLOTS
    split = shards == 1
    repeats = max(shards // 2, 1)
    chips = devices // 2
    rows, width = tokens.shape
    hidden = w_down.shape[0]
    twin_in, twin_down = from_twin(w_in), from_twin(w_down)
    operands = (new_place, old_place, expert_ids.T, replica.T, tokens)
    combine = combine.T
    block = jax.ShapeDtypeStruct((CAP * (2 if split else 1), width), jnp.bfloat16)
    found, *blocks = call(
        functools.partial(dispatch_kernel, shards),
        [shape_of(operands[2])] + [block] * (chips // repeats),
        operands,
        2 * SLOTS * CAP * rows * width,
        [HBM] * len(operands),
        scratch=scratch_for(operands[:2], operands[2:]),
    )
    received = exchange([blocks[c // repeats] for c in range(chips)], split)
    own_in, own_down, weight = call(
        prepare_kernel,
        [
            shape_of(w_in),
            shape_of(w_down),
            jax.ShapeDtypeStruct((2 * rows, SLOTS * CAP), jnp.bfloat16),
        ],
        (found, combine, w_in, w_down),
        0,
        [VMEM, HBM, HBM, HBM],
        scratch=[pltpu.VMEM(combine.shape, combine.dtype), pltpu.SemaphoreType.DMA((3,))],
    )
    pieces = call(
        functools.partial(expert_kernel, split),
        [block] * chips,
        (own_in, own_down, twin_in, twin_down, *received),
        12 * chips * block.shape[0] * hidden * width,
    )
    returned = exchange(pieces, split, back=True)
    parts = 4 if width % 512 == 0 else 1
    return call(
        functools.partial(mix_kernel, repeats),
        shape_of(tokens),
        (weight, *returned),
        4 * SLOTS * CAP * rows * width,
        out_specs=HBM,
        scratch=[pltpu.VMEM(tokens.shape, tokens.dtype), pltpu.SemaphoreType.DMA((parts,))],
    )


def solution(mesh):
    placed = (
        P(("group", "expert"), None),
        P(None, None, ("group", "expert")),
        P(("group", "expert"), None),
        P("group"),
        P("group"),
        P(("group", "expert"), None),
        P(("group", "expert"), None),
        P(("group", "expert"), None),
    )
    return jax.shard_map(
        body, mesh=mesh, in_specs=placed, out_specs=P(("group", "expert"), None), check_vma=False
    )
```

```python
import functools

import jax
import jax.numpy as jnp
from jax import lax
from jax.experimental import pallas as pl
from jax.experimental.pallas import tpu as pltpu
from jax.sharding import PartitionSpec as P

SLOTS = 8
CAP = 4
CHIP_STEPS = ((0, 3, 1, 2), (0, 3, 2, 1))

VMEM = pl.BlockSpec(memory_space=pltpu.VMEM)
HBM = pl.BlockSpec(memory_space=pltpu.HBM)


def targets(shards, new_ref, old_ref, ids, replica):
    slots, rows = new_ref.shape[0], ids.shape[1]
    device = lax.axis_index("expert")
    down = lax.broadcasted_iota(jnp.int32, (slots, rows), 0)
    expert = jnp.zeros((slots, rows), jnp.int32)
    line = jnp.zeros((slots, rows), jnp.int32)
    for slot in range(slots):
        source = jnp.where(new_ref[slot] == old_ref[slot], slot, slot ^ 1)
        away = source ^ (device // shards)
        if shards == 1:
            chip = away >> 1
            even, odd = [
                sum(jnp.where(chip == c, k, 0) for k, c in enumerate(steps)) for steps in CHIP_STEPS
            ]
            away = (source & 1) | (jnp.where((device & 1) == 1, odd, even) << 1)
        expert = jnp.where(down == slot, new_ref[slot], expert)
        line = jnp.where(down == slot, CAP * away, line)
    count = jnp.zeros((slots, rows), jnp.int32)
    rank = jnp.zeros((slots, rows), jnp.int32)
    for slot in range(slots):
        same = expert == new_ref[slot]
        count += jnp.where(same, 1, 0)
        rank += jnp.where(same & (down > slot), 1, 0)
    chosen = []
    for k in range(ids.shape[0]):
        hit = (ids[k : k + 1] == expert) & (rank == (replica[k : k + 1] & (count - 1)))
        chosen.append(jnp.where(hit, 1.0, 0.0))
    earlier = lax.broadcasted_iota(jnp.int32, (rows, rows), 0) < lax.broadcasted_iota(
        jnp.int32, (rows, rows), 1
    )
    any_choice = functools.reduce(jnp.add, chosen)
    position = jnp.dot(
        any_choice.astype(jnp.bfloat16),
        jnp.where(earlier, 1.0, 0.0).astype(jnp.bfloat16),
        preferred_element_type=jnp.float32,
    )
    line = line.astype(jnp.float32)
    found = []
    for hit in chosen:
        place = jnp.where(position < CAP, line + position + 1.0, 0.0)
        found.append((jnp.sum(hit * place, axis=0, keepdims=True) - 1.0).astype(jnp.int32))
        position = position + hit
    return found


def start_copies(sources, buffers, sems):
    copies = [pltpu.make_async_copy(*pair, sems.at[i]) for i, pair in enumerate(zip(sources, buffers))]
    for copy in copies:
        copy.start()
    return copies


def dispatch_kernel(shards, *refs):
    sources, refs = refs[:5], refs[5:]
    found_ref, *block_refs = refs[:-6]
    buffers, sems = refs[-6:-1], refs[-1]
    copies = start_copies(sources, buffers, sems)
    for copy in copies[:-1]:
        copy.wait()
    found = targets(shards, *buffers[:2], *[ref[...] for ref in buffers[2:-1]])
    found_ref[...] = jnp.concatenate(found, axis=0)
    tokens_ref = buffers[-1]
    size = block_refs[0].shape[0]
    line = lax.broadcasted_iota(jnp.int32, (size * len(block_refs), tokens_ref.shape[0]), 0)
    picked = functools.reduce(jnp.logical_or, [line == target for target in found])
    selector = jnp.where(picked, 1.0, 0.0).astype(jnp.bfloat16)
    copies[-1].wait()
    buffer = jnp.dot(selector, tokens_ref[...], preferred_element_type=jnp.float32)
    for b, block_ref in enumerate(block_refs):
        block_ref[...] = buffer[size * b : size * (b + 1)].astype(jnp.bfloat16)


def prepare_kernel(
    found_ref, combine_hbm, in_hbm, down_hbm, in_ref, down_ref, weight_ref, combine_ref, sems
):
    copies = start_copies(
        (combine_hbm, in_hbm, down_hbm), (combine_ref, in_ref, down_ref), sems
    )
    copies[0].wait()
    line = lax.broadcasted_iota(jnp.int32, (weight_ref.shape[1], combine_ref.shape[1]), 0)
    weight = functools.reduce(
        jnp.add,
        [
            jnp.where(line == found_ref[k : k + 1], combine_ref[k : k + 1], 0.0)
            for k in range(found_ref.shape[0])
        ],
    ).T
    high = weight.astype(jnp.bfloat16)
    low = (weight - high.astype(jnp.float32)).astype(jnp.bfloat16)
    weight_ref[...] = jnp.concatenate([high, low], axis=0)
    for copy in copies[1:]:
        copy.wait()


def stack(refs):
    return jnp.concatenate([ref[...].astype(jnp.float32) for ref in refs], axis=0)


def hidden_kernel(split, in_ref, twin_in_ref, *refs):
    *refs, out_ref = refs
    odd = lax.axis_index("expert") & 1
    rows = stack(refs).astype(jnp.bfloat16)
    half_size = refs[0].shape[0] // 2
    hidden = []
    for half, ref in enumerate((in_ref, twin_in_ref)):
        gate = jnp.dot(rows, ref[0], preferred_element_type=jnp.float32)
        up = jnp.dot(rows, ref[1], preferred_element_type=jnp.float32)
        value = jax.nn.silu(gate) * up
        if split:
            place = lax.broadcasted_iota(jnp.int32, value.shape, 0) // half_size
            value = jnp.where((place & 1) == (odd ^ half), value, 0.0)
        hidden.append(value.astype(jnp.bfloat16))
    out_ref[...] = jnp.concatenate(hidden, axis=1)


def down_kernel(hidden_ref, down_ref, twin_down_ref, *refs):
    piece = jnp.dot(
        hidden_ref[...],
        jnp.concatenate([down_ref[...], twin_down_ref[...]], axis=0),
        preferred_element_type=jnp.float32,
    )
    size = refs[0].shape[0]
    for b, out_ref in enumerate(refs):
        out_ref[...] = piece[size * b : size * (b + 1)].astype(jnp.bfloat16)


def mix_kernel(repeats, weight_ref, *refs):
    out_hbm, out_ref, sems = refs[-3:]
    refs = refs[:-3]
    rows, width = out_ref.shape
    parts = sems.shape[0]
    step = width // parts
    copies = []
    for part in range(parts):
        columns = slice(part * step, (part + 1) * step)
        total = functools.reduce(
            jnp.add,
            [stack([ref.at[:, columns] for ref in refs[j::repeats]]) for j in range(repeats)],
        )
        high = total.astype(jnp.bfloat16)
        mixed = jnp.dot(weight_ref[...], high, preferred_element_type=jnp.float32)
        if repeats > 1:
            low = (total - high.astype(jnp.float32)).astype(jnp.bfloat16)
            mixed += jnp.dot(weight_ref[...], low, preferred_element_type=jnp.float32)
        out_ref[:, columns] = (mixed[:rows] + mixed[rows:]).astype(jnp.bfloat16)
        copies.append(
            pltpu.make_async_copy(out_ref.at[:, columns], out_hbm.at[:, columns], sems.at[part])
        )
        copies[-1].start()
    for copy in copies:
        copy.wait()


def call(kernel, outs, args, flops, arg_specs=None, out_specs=None, scratch=()):
    arg_specs = arg_specs or [VMEM] * len(args)
    nbytes = sum(x.size * x.dtype.itemsize for x in jax.tree.leaves((outs, args)))
    return pl.pallas_call(
        kernel,
        out_shape=outs,
        in_specs=arg_specs,
        out_specs=out_specs or jax.tree.map(lambda _: VMEM, outs),
        scratch_shapes=scratch,
        compiler_params=pltpu.CompilerParams(vmem_limit_bytes=16 << 20),
        cost_estimate=pl.CostEstimate(flops=flops, bytes_accessed=nbytes, transcendentals=0),
    )(*[pltpu.with_memory_space_constraint(x, s.memory_space) for x, s in zip(args, arg_specs)])


def shape_of(array):
    return jax.ShapeDtypeStruct(array.shape, array.dtype)


def scratch_for(scalars, arrays):
    return [
        *[pltpu.SMEM(x.shape, x.dtype) for x in scalars],
        *[pltpu.VMEM(x.shape, x.dtype) for x in arrays],
        pltpu.SemaphoreType.DMA((len(scalars) + len(arrays),)),
    ]


def exchange(blocks, split, back=False):
    devices = lax.axis_size("expert")
    result = list(blocks)
    for k in range(1, len(blocks)):
        if split:
            pairs = [(i, i ^ 1 ^ 2 * CHIP_STEPS[i & 1][k]) for i in range(devices)]
        else:
            pairs = [(i, i ^ 2 * k) for i in range(devices)]
        if back:
            pairs = [(target, source) for source, target in pairs]
        result[k] = lax.ppermute(blocks[k], "expert", pairs)
    return result


def from_twin(array):
    pairs = [(i, i ^ 1) for i in range(lax.axis_size("expert"))]
    return lax.ppermute(array, "expert", pairs)


def body(tokens, w_in, w_down, old_place, new_place, expert_ids, replica, combine):
    devices = lax.axis_size("expert")
    shards = devices // SLOTS
    split = shards == 1
    repeats = max(shards // 2, 1)
    chips = devices // 2
    rows, width = tokens.shape
    hidden = w_down.shape[0]
    twin_in = from_twin(w_in)
    operands = (new_place, old_place, expert_ids.T, replica.T, tokens)
    combine = combine.T
    block = jax.ShapeDtypeStruct((CAP * (2 if split else 1), width), jnp.bfloat16)
    found, *blocks = call(
        functools.partial(dispatch_kernel, shards),
        [shape_of(operands[2])] + [block] * (chips // repeats),
        operands,
        2 * SLOTS * CAP * rows * width,
        [HBM] * len(operands),
        scratch=scratch_for(operands[:2], operands[2:]),
    )
    received = exchange([blocks[c // repeats] for c in range(chips)], split)
    twin_down = from_twin(lax.optimization_barrier((w_down, found))[0])
    own_in, own_down, weight = call(
        prepare_kernel,
        [
            shape_of(w_in),
            shape_of(w_down),
            jax.ShapeDtypeStruct((2 * rows, SLOTS * CAP), jnp.bfloat16),
        ],
        (found, combine, w_in, w_down),
        0,
        [VMEM, HBM, HBM, HBM],
        scratch=[pltpu.VMEM(combine.shape, combine.dtype), pltpu.SemaphoreType.DMA((3,))],
    )
    units = call(
        functools.partial(hidden_kernel, split),
        jax.ShapeDtypeStruct((chips * block.shape[0], 2 * hidden), jnp.bfloat16),
        (own_in, twin_in, *received),
        800 * chips * block.shape[0] * hidden * width,
    )
    pieces = call(
        down_kernel,
        [block] * chips,
        (units, own_down, twin_down),
        4 * chips * block.shape[0] * hidden * width,
    )
    returned = exchange(pieces, split, back=True)
    parts = 4 if width % 512 == 0 else 1
    return call(
        functools.partial(mix_kernel, repeats),
        shape_of(tokens),
        (weight, *returned),
        4 * SLOTS * CAP * rows * width,
        out_specs=HBM,
        scratch=[pltpu.VMEM(tokens.shape, tokens.dtype), pltpu.SemaphoreType.DMA((parts,))],
    )


def solution(mesh):
    placed = (
        P(("group", "expert"), None),
        P(None, None, ("group", "expert")),
        P(("group", "expert"), None),
        P("group"),
        P("group"),
        P(("group", "expert"), None),
        P(("group", "expert"), None),
        P(("group", "expert"), None),
    )
    return jax.shard_map(
        body, mesh=mesh, in_specs=placed, out_specs=P(("group", "expert"), None), check_vma=False
    )
```

```python
import functools

import jax
import jax.numpy as jnp
from jax import lax
from jax.experimental import pallas as pl
from jax.experimental.pallas import tpu as pltpu
from jax.sharding import PartitionSpec as P

SLOTS = 8
CAP = 4
CHIP_STEPS = ((0, 3, 1, 2), (0, 3, 2, 1))

VMEM = pl.BlockSpec(memory_space=pltpu.VMEM)
HBM = pl.BlockSpec(memory_space=pltpu.HBM)


def targets(shards, new_ref, old_ref, ids, replica):
    slots, rows = new_ref.shape[0], ids.shape[1]
    device = lax.axis_index("expert")
    down = lax.broadcasted_iota(jnp.int32, (slots, rows), 0)
    expert = jnp.zeros((slots, rows), jnp.int32)
    line = jnp.zeros((slots, rows), jnp.int32)
    for slot in range(slots):
        source = jnp.where(new_ref[slot] == old_ref[slot], slot, slot ^ 1)
        away = source ^ (device // shards)
        if shards == 1:
            chip = away >> 1
            even, odd = [
                sum(jnp.where(chip == c, k, 0) for k, c in enumerate(steps)) for steps in CHIP_STEPS
            ]
            away = (source & 1) | (jnp.where((device & 1) == 1, odd, even) << 1)
        expert = jnp.where(down == slot, new_ref[slot], expert)
        line = jnp.where(down == slot, CAP * away, line)
    count = jnp.zeros((slots, rows), jnp.int32)
    rank = jnp.zeros((slots, rows), jnp.int32)
    for slot in range(slots):
        same = expert == new_ref[slot]
        count += jnp.where(same, 1, 0)
        rank += jnp.where(same & (down > slot), 1, 0)
    chosen = []
    for k in range(ids.shape[0]):
        hit = (ids[k : k + 1] == expert) & (rank == (replica[k : k + 1] & (count - 1)))
        chosen.append(jnp.where(hit, 1.0, 0.0))
    earlier = lax.broadcasted_iota(jnp.int32, (rows, rows), 0) < lax.broadcasted_iota(
        jnp.int32, (rows, rows), 1
    )
    any_choice = functools.reduce(jnp.add, chosen)
    position = jnp.dot(
        any_choice.astype(jnp.bfloat16),
        jnp.where(earlier, 1.0, 0.0).astype(jnp.bfloat16),
        preferred_element_type=jnp.float32,
    )
    line = line.astype(jnp.float32)
    found = []
    for hit in chosen:
        place = jnp.where(position < CAP, line + position + 1.0, 0.0)
        found.append((jnp.sum(hit * place, axis=0, keepdims=True) - 1.0).astype(jnp.int32))
        position = position + hit
    return found


def start_copies(sources, buffers, sems):
    copies = [pltpu.make_async_copy(*pair, sems.at[i]) for i, pair in enumerate(zip(sources, buffers))]
    for copy in copies:
        copy.start()
    return copies


def dispatch_kernel(shards, *refs):
    sources, refs = refs[:5], refs[5:]
    found_ref, *block_refs = refs[:-6]
    buffers, sems = refs[-6:-1], refs[-1]
    copies = start_copies(sources, buffers, sems)
    for copy in copies[:-1]:
        copy.wait()
    found = targets(shards, *buffers[:2], *[ref[...] for ref in buffers[2:-1]])
    found_ref[...] = jnp.concatenate(found, axis=0)
    tokens_ref = buffers[-1]
    size = block_refs[0].shape[0]
    line = lax.broadcasted_iota(jnp.int32, (size * len(block_refs), tokens_ref.shape[0]), 0)
    picked = functools.reduce(jnp.logical_or, [line == target for target in found])
    selector = jnp.where(picked, 1.0, 0.0).astype(jnp.bfloat16)
    copies[-1].wait()
    buffer = jnp.dot(selector, tokens_ref[...], preferred_element_type=jnp.float32)
    for b, block_ref in enumerate(block_refs):
        block_ref[...] = buffer[size * b : size * (b + 1)].astype(jnp.bfloat16)


def prepare_kernel(
    found_ref, combine_hbm, in_hbm, down_hbm, in_ref, down_ref, weight_ref, combine_ref, sems
):
    copies = start_copies(
        (combine_hbm, in_hbm, down_hbm), (combine_ref, in_ref, down_ref), sems
    )
    copies[0].wait()
    line = lax.broadcasted_iota(jnp.int32, (weight_ref.shape[1], combine_ref.shape[1]), 0)
    weight = functools.reduce(
        jnp.add,
        [
            jnp.where(line == found_ref[k : k + 1], combine_ref[k : k + 1], 0.0)
            for k in range(found_ref.shape[0])
        ],
    ).T
    high = weight.astype(jnp.bfloat16)
    low = (weight - high.astype(jnp.float32)).astype(jnp.bfloat16)
    weight_ref[...] = jnp.concatenate([high, low], axis=0)
    for copy in copies[1:]:
        copy.wait()


def stack(refs):
    return jnp.concatenate([ref[...] for ref in refs], axis=0)


def hidden_kernel(split, in_ref, twin_in_ref, *refs):
    *refs, out_ref = refs
    odd = lax.axis_index("expert") & 1
    rows = stack(refs)
    half_size = refs[0].shape[0] // 2
    hidden = []
    for half, ref in enumerate((in_ref, twin_in_ref)):
        gate = jnp.dot(rows, ref[0], preferred_element_type=jnp.float32)
        up = jnp.dot(rows, ref[1], preferred_element_type=jnp.float32)
        value = jax.nn.silu(gate) * up
        if split:
            place = lax.broadcasted_iota(jnp.int32, value.shape, 0) // half_size
            value = jnp.where((place & 1) == (odd ^ half), value, 0.0)
        hidden.append(value.astype(jnp.bfloat16))
    out_ref[...] = jnp.concatenate(hidden, axis=1)


def down_kernel(hidden_ref, down_ref, twin_down_ref, *refs):
    units = down_ref.shape[0]
    own = hidden_ref[:, :units], down_ref[...]
    twin = hidden_ref[:, units:], twin_down_ref[...]
    piece = jnp.dot(*own, preferred_element_type=jnp.float32)
    piece += jnp.dot(*twin, preferred_element_type=jnp.float32)
    size = refs[0].shape[0]
    for b, out_ref in enumerate(refs):
        out_ref[...] = piece[size * b : size * (b + 1)].astype(jnp.bfloat16)


def mix_kernel(repeats, weight_ref, *refs):
    out_hbm, out_ref, sems = refs[-3:]
    refs = refs[:-3]
    rows, width = out_ref.shape
    parts = sems.shape[0]
    step = width // parts
    copies = []
    for part in range(parts):
        columns = slice(part * step, (part + 1) * step)
        pieces = [stack([ref.at[:, columns] for ref in refs[j::repeats]]) for j in range(repeats)]
        if repeats == 1:
            mixed = jnp.dot(weight_ref[...], pieces[0], preferred_element_type=jnp.float32)
        else:
            total = sum(piece.astype(jnp.float32) for piece in pieces)
            high = total.astype(jnp.bfloat16)
            low = (total - high.astype(jnp.float32)).astype(jnp.bfloat16)
            mixed = jnp.dot(weight_ref[...], high, preferred_element_type=jnp.float32)
            mixed += jnp.dot(weight_ref[...], low, preferred_element_type=jnp.float32)
        out_ref[:, columns] = (mixed[:rows] + mixed[rows:]).astype(jnp.bfloat16)
        copies.append(
            pltpu.make_async_copy(out_ref.at[:, columns], out_hbm.at[:, columns], sems.at[part])
        )
        copies[-1].start()
    for copy in copies:
        copy.wait()


def call(kernel, outs, args, flops, arg_specs=None, out_specs=None, scratch=()):
    arg_specs = arg_specs or [VMEM] * len(args)
    nbytes = sum(x.size * x.dtype.itemsize for x in jax.tree.leaves((outs, args)))
    return pl.pallas_call(
        kernel,
        out_shape=outs,
        in_specs=arg_specs,
        out_specs=out_specs or jax.tree.map(lambda _: VMEM, outs),
        scratch_shapes=scratch,
        compiler_params=pltpu.CompilerParams(vmem_limit_bytes=16 << 20),
        cost_estimate=pl.CostEstimate(flops=flops, bytes_accessed=nbytes, transcendentals=0),
    )(*[pltpu.with_memory_space_constraint(x, s.memory_space) for x, s in zip(args, arg_specs)])


def shape_of(array):
    return jax.ShapeDtypeStruct(array.shape, array.dtype)


def scratch_for(scalars, arrays):
    return [
        *[pltpu.SMEM(x.shape, x.dtype) for x in scalars],
        *[pltpu.VMEM(x.shape, x.dtype) for x in arrays],
        pltpu.SemaphoreType.DMA((len(scalars) + len(arrays),)),
    ]


def exchange(blocks, split, back=False):
    devices = lax.axis_size("expert")
    result = list(blocks)
    for k in range(1, len(blocks)):
        if split:
            pairs = [(i, i ^ 1 ^ 2 * CHIP_STEPS[i & 1][k]) for i in range(devices)]
        else:
            pairs = [(i, i ^ 2 * k) for i in range(devices)]
        if back:
            pairs = [(target, source) for source, target in pairs]
        result[k] = lax.ppermute(blocks[k], "expert", pairs)
    return result


def from_twin(array):
    pairs = [(i, i ^ 1) for i in range(lax.axis_size("expert"))]
    return lax.ppermute(array, "expert", pairs)


def body(tokens, w_in, w_down, old_place, new_place, expert_ids, replica, combine):
    devices = lax.axis_size("expert")
    shards = devices // SLOTS
    split = shards == 1
    repeats = max(shards // 2, 1)
    chips = devices // 2
    rows, width = tokens.shape
    hidden = w_down.shape[0]
    twin_in = from_twin(w_in)
    operands = (new_place, old_place, expert_ids.T, replica.T, tokens)
    combine = combine.T
    block = jax.ShapeDtypeStruct((CAP * (2 if split else 1), width), jnp.bfloat16)
    found, *blocks = call(
        functools.partial(dispatch_kernel, shards),
        [shape_of(operands[2])] + [block] * (chips // repeats),
        operands,
        2 * SLOTS * CAP * rows * width,
        [HBM] * len(operands),
        scratch=scratch_for(operands[:2], operands[2:]),
    )
    received = exchange([blocks[c // repeats] for c in range(chips)], split)
    twin_down = from_twin(lax.optimization_barrier((w_down, found))[0])
    own_in, own_down, weight = call(
        prepare_kernel,
        [
            shape_of(w_in),
            shape_of(w_down),
            jax.ShapeDtypeStruct((2 * rows, SLOTS * CAP), jnp.bfloat16),
        ],
        (found, combine, w_in, w_down),
        0,
        [VMEM, HBM, HBM, HBM],
        scratch=[pltpu.VMEM(combine.shape, combine.dtype), pltpu.SemaphoreType.DMA((3,))],
    )
    units = call(
        functools.partial(hidden_kernel, split),
        jax.ShapeDtypeStruct((chips * block.shape[0], 2 * hidden), jnp.bfloat16),
        (own_in, twin_in, *received),
        800 * chips * block.shape[0] * hidden * width,
    )
    pieces = call(
        down_kernel,
        [block] * chips,
        (units, own_down, twin_down),
        4 * chips * block.shape[0] * hidden * width,
    )
    returned = exchange(pieces, split, back=True)
    parts = 4 if width % 512 == 0 else 1
    return call(
        functools.partial(mix_kernel, repeats),
        shape_of(tokens),
        (weight, *returned),
        4 * SLOTS * CAP * rows * width,
        out_specs=HBM,
        scratch=[pltpu.VMEM(tokens.shape, tokens.dtype), pltpu.SemaphoreType.DMA((parts,))],
    )


def solution(mesh):
    placed = (
        P(("group", "expert"), None),
        P(None, None, ("group", "expert")),
        P(("group", "expert"), None),
        P("group"),
        P("group"),
        P(("group", "expert"), None),
        P(("group", "expert"), None),
        P(("group", "expert"), None),
    )
    return jax.shard_map(
        body, mesh=mesh, in_specs=placed, out_specs=P(("group", "expert"), None), check_vma=False
    )
```

```python
import functools

import jax
import jax.numpy as jnp
from jax import lax
from jax.experimental import pallas as pl
from jax.experimental.pallas import tpu as pltpu
from jax.sharding import PartitionSpec as P

SLOTS = 8
CAP = 4
CHIP_STEPS = ((0, 3, 1, 2), (0, 3, 1, 2))

VMEM = pl.BlockSpec(memory_space=pltpu.VMEM)
HBM = pl.BlockSpec(memory_space=pltpu.HBM)


def targets(shards, new_ref, old_ref, ids, replica):
    slots, rows = new_ref.shape[0], ids.shape[1]
    device = lax.axis_index("expert")
    down = lax.broadcasted_iota(jnp.int32, (slots, rows), 0)
    expert = jnp.zeros((slots, rows), jnp.int32)
    line = jnp.zeros((slots, rows), jnp.int32)
    for slot in range(slots):
        source = jnp.where(new_ref[slot] == old_ref[slot], slot, slot ^ 1)
        away = source ^ (device // shards)
        if shards == 1:
            chip = away >> 1
            even, odd = [
                sum(jnp.where(chip == c, k, 0) for k, c in enumerate(steps)) for steps in CHIP_STEPS
            ]
            away = (source & 1) | (jnp.where((device & 1) == 1, odd, even) << 1)
        expert = jnp.where(down == slot, new_ref[slot], expert)
        line = jnp.where(down == slot, CAP * away, line)
    count = jnp.zeros((slots, rows), jnp.int32)
    rank = jnp.zeros((slots, rows), jnp.int32)
    for slot in range(slots):
        same = expert == new_ref[slot]
        count += jnp.where(same, 1, 0)
        rank += jnp.where(same & (down > slot), 1, 0)
    chosen = []
    for k in range(ids.shape[0]):
        hit = (ids[k : k + 1] == expert) & (rank == (replica[k : k + 1] & (count - 1)))
        chosen.append(jnp.where(hit, 1.0, 0.0))
    earlier = lax.broadcasted_iota(jnp.int32, (rows, rows), 0) < lax.broadcasted_iota(
        jnp.int32, (rows, rows), 1
    )
    any_choice = functools.reduce(jnp.add, chosen)
    position = jnp.dot(
        any_choice.astype(jnp.bfloat16),
        jnp.where(earlier, 1.0, 0.0).astype(jnp.bfloat16),
        preferred_element_type=jnp.float32,
    )
    line = line.astype(jnp.float32)
    found = []
    for hit in chosen:
        place = jnp.where(position < CAP, line + position + 1.0, 0.0)
        found.append((jnp.sum(hit * place, axis=0, keepdims=True) - 1.0).astype(jnp.int32))
        position = position + hit
    return found


def start_copies(sources, buffers, sems):
    copies = [pltpu.make_async_copy(*pair, sems.at[i]) for i, pair in enumerate(zip(sources, buffers))]
    for copy in copies:
        copy.start()
    return copies


def dispatch_kernel(shards, *refs):
    sources, refs = refs[:5], refs[5:]
    found_ref, *block_refs = refs[:-6]
    buffers, sems = refs[-6:-1], refs[-1]
    copies = start_copies(sources, buffers, sems)
    for copy in copies[:-1]:
        copy.wait()
    found = targets(shards, *buffers[:2], *[ref[...] for ref in buffers[2:-1]])
    found_ref[...] = jnp.concatenate(found, axis=0)
    tokens_ref = buffers[-1]
    size = block_refs[0].shape[0]
    line = lax.broadcasted_iota(jnp.int32, (size * len(block_refs), tokens_ref.shape[0]), 0)
    picked = functools.reduce(jnp.logical_or, [line == target for target in found])
    selector = jnp.where(picked, 1.0, 0.0).astype(jnp.bfloat16)
    copies[-1].wait()
    buffer = jnp.dot(selector, tokens_ref[...], preferred_element_type=jnp.float32)
    for b, block_ref in enumerate(block_refs):
        block_ref[...] = buffer[size * b : size * (b + 1)].astype(jnp.bfloat16)


def prepare_kernel(
    found_ref, combine_hbm, in_hbm, down_hbm, in_ref, down_ref, weight_ref, combine_ref, sems
):
    copies = start_copies(
        (combine_hbm, in_hbm, down_hbm), (combine_ref, in_ref, down_ref), sems
    )
    copies[0].wait()
    line = lax.broadcasted_iota(jnp.int32, (weight_ref.shape[1], combine_ref.shape[1]), 0)
    weight = functools.reduce(
        jnp.add,
        [
            jnp.where(line == found_ref[k : k + 1], combine_ref[k : k + 1], 0.0)
            for k in range(found_ref.shape[0])
        ],
    ).T
    high = weight.astype(jnp.bfloat16)
    low = (weight - high.astype(jnp.float32)).astype(jnp.bfloat16)
    weight_ref[...] = jnp.concatenate([high, low], axis=0)
    for copy in copies[1:]:
        copy.wait()


def stack(refs):
    return jnp.concatenate([ref[...] for ref in refs], axis=0)


def hidden_kernel(split, in_ref, twin_in_ref, *refs):
    *refs, out_ref = refs
    odd = lax.axis_index("expert") & 1
    rows = stack(refs)
    half_size = refs[0].shape[0] // 2
    hidden = []
    for half, ref in enumerate((in_ref, twin_in_ref)):
        gate = jnp.dot(rows, ref[0], preferred_element_type=jnp.float32)
        up = jnp.dot(rows, ref[1], preferred_element_type=jnp.float32)
        value = jax.nn.silu(gate) * up
        if split:
            place = lax.broadcasted_iota(jnp.int32, value.shape, 0) // half_size
            value = jnp.where((place & 1) == (odd ^ half), value, 0.0)
        hidden.append(value.astype(jnp.bfloat16))
    out_ref[...] = jnp.concatenate(hidden, axis=1)


def down_kernel(hidden_ref, down_ref, twin_down_ref, *refs):
    units = down_ref.shape[0]
    own = hidden_ref[:, :units], down_ref[...]
    twin = hidden_ref[:, units:], twin_down_ref[...]
    piece = jnp.dot(*own, preferred_element_type=jnp.float32)
    piece += jnp.dot(*twin, preferred_element_type=jnp.float32)
    size = refs[0].shape[0]
    for b, out_ref in enumerate(refs):
        out_ref[...] = piece[size * b : size * (b + 1)].astype(jnp.bfloat16)


def mix_kernel(repeats, weight_ref, *refs):
    out_hbm, out_ref, sems = refs[-3:]
    refs = refs[:-3]
    rows, width = out_ref.shape
    parts = sems.shape[0]
    step = width // parts
    copies = []
    for part in range(parts):
        columns = slice(part * step, (part + 1) * step)
        pieces = [stack([ref.at[:, columns] for ref in refs[j::repeats]]) for j in range(repeats)]
        if repeats == 1:
            mixed = jnp.dot(weight_ref[...], pieces[0], preferred_element_type=jnp.float32)
        else:
            total = sum(piece.astype(jnp.float32) for piece in pieces)
            high = total.astype(jnp.bfloat16)
            low = (total - high.astype(jnp.float32)).astype(jnp.bfloat16)
            mixed = jnp.dot(weight_ref[...], high, preferred_element_type=jnp.float32)
            mixed += jnp.dot(weight_ref[...], low, preferred_element_type=jnp.float32)
        out_ref[:, columns] = (mixed[:rows] + mixed[rows:]).astype(jnp.bfloat16)
        copies.append(
            pltpu.make_async_copy(out_ref.at[:, columns], out_hbm.at[:, columns], sems.at[part])
        )
        copies[-1].start()
    for copy in copies:
        copy.wait()


def call(kernel, outs, args, flops, arg_specs=None, out_specs=None, scratch=()):
    arg_specs = arg_specs or [VMEM] * len(args)
    nbytes = sum(x.size * x.dtype.itemsize for x in jax.tree.leaves((outs, args)))
    return pl.pallas_call(
        kernel,
        out_shape=outs,
        in_specs=arg_specs,
        out_specs=out_specs or jax.tree.map(lambda _: VMEM, outs),
        scratch_shapes=scratch,
        compiler_params=pltpu.CompilerParams(vmem_limit_bytes=16 << 20),
        cost_estimate=pl.CostEstimate(flops=flops, bytes_accessed=nbytes, transcendentals=0),
    )(*[pltpu.with_memory_space_constraint(x, s.memory_space) for x, s in zip(args, arg_specs)])


def shape_of(array):
    return jax.ShapeDtypeStruct(array.shape, array.dtype)


def scratch_for(scalars, arrays):
    return [
        *[pltpu.SMEM(x.shape, x.dtype) for x in scalars],
        *[pltpu.VMEM(x.shape, x.dtype) for x in arrays],
        pltpu.SemaphoreType.DMA((len(scalars) + len(arrays),)),
    ]


def exchange(blocks, split, back=False):
    devices = lax.axis_size("expert")
    result = list(blocks)
    for k in range(1, len(blocks)):
        if split:
            pairs = [(i, i ^ 1 ^ 2 * CHIP_STEPS[i & 1][k]) for i in range(devices)]
        else:
            pairs = [(i, i ^ 2 * k) for i in range(devices)]
        if back:
            pairs = [(target, source) for source, target in pairs]
        result[k] = lax.ppermute(blocks[k], "expert", pairs)
    return result


def from_twin(array):
    pairs = [(i, i ^ 1) for i in range(lax.axis_size("expert"))]
    return lax.ppermute(array, "expert", pairs)


def body(tokens, w_in, w_down, old_place, new_place, expert_ids, replica, combine):
    devices = lax.axis_size("expert")
    shards = devices // SLOTS
    split = shards == 1
    repeats = max(shards // 2, 1)
    chips = devices // 2
    rows, width = tokens.shape
    hidden = w_down.shape[0]
    twin_in = from_twin(w_in)
    operands = (new_place, old_place, expert_ids.T, replica.T, tokens)
    combine = combine.T
    block = jax.ShapeDtypeStruct((CAP * (2 if split else 1), width), jnp.bfloat16)
    found, *blocks = call(
        functools.partial(dispatch_kernel, shards),
        [shape_of(operands[2])] + [block] * (chips // repeats),
        operands,
        2 * SLOTS * CAP * rows * width,
        [HBM] * len(operands),
        scratch=scratch_for(operands[:2], operands[2:]),
    )
    received = exchange([blocks[c // repeats] for c in range(chips)], split)
    twin_down = from_twin(lax.optimization_barrier((w_down, found))[0])
    own_in, own_down, weight = call(
        prepare_kernel,
        [
            shape_of(w_in),
            shape_of(w_down),
            jax.ShapeDtypeStruct((2 * rows, SLOTS * CAP), jnp.bfloat16),
        ],
        (found, combine, w_in, w_down),
        0,
        [VMEM, HBM, HBM, HBM],
        scratch=[pltpu.VMEM(combine.shape, combine.dtype), pltpu.SemaphoreType.DMA((3,))],
    )
    units = call(
        functools.partial(hidden_kernel, split),
        jax.ShapeDtypeStruct((chips * block.shape[0], 2 * hidden), jnp.bfloat16),
        (own_in, twin_in, *received),
        800 * chips * block.shape[0] * hidden * width,
    )
    pieces = call(
        down_kernel,
        [block] * chips,
        (units, own_down, twin_down),
        4 * chips * block.shape[0] * hidden * width,
    )
    returned = exchange(pieces, split, back=True)
    parts = 4 if width % 512 == 0 else 1
    return call(
        functools.partial(mix_kernel, repeats),
        shape_of(tokens),
        (weight, *returned),
        4 * SLOTS * CAP * rows * width,
        out_specs=HBM,
        scratch=[pltpu.VMEM(tokens.shape, tokens.dtype), pltpu.SemaphoreType.DMA((parts,))],
    )


def solution(mesh):
    placed = (
        P(("group", "expert"), None),
        P(None, None, ("group", "expert")),
        P(("group", "expert"), None),
        P("group"),
        P("group"),
        P(("group", "expert"), None),
        P(("group", "expert"), None),
        P(("group", "expert"), None),
    )
    return jax.shard_map(
        body, mesh=mesh, in_specs=placed, out_specs=P(("group", "expert"), None), check_vma=False
    )
```

```python
import functools

import jax
import jax.numpy as jnp
from jax import lax
from jax.experimental import pallas as pl
from jax.experimental.pallas import tpu as pltpu
from jax.sharding import PartitionSpec as P

SLOTS = 8
CAP = 4
CHIP_STEPS = ((0, 3, 1, 2), (0, 3, 2, 1))

VMEM = pl.BlockSpec(memory_space=pltpu.VMEM)
HBM = pl.BlockSpec(memory_space=pltpu.HBM)


def targets(shards, new_ref, old_ref, ids, replica):
    slots, rows = new_ref.shape[0], ids.shape[1]
    device = lax.axis_index("expert")
    down = lax.broadcasted_iota(jnp.int32, (slots, rows), 0)
    expert = jnp.zeros((slots, rows), jnp.int32)
    line = jnp.zeros((slots, rows), jnp.int32)
    for slot in range(slots):
        source = jnp.where(new_ref[slot] == old_ref[slot], slot, slot ^ 1)
        away = source ^ (device // shards)
        if shards == 1:
            chip = away >> 1
            even, odd = [
                sum(jnp.where(chip == c, k, 0) for k, c in enumerate(steps)) for steps in CHIP_STEPS
            ]
            away = (source & 1) | (jnp.where((device & 1) == 1, odd, even) << 1)
        expert = jnp.where(down == slot, new_ref[slot], expert)
        line = jnp.where(down == slot, CAP * away, line)
    count = jnp.zeros((slots, rows), jnp.int32)
    rank = jnp.zeros((slots, rows), jnp.int32)
    for slot in range(slots):
        same = expert == new_ref[slot]
        count += jnp.where(same, 1, 0)
        rank += jnp.where(same & (down > slot), 1, 0)
    chosen = []
    for k in range(ids.shape[0]):
        hit = (ids[k : k + 1] == expert) & (rank == (replica[k : k + 1] & (count - 1)))
        chosen.append(jnp.where(hit, 1.0, 0.0))
    earlier = lax.broadcasted_iota(jnp.int32, (rows, rows), 0) < lax.broadcasted_iota(
        jnp.int32, (rows, rows), 1
    )
    any_choice = functools.reduce(jnp.add, chosen)
    position = jnp.dot(
        any_choice.astype(jnp.bfloat16),
        jnp.where(earlier, 1.0, 0.0).astype(jnp.bfloat16),
        preferred_element_type=jnp.float32,
    )
    line = line.astype(jnp.float32)
    found = []
    for hit in chosen:
        place = jnp.where(position < CAP, line + position + 1.0, 0.0)
        found.append((jnp.sum(hit * place, axis=0, keepdims=True) - 1.0).astype(jnp.int32))
        position = position + hit
    return found


def start_copies(sources, buffers, sems):
    copies = [pltpu.make_async_copy(*pair, sems.at[i]) for i, pair in enumerate(zip(sources, buffers))]
    for copy in copies:
        copy.start()
    return copies


def dispatch_kernel(shards, *refs):
    sources, refs = refs[:5], refs[5:]
    found_ref, *block_refs = refs[:-6]
    buffers, sems = refs[-6:-1], refs[-1]
    copies = start_copies(sources, buffers, sems)
    for copy in copies[:-1]:
        copy.wait()
    found = targets(shards, *buffers[:2], *[ref[...] for ref in buffers[2:-1]])
    found_ref[...] = jnp.concatenate(found, axis=0)
    tokens_ref = buffers[-1]
    size = block_refs[0].shape[0]
    line = lax.broadcasted_iota(jnp.int32, (size * len(block_refs), tokens_ref.shape[0]), 0)
    picked = functools.reduce(jnp.logical_or, [line == target for target in found])
    selector = jnp.where(picked, 1.0, 0.0).astype(jnp.bfloat16)
    copies[-1].wait()
    buffer = jnp.dot(selector, tokens_ref[...], preferred_element_type=jnp.float32)
    for b, block_ref in enumerate(block_refs):
        block_ref[...] = buffer[size * b : size * (b + 1)].astype(jnp.bfloat16)


def prepare_kernel(
    found_ref, combine_hbm, in_hbm, down_hbm, in_ref, down_ref, weight_ref, combine_ref, sems
):
    copies = start_copies(
        (combine_hbm, in_hbm, down_hbm), (combine_ref, in_ref, down_ref), sems
    )
    copies[0].wait()
    line = lax.broadcasted_iota(jnp.int32, (weight_ref.shape[1], combine_ref.shape[1]), 0)
    weight = functools.reduce(
        jnp.add,
        [
            jnp.where(line == found_ref[k : k + 1], combine_ref[k : k + 1], 0.0)
            for k in range(found_ref.shape[0])
        ],
    ).T
    high = weight.astype(jnp.bfloat16)
    low = (weight - high.astype(jnp.float32)).astype(jnp.bfloat16)
    weight_ref[...] = jnp.concatenate([high, low], axis=0)
    for copy in copies[1:]:
        copy.wait()


def stack(refs):
    return jnp.concatenate([ref[...] for ref in refs], axis=0)


def hidden_kernel(split, in_ref, twin_in_ref, *refs):
    *refs, out_ref = refs
    odd = lax.axis_index("expert") & 1
    rows = stack(refs)
    half_size = refs[0].shape[0] // 2
    hidden = []
    for half, ref in enumerate((in_ref, twin_in_ref)):
        gate = jnp.dot(rows, ref[0], preferred_element_type=jnp.float32)
        up = jnp.dot(rows, ref[1], preferred_element_type=jnp.float32)
        value = jax.nn.silu(gate) * up
        if split:
            place = lax.broadcasted_iota(jnp.int32, value.shape, 0) // half_size
            value = jnp.where((place & 1) == (odd ^ half), value, 0.0)
        hidden.append(value.astype(jnp.bfloat16))
    out_ref[...] = jnp.concatenate(hidden, axis=1)


def down_kernel(hidden_ref, down_ref, twin_down_ref, *refs):
    units = down_ref.shape[0]
    own = hidden_ref[:, :units], down_ref[...]
    twin = hidden_ref[:, units:], twin_down_ref[...]
    piece = jnp.dot(*own, preferred_element_type=jnp.float32)
    piece += jnp.dot(*twin, preferred_element_type=jnp.float32)
    size = refs[0].shape[0]
    for b, out_ref in enumerate(refs):
        out_ref[...] = piece[size * b : size * (b + 1)].astype(jnp.bfloat16)


def mix_kernel(repeats, order, weight_ref, *refs):
    out_hbm, out_ref, sems = refs[-3:]
    refs = [ref for _, ref in sorted(zip(order, refs[:-3]), key=lambda pair: pair[0])]
    rows, width = out_ref.shape
    parts = sems.shape[0]
    step = width // parts
    copies = []
    for part in range(parts):
        columns = slice(part * step, (part + 1) * step)
        pieces = [stack([ref.at[:, columns] for ref in refs[j::repeats]]) for j in range(repeats)]
        if repeats == 1:
            mixed = jnp.dot(weight_ref[...], pieces[0], preferred_element_type=jnp.float32)
        else:
            total = sum(piece.astype(jnp.float32) for piece in pieces)
            high = total.astype(jnp.bfloat16)
            low = (total - high.astype(jnp.float32)).astype(jnp.bfloat16)
            mixed = jnp.dot(weight_ref[...], high, preferred_element_type=jnp.float32)
            mixed += jnp.dot(weight_ref[...], low, preferred_element_type=jnp.float32)
        out_ref[:, columns] = (mixed[:rows] + mixed[rows:]).astype(jnp.bfloat16)
        copies.append(
            pltpu.make_async_copy(out_ref.at[:, columns], out_hbm.at[:, columns], sems.at[part])
        )
        copies[-1].start()
    for copy in copies:
        copy.wait()


def call(kernel, outs, args, flops, arg_specs=None, out_specs=None, scratch=()):
    arg_specs = arg_specs or [VMEM] * len(args)
    nbytes = sum(x.size * x.dtype.itemsize for x in jax.tree.leaves((outs, args)))
    return pl.pallas_call(
        kernel,
        out_shape=outs,
        in_specs=arg_specs,
        out_specs=out_specs or jax.tree.map(lambda _: VMEM, outs),
        scratch_shapes=scratch,
        compiler_params=pltpu.CompilerParams(vmem_limit_bytes=16 << 20),
        cost_estimate=pl.CostEstimate(flops=flops, bytes_accessed=nbytes, transcendentals=0),
    )(*[pltpu.with_memory_space_constraint(x, s.memory_space) for x, s in zip(args, arg_specs)])


def shape_of(array):
    return jax.ShapeDtypeStruct(array.shape, array.dtype)


def scratch_for(scalars, arrays):
    return [
        *[pltpu.SMEM(x.shape, x.dtype) for x in scalars],
        *[pltpu.VMEM(x.shape, x.dtype) for x in arrays],
        pltpu.SemaphoreType.DMA((len(scalars) + len(arrays),)),
    ]


def exchange(blocks, split, back=False):
    devices = lax.axis_size("expert")
    steps = {}
    for k in range(1, len(blocks)):
        if split:
            steps[k] = [(i, i ^ 1 ^ 2 * CHIP_STEPS[i & 1][k]) for i in range(devices)]
        else:
            steps[k] = [(i, i ^ 2 * k) for i in range(devices)]
    result = {0: blocks[0]}
    for k, pairs in steps.items():
        came = sorted((target, source) for source, target in pairs)
        block = next(m for m in steps if steps[m] == came) if back else k
        result[block] = lax.ppermute(blocks[block], "expert", pairs)
    return result


def from_twin(array):
    pairs = [(i, i ^ 1) for i in range(lax.axis_size("expert"))]
    return lax.ppermute(array, "expert", pairs)


def body(tokens, w_in, w_down, old_place, new_place, expert_ids, replica, combine):
    devices = lax.axis_size("expert")
    shards = devices // SLOTS
    split = shards == 1
    repeats = max(shards // 2, 1)
    chips = devices // 2
    rows, width = tokens.shape
    hidden = w_down.shape[0]
    twin_in = from_twin(w_in)
    operands = (new_place, old_place, expert_ids.T, replica.T, tokens)
    combine = combine.T
    block = jax.ShapeDtypeStruct((CAP * (2 if split else 1), width), jnp.bfloat16)
    found, *blocks = call(
        functools.partial(dispatch_kernel, shards),
        [shape_of(operands[2])] + [block] * (chips // repeats),
        operands,
        2 * SLOTS * CAP * rows * width,
        [HBM] * len(operands),
        scratch=scratch_for(operands[:2], operands[2:]),
    )
    received = exchange([blocks[c // repeats] for c in range(chips)], split)
    twin_down = from_twin(lax.optimization_barrier((w_down, found))[0])
    own_in, own_down, weight = call(
        prepare_kernel,
        [
            shape_of(w_in),
            shape_of(w_down),
            jax.ShapeDtypeStruct((2 * rows, SLOTS * CAP), jnp.bfloat16),
        ],
        (found, combine, w_in, w_down),
        0,
        [VMEM, HBM, HBM, HBM],
        scratch=[pltpu.VMEM(combine.shape, combine.dtype), pltpu.SemaphoreType.DMA((3,))],
    )
    units = call(
        functools.partial(hidden_kernel, split),
        jax.ShapeDtypeStruct((chips * block.shape[0], 2 * hidden), jnp.bfloat16),
        (own_in, twin_in, *received.values()),
        800 * chips * block.shape[0] * hidden * width,
    )
    pieces = call(
        down_kernel,
        [block] * chips,
        (units, own_down, twin_down),
        4 * chips * block.shape[0] * hidden * width,
    )
    returned = exchange(pieces, split, back=True)
    parts = 4 if width % 512 == 0 else 1
    return call(
        functools.partial(mix_kernel, repeats, tuple(returned)),
        shape_of(tokens),
        (weight, *returned.values()),
        4 * SLOTS * CAP * rows * width,
        out_specs=HBM,
        scratch=[pltpu.VMEM(tokens.shape, tokens.dtype), pltpu.SemaphoreType.DMA((parts,))],
    )


def solution(mesh):
    placed = (
        P(("group", "expert"), None),
        P(None, None, ("group", "expert")),
        P(("group", "expert"), None),
        P("group"),
        P("group"),
        P(("group", "expert"), None),
        P(("group", "expert"), None),
        P(("group", "expert"), None),
    )
    return jax.shard_map(
        body, mesh=mesh, in_specs=placed, out_specs=P(("group", "expert"), None), check_vma=False
    )
```

```python
import functools

import jax
import jax.numpy as jnp
from jax import lax
from jax.experimental import pallas as pl
from jax.experimental.pallas import tpu as pltpu
from jax.sharding import PartitionSpec as P

SLOTS = 8
CAP = 4
CHIP_STEPS = ((0, 3, 1, 2), (0, 3, 2, 1))

VMEM = pl.BlockSpec(memory_space=pltpu.VMEM)
HBM = pl.BlockSpec(memory_space=pltpu.HBM)


def targets(shards, new_ref, old_ref, ids, replica):
    slots, rows = new_ref.shape[0], ids.shape[1]
    device = lax.axis_index("expert")
    down = lax.broadcasted_iota(jnp.int32, (slots, rows), 0)
    expert = jnp.zeros((slots, rows), jnp.int32)
    line = jnp.zeros((slots, rows), jnp.int32)
    for slot in range(slots):
        source = jnp.where(new_ref[slot] == old_ref[slot], slot, slot ^ 1)
        away = source ^ (device // shards)
        if shards == 1:
            chip = away >> 1
            even, odd = [
                sum(jnp.where(chip == c, k, 0) for k, c in enumerate(steps)) for steps in CHIP_STEPS
            ]
            away = (source & 1) | (jnp.where((device & 1) == 1, odd, even) << 1)
        expert = jnp.where(down == slot, new_ref[slot], expert)
        line = jnp.where(down == slot, CAP * away, line)
    count = jnp.zeros((slots, rows), jnp.int32)
    rank = jnp.zeros((slots, rows), jnp.int32)
    for slot in range(slots):
        same = expert == new_ref[slot]
        count += jnp.where(same, 1, 0)
        rank += jnp.where(same & (down > slot), 1, 0)
    chosen = []
    for k in range(ids.shape[0]):
        hit = (ids[k : k + 1] == expert) & (rank == (replica[k : k + 1] & (count - 1)))
        chosen.append(jnp.where(hit, 1.0, 0.0))
    earlier = lax.broadcasted_iota(jnp.int32, (rows, rows), 0) < lax.broadcasted_iota(
        jnp.int32, (rows, rows), 1
    )
    any_choice = functools.reduce(jnp.add, chosen)
    position = jnp.dot(
        any_choice.astype(jnp.bfloat16),
        jnp.where(earlier, 1.0, 0.0).astype(jnp.bfloat16),
        preferred_element_type=jnp.float32,
    )
    line = line.astype(jnp.float32)
    found = []
    for hit in chosen:
        place = jnp.where(position < CAP, line + position + 1.0, 0.0)
        found.append((jnp.sum(hit * place, axis=0, keepdims=True) - 1.0).astype(jnp.int32))
        position = position + hit
    return found


def start_copies(sources, buffers, sems):
    copies = [pltpu.make_async_copy(*pair, sems.at[i]) for i, pair in enumerate(zip(sources, buffers))]
    for copy in copies:
        copy.start()
    return copies


def dispatch_kernel(shards, *refs):
    sources, refs = refs[:5], refs[5:]
    found_ref, *block_refs = refs[:-6]
    buffers, sems = refs[-6:-1], refs[-1]
    copies = start_copies(sources, buffers, sems)
    for copy in copies[:-1]:
        copy.wait()
    found = targets(shards, *buffers[:2], *[ref[...] for ref in buffers[2:-1]])
    found_ref[...] = jnp.concatenate(found, axis=0)
    tokens_ref = buffers[-1]
    size = block_refs[0].shape[0]
    line = lax.broadcasted_iota(jnp.int32, (size * len(block_refs), tokens_ref.shape[0]), 0)
    picked = functools.reduce(jnp.logical_or, [line == target for target in found])
    selector = jnp.where(picked, 1.0, 0.0).astype(jnp.bfloat16)
    copies[-1].wait()
    buffer = jnp.dot(selector, tokens_ref[...], preferred_element_type=jnp.float32)
    for b, block_ref in enumerate(block_refs):
        block_ref[...] = buffer[size * b : size * (b + 1)].astype(jnp.bfloat16)


def prepare_kernel(
    found_ref, combine_hbm, in_hbm, down_hbm, in_ref, down_ref, weight_ref, combine_ref, sems
):
    copies = start_copies(
        (combine_hbm, in_hbm, down_hbm), (combine_ref, in_ref, down_ref), sems
    )
    copies[0].wait()
    line = lax.broadcasted_iota(jnp.int32, (weight_ref.shape[1], combine_ref.shape[1]), 0)
    weight = functools.reduce(
        jnp.add,
        [
            jnp.where(line == found_ref[k : k + 1], combine_ref[k : k + 1], 0.0)
            for k in range(found_ref.shape[0])
        ],
    ).T
    high = weight.astype(jnp.bfloat16)
    low = (weight - high.astype(jnp.float32)).astype(jnp.bfloat16)
    weight_ref[...] = jnp.concatenate([high, low], axis=0)
    for copy in copies[1:]:
        copy.wait()


def stack(refs):
    return jnp.concatenate([ref[...] for ref in refs], axis=0)


def hidden_kernel(split, in_ref, twin_in_ref, *refs):
    *refs, out_ref = refs
    odd = lax.axis_index("expert") & 1
    rows = stack(refs)
    half_size = refs[0].shape[0] // 2
    middle = rows.shape[1] // 256 * 128
    hidden = []
    for half, ref in enumerate((in_ref, twin_in_ref)):
        gate, up = [
            sum(
                jnp.dot(rows[:, part], ref[g, part], preferred_element_type=jnp.float32)
                for part in (slice(0, middle), slice(middle, None))
            )
            for g in range(2)
        ]
        value = jax.nn.silu(gate) * up
        if split:
            place = lax.broadcasted_iota(jnp.int32, value.shape, 0) // half_size
            value = jnp.where((place & 1) == (odd ^ half), value, 0.0)
        hidden.append(value.astype(jnp.bfloat16))
    out_ref[...] = jnp.concatenate(hidden, axis=1)


def down_kernel(hidden_ref, down_ref, twin_down_ref, *refs):
    units = down_ref.shape[0]
    own = hidden_ref[:, :units], down_ref[...]
    twin = hidden_ref[:, units:], twin_down_ref[...]
    piece = jnp.dot(*own, preferred_element_type=jnp.float32)
    piece += jnp.dot(*twin, preferred_element_type=jnp.float32)
    size = refs[0].shape[0]
    for b, out_ref in enumerate(refs):
        out_ref[...] = piece[size * b : size * (b + 1)].astype(jnp.bfloat16)


def mix_kernel(repeats, order, weight_ref, *refs):
    out_hbm, out_ref, sems = refs[-3:]
    refs = [ref for _, ref in sorted(zip(order, refs[:-3]), key=lambda pair: pair[0])]
    rows, width = out_ref.shape
    parts = sems.shape[0]
    step = width // parts
    copies = []
    for part in range(parts):
        columns = slice(part * step, (part + 1) * step)
        pieces = [stack([ref.at[:, columns] for ref in refs[j::repeats]]) for j in range(repeats)]
        if repeats == 1:
            mixed = jnp.dot(weight_ref[...], pieces[0], preferred_element_type=jnp.float32)
        else:
            total = sum(piece.astype(jnp.float32) for piece in pieces)
            high = total.astype(jnp.bfloat16)
            low = (total - high.astype(jnp.float32)).astype(jnp.bfloat16)
            mixed = jnp.dot(weight_ref[...], high, preferred_element_type=jnp.float32)
            mixed += jnp.dot(weight_ref[...], low, preferred_element_type=jnp.float32)
        out_ref[:, columns] = (mixed[:rows] + mixed[rows:]).astype(jnp.bfloat16)
        copies.append(
            pltpu.make_async_copy(out_ref.at[:, columns], out_hbm.at[:, columns], sems.at[part])
        )
        copies[-1].start()
    for copy in copies:
        copy.wait()


def call(kernel, outs, args, flops, arg_specs=None, out_specs=None, scratch=()):
    arg_specs = arg_specs or [VMEM] * len(args)
    nbytes = sum(x.size * x.dtype.itemsize for x in jax.tree.leaves((outs, args)))
    return pl.pallas_call(
        kernel,
        out_shape=outs,
        in_specs=arg_specs,
        out_specs=out_specs or jax.tree.map(lambda _: VMEM, outs),
        scratch_shapes=scratch,
        compiler_params=pltpu.CompilerParams(vmem_limit_bytes=16 << 20),
        cost_estimate=pl.CostEstimate(flops=flops, bytes_accessed=nbytes, transcendentals=0),
    )(*[pltpu.with_memory_space_constraint(x, s.memory_space) for x, s in zip(args, arg_specs)])


def shape_of(array):
    return jax.ShapeDtypeStruct(array.shape, array.dtype)


def scratch_for(scalars, arrays):
    return [
        *[pltpu.SMEM(x.shape, x.dtype) for x in scalars],
        *[pltpu.VMEM(x.shape, x.dtype) for x in arrays],
        pltpu.SemaphoreType.DMA((len(scalars) + len(arrays),)),
    ]


def exchange(blocks, split, back=False):
    devices = lax.axis_size("expert")
    steps = {}
    for k in range(1, len(blocks)):
        if split:
            steps[k] = [(i, i ^ 1 ^ 2 * CHIP_STEPS[i & 1][k]) for i in range(devices)]
        else:
            steps[k] = [(i, i ^ 2 * k) for i in range(devices)]
    result = {0: blocks[0]}
    for k, pairs in steps.items():
        came = sorted((target, source) for source, target in pairs)
        block = next(m for m in steps if steps[m] == came) if back else k
        result[block] = lax.ppermute(blocks[block], "expert", pairs)
    return result


def from_twin(array):
    pairs = [(i, i ^ 1) for i in range(lax.axis_size("expert"))]
    return lax.ppermute(array, "expert", pairs)


def body(tokens, w_in, w_down, old_place, new_place, expert_ids, replica, combine):
    devices = lax.axis_size("expert")
    shards = devices // SLOTS
    split = shards == 1
    repeats = max(shards // 2, 1)
    chips = devices // 2
    rows, width = tokens.shape
    hidden = w_down.shape[0]
    twin_in = from_twin(w_in)
    operands = (new_place, old_place, expert_ids.T, replica.T, tokens)
    combine = combine.T
    block = jax.ShapeDtypeStruct((CAP * (2 if split else 1), width), jnp.bfloat16)
    found, *blocks = call(
        functools.partial(dispatch_kernel, shards),
        [shape_of(operands[2])] + [block] * (chips // repeats),
        operands,
        2 * SLOTS * CAP * rows * width,
        [HBM] * len(operands),
        scratch=scratch_for(operands[:2], operands[2:]),
    )
    received = exchange([blocks[c // repeats] for c in range(chips)], split)
    twin_down = from_twin(lax.optimization_barrier((w_down, found))[0])
    own_in, own_down, weight = call(
        prepare_kernel,
        [
            shape_of(w_in),
            shape_of(w_down),
            jax.ShapeDtypeStruct((2 * rows, SLOTS * CAP), jnp.bfloat16),
        ],
        (found, combine, w_in, w_down),
        0,
        [VMEM, HBM, HBM, HBM],
        scratch=[pltpu.VMEM(combine.shape, combine.dtype), pltpu.SemaphoreType.DMA((3,))],
    )
    units = call(
        functools.partial(hidden_kernel, split),
        jax.ShapeDtypeStruct((chips * block.shape[0], 2 * hidden), jnp.bfloat16),
        (own_in, twin_in, *received.values()),
        800 * chips * block.shape[0] * hidden * width,
    )
    pieces = call(
        down_kernel,
        [block] * chips,
        (units, own_down, twin_down),
        4 * chips * block.shape[0] * hidden * width,
    )
    returned = exchange(pieces, split, back=True)
    parts = 2 if width % 256 == 0 else 1
    return call(
        functools.partial(mix_kernel, repeats, tuple(returned)),
        shape_of(tokens),
        (weight, *returned.values()),
        4 * SLOTS * CAP * rows * width,
        out_specs=HBM,
        scratch=[pltpu.VMEM(tokens.shape, tokens.dtype), pltpu.SemaphoreType.DMA((parts,))],
    )


def solution(mesh):
    placed = (
        P(("group", "expert"), None),
        P(None, None, ("group", "expert")),
        P(("group", "expert"), None),
        P("group"),
        P("group"),
        P(("group", "expert"), None),
        P(("group", "expert"), None),
        P(("group", "expert"), None),
    )
    return jax.shard_map(
        body, mesh=mesh, in_specs=placed, out_specs=P(("group", "expert"), None), check_vma=False
    )
```

```python
import functools

import jax
import jax.numpy as jnp
from jax import lax
from jax.experimental import pallas as pl
from jax.experimental.pallas import tpu as pltpu
from jax.sharding import PartitionSpec as P

SLOTS = 8
CAP = 4
SENDS = (
    ((3, 2, 0, 1), (2, 3, 1, 0), (1, 0, 3, 2)),
    ((1, 2, 3, 0), (2, 3, 0, 1), (3, 0, 1, 2)),
)
BACK = ((3, 2, 1), (2, 1, 3))

VMEM = pl.BlockSpec(memory_space=pltpu.VMEM)
HBM = pl.BlockSpec(memory_space=pltpu.HBM)


def targets(shards, goes, new_ref, old_ref, ids, replica):
    slots, rows = new_ref.shape[0], ids.shape[1]
    device = lax.axis_index("expert")
    down = lax.broadcasted_iota(jnp.int32, (slots, rows), 0)
    expert = jnp.zeros((slots, rows), jnp.int32)
    line = jnp.zeros((slots, rows), jnp.int32)
    for slot in range(slots):
        source = jnp.where(new_ref[slot] == old_ref[slot], slot, slot ^ 1)
        away = source ^ (device // shards)
        if shards == 1:
            step = sum(jnp.where(source >> 1 == chip, k, 0) for k, chip in enumerate(goes, 1))
            away = (source & 1) | (step << 1)
        expert = jnp.where(down == slot, new_ref[slot], expert)
        line = jnp.where(down == slot, CAP * away, line)
    count = jnp.zeros((slots, rows), jnp.int32)
    rank = jnp.zeros((slots, rows), jnp.int32)
    for slot in range(slots):
        same = expert == new_ref[slot]
        count += jnp.where(same, 1, 0)
        rank += jnp.where(same & (down > slot), 1, 0)
    chosen = []
    for k in range(ids.shape[0]):
        hit = (ids[k : k + 1] == expert) & (rank == (replica[k : k + 1] & (count - 1)))
        chosen.append(jnp.where(hit, 1.0, 0.0))
    earlier = lax.broadcasted_iota(jnp.int32, (rows, rows), 0) < lax.broadcasted_iota(
        jnp.int32, (rows, rows), 1
    )
    any_choice = functools.reduce(jnp.add, chosen)
    position = jnp.dot(
        any_choice.astype(jnp.bfloat16),
        jnp.where(earlier, 1.0, 0.0).astype(jnp.bfloat16),
        preferred_element_type=jnp.float32,
    )
    line = line.astype(jnp.float32)
    found = []
    for hit in chosen:
        place = jnp.where(position < CAP, line + position + 1.0, 0.0)
        found.append((jnp.sum(hit * place, axis=0, keepdims=True) - 1.0).astype(jnp.int32))
        position = position + hit
    return found


def start_copies(sources, buffers, sems):
    copies = [pltpu.make_async_copy(*pair, sems.at[i]) for i, pair in enumerate(zip(sources, buffers))]
    for copy in copies:
        copy.start()
    return copies


def by_device(table):
    device = lax.axis_index("expert")
    return sum(jnp.where(device == i, entry, 0) for i, entry in enumerate(table))


def dispatch_kernel(shards, *refs):
    sources, refs = refs[:5], refs[5:]
    found_ref, *block_refs = refs[:-6]
    buffers, sems = refs[-6:-1], refs[-1]
    copies = start_copies(sources, buffers, sems)
    goes = [by_device([SENDS[i & 1][k][i >> 1] for i in range(SLOTS)]) for k in range(3)]
    for copy in copies[:-1]:
        copy.wait()
    found = targets(shards, goes, *buffers[:2], *[ref[...] for ref in buffers[2:-1]])
    found_ref[...] = jnp.concatenate(found, axis=0)
    tokens_ref = buffers[-1]
    size = block_refs[0].shape[0]
    line = lax.broadcasted_iota(jnp.int32, (size * len(block_refs), tokens_ref.shape[0]), 0)
    picked = functools.reduce(jnp.logical_or, [line == target for target in found])
    selector = jnp.where(picked, 1.0, 0.0).astype(jnp.bfloat16)
    copies[-1].wait()
    buffer = jnp.dot(selector, tokens_ref[...], preferred_element_type=jnp.float32)
    for b, block_ref in enumerate(block_refs):
        block_ref[...] = buffer[size * b : size * (b + 1)].astype(jnp.bfloat16)


def prepare_kernel(
    split, found_ref, combine_hbm, in_hbm, down_hbm, in_ref, down_ref, weight_ref, combine_ref, sems
):
    copies = start_copies(
        (combine_hbm, in_hbm, down_hbm), (combine_ref, in_ref, down_ref), sems
    )
    copies[0].wait()
    line = lax.broadcasted_iota(jnp.int32, (weight_ref.shape[1], combine_ref.shape[1]), 0)
    if split:
        even = (lax.axis_index("expert") & 1) == 0
        block = line // (2 * CAP)
        for at, steps in enumerate(zip(BACK[1], BACK[0]), 1):
            came = jnp.where(even, *steps)
            line = jnp.where(block == at, line + 2 * CAP * (came - at), line)
    weight = functools.reduce(
        jnp.add,
        [
            jnp.where(line == found_ref[k : k + 1], combine_ref[k : k + 1], 0.0)
            for k in range(found_ref.shape[0])
        ],
    ).T
    high = weight.astype(jnp.bfloat16)
    low = (weight - high.astype(jnp.float32)).astype(jnp.bfloat16)
    weight_ref[...] = jnp.concatenate([high, low], axis=0)
    for copy in copies[1:]:
        copy.wait()


def stack(refs):
    return jnp.concatenate([ref[...] for ref in refs], axis=0)


def hidden_kernel(split, in_ref, twin_in_ref, *refs):
    *refs, out_ref = refs
    odd = lax.axis_index("expert") & 1
    rows = stack(refs)
    half_size = refs[0].shape[0] // 2
    hidden = []
    for half, ref in enumerate((in_ref, twin_in_ref)):
        gate = jnp.dot(rows, ref[0], preferred_element_type=jnp.float32)
        up = jnp.dot(rows, ref[1], preferred_element_type=jnp.float32)
        value = jax.nn.silu(gate) * up
        if split:
            place = lax.broadcasted_iota(jnp.int32, value.shape, 0) // half_size
            value = jnp.where((place & 1) == (odd ^ half), value, 0.0)
        hidden.append(value.astype(jnp.bfloat16))
    out_ref[...] = jnp.concatenate(hidden, axis=1)


def down_kernel(split, hidden_ref, down_ref, twin_down_ref, *refs):
    units = down_ref.shape[0]
    own = hidden_ref[:, :units], down_ref[...]
    twin = hidden_ref[:, units:], twin_down_ref[...]
    piece = jnp.dot(*own, preferred_element_type=jnp.float32)
    piece += jnp.dot(*twin, preferred_element_type=jnp.float32)
    size = refs[0].shape[0]
    blocks = [piece[size * b : size * (b + 1)] for b in range(len(refs))]
    if split:
        even = (lax.axis_index("expert") & 1) == 0
        blocks[1:] = [jnp.where(even, blocks[e], blocks[o]) for e, o in zip(*BACK)]
    for block, out_ref in zip(blocks, refs):
        out_ref[...] = block.astype(jnp.bfloat16)


def mix_kernel(repeats, weight_ref, *refs):
    out_hbm, out_ref, sems = refs[-3:]
    refs = refs[:-3]
    rows, width = out_ref.shape
    parts = sems.shape[0]
    step = width // parts
    copies = []
    for part in range(parts):
        columns = slice(part * step, (part + 1) * step)
        pieces = [stack([ref.at[:, columns] for ref in refs[j::repeats]]) for j in range(repeats)]
        if repeats == 1:
            mixed = jnp.dot(weight_ref[...], pieces[0], preferred_element_type=jnp.float32)
        else:
            total = sum(piece.astype(jnp.float32) for piece in pieces)
            high = total.astype(jnp.bfloat16)
            low = (total - high.astype(jnp.float32)).astype(jnp.bfloat16)
            mixed = jnp.dot(weight_ref[...], high, preferred_element_type=jnp.float32)
            mixed += jnp.dot(weight_ref[...], low, preferred_element_type=jnp.float32)
        out_ref[:, columns] = (mixed[:rows] + mixed[rows:]).astype(jnp.bfloat16)
        copies.append(
            pltpu.make_async_copy(out_ref.at[:, columns], out_hbm.at[:, columns], sems.at[part])
        )
        copies[-1].start()
    for copy in copies:
        copy.wait()


def call(kernel, outs, args, flops, arg_specs=None, out_specs=None, scratch=()):
    arg_specs = arg_specs or [VMEM] * len(args)
    nbytes = sum(x.size * x.dtype.itemsize for x in jax.tree.leaves((outs, args)))
    return pl.pallas_call(
        kernel,
        out_shape=outs,
        in_specs=arg_specs,
        out_specs=out_specs or jax.tree.map(lambda _: VMEM, outs),
        scratch_shapes=scratch,
        compiler_params=pltpu.CompilerParams(vmem_limit_bytes=16 << 20),
        cost_estimate=pl.CostEstimate(flops=flops, bytes_accessed=nbytes, transcendentals=0),
    )(*[pltpu.with_memory_space_constraint(x, s.memory_space) for x, s in zip(args, arg_specs)])


def shape_of(array):
    return jax.ShapeDtypeStruct(array.shape, array.dtype)


def scratch_for(scalars, arrays):
    return [
        *[pltpu.SMEM(x.shape, x.dtype) for x in scalars],
        *[pltpu.VMEM(x.shape, x.dtype) for x in arrays],
        pltpu.SemaphoreType.DMA((len(scalars) + len(arrays),)),
    ]


def exchange(blocks, split, back=False):
    devices = lax.axis_size("expert")

    def sends(i, k):
        return 2 * SENDS[i & 1][k - 1][i >> 1] + (1 - (i & 1)) if split else i ^ 2 * k

    def sent_from(i, k):
        return next(j for j in range(devices) if sends(j, k) == i)

    result = [blocks[0]]
    for k in range(1, len(blocks)):
        if back and split:
            pairs = [(i, sent_from(i, BACK[i & 1][k - 1])) for i in range(devices)]
        else:
            pairs = [(i, sends(i, k)) for i in range(devices)]
        result.append(lax.ppermute(blocks[k], "expert", pairs))
    return result


def from_twin(array):
    pairs = [(i, i ^ 1) for i in range(lax.axis_size("expert"))]
    return lax.ppermute(array, "expert", pairs)


def body(tokens, w_in, w_down, old_place, new_place, expert_ids, replica, combine):
    devices = lax.axis_size("expert")
    shards = devices // SLOTS
    split = shards == 1
    repeats = max(shards // 2, 1)
    chips = devices // 2
    rows, width = tokens.shape
    hidden = w_down.shape[0]
    twin_in = from_twin(w_in)
    operands = (new_place, old_place, expert_ids.T, replica.T, tokens)
    combine = combine.T
    block = jax.ShapeDtypeStruct((CAP * (2 if split else 1), width), jnp.bfloat16)
    found, *blocks = call(
        functools.partial(dispatch_kernel, shards),
        [shape_of(operands[2])] + [block] * (chips // repeats),
        operands,
        2 * SLOTS * CAP * rows * width,
        [HBM] * len(operands),
        scratch=scratch_for(operands[:2], operands[2:]),
    )
    received = exchange([blocks[c // repeats] for c in range(chips)], split)
    twin_down = from_twin(lax.optimization_barrier((w_down, found))[0])
    own_in, own_down, weight = call(
        functools.partial(prepare_kernel, split),
        [
            shape_of(w_in),
            shape_of(w_down),
            jax.ShapeDtypeStruct((2 * rows, SLOTS * CAP), jnp.bfloat16),
        ],
        (found, combine, w_in, w_down),
        0,
        [VMEM, HBM, HBM, HBM],
        scratch=[pltpu.VMEM(combine.shape, combine.dtype), pltpu.SemaphoreType.DMA((3,))],
    )
    units = call(
        functools.partial(hidden_kernel, split),
        jax.ShapeDtypeStruct((chips * block.shape[0], 2 * hidden), jnp.bfloat16),
        (own_in, twin_in, *received),
        800 * chips * block.shape[0] * hidden * width,
    )
    pieces = call(
        functools.partial(down_kernel, split),
        [block] * chips,
        (units, own_down, twin_down),
        4 * chips * block.shape[0] * hidden * width,
    )
    returned = exchange(pieces, split, back=True)
    parts = 4 if width % 512 == 0 else 1
    return call(
        functools.partial(mix_kernel, repeats),
        shape_of(tokens),
        (weight, *returned),
        4 * SLOTS * CAP * rows * width,
        out_specs=HBM,
        scratch=[pltpu.VMEM(tokens.shape, tokens.dtype), pltpu.SemaphoreType.DMA((parts,))],
    )


def solution(mesh):
    placed = (
        P(("group", "expert"), None),
        P(None, None, ("group", "expert")),
        P(("group", "expert"), None),
        P("group"),
        P("group"),
        P(("group", "expert"), None),
        P(("group", "expert"), None),
        P(("group", "expert"), None),
    )
    return jax.shard_map(
        body, mesh=mesh, in_specs=placed, out_specs=P(("group", "expert"), None), check_vma=False
    )
```

```python
import functools

import jax
import jax.numpy as jnp
from jax import lax
from jax.experimental import pallas as pl
from jax.experimental.pallas import tpu as pltpu
from jax.sharding import PartitionSpec as P

SLOTS = 8
CAP = 4
SENDS = (
    ((2, 3, 1, 0), (3, 2, 0, 1), (1, 0, 3, 2)),
    ((3, 2, 0, 1), (2, 3, 1, 0), (1, 0, 3, 2)),
)
BACK = ((1, 3, 2), (2, 3, 1))

VMEM = pl.BlockSpec(memory_space=pltpu.VMEM)
HBM = pl.BlockSpec(memory_space=pltpu.HBM)


def targets(shards, goes, new_ref, old_ref, ids, replica):
    slots, rows = new_ref.shape[0], ids.shape[1]
    device = lax.axis_index("expert")
    down = lax.broadcasted_iota(jnp.int32, (slots, rows), 0)
    expert = jnp.zeros((slots, rows), jnp.int32)
    line = jnp.zeros((slots, rows), jnp.int32)
    for slot in range(slots):
        source = jnp.where(new_ref[slot] == old_ref[slot], slot, slot ^ 1)
        away = source ^ (device // shards)
        if shards == 1:
            step = sum(jnp.where(source >> 1 == chip, k, 0) for k, chip in enumerate(goes, 1))
            away = (source & 1) | (step << 1)
        expert = jnp.where(down == slot, new_ref[slot], expert)
        line = jnp.where(down == slot, CAP * away, line)
    count = jnp.zeros((slots, rows), jnp.int32)
    rank = jnp.zeros((slots, rows), jnp.int32)
    for slot in range(slots):
        same = expert == new_ref[slot]
        count += jnp.where(same, 1, 0)
        rank += jnp.where(same & (down > slot), 1, 0)
    chosen = []
    for k in range(ids.shape[0]):
        hit = (ids[k : k + 1] == expert) & (rank == (replica[k : k + 1] & (count - 1)))
        chosen.append(jnp.where(hit, 1.0, 0.0))
    earlier = lax.broadcasted_iota(jnp.int32, (rows, rows), 0) < lax.broadcasted_iota(
        jnp.int32, (rows, rows), 1
    )
    any_choice = functools.reduce(jnp.add, chosen)
    position = jnp.dot(
        any_choice.astype(jnp.bfloat16),
        jnp.where(earlier, 1.0, 0.0).astype(jnp.bfloat16),
        preferred_element_type=jnp.float32,
    )
    line = line.astype(jnp.float32)
    found = []
    for hit in chosen:
        place = jnp.where(position < CAP, line + position + 1.0, 0.0)
        found.append((jnp.sum(hit * place, axis=0, keepdims=True) - 1.0).astype(jnp.int32))
        position = position + hit
    return found


def start_copies(sources, buffers, sems):
    copies = [pltpu.make_async_copy(*pair, sems.at[i]) for i, pair in enumerate(zip(sources, buffers))]
    for copy in copies:
        copy.start()
    return copies


def by_device(table):
    device = lax.axis_index("expert")
    return sum(jnp.where(device == i, entry, 0) for i, entry in enumerate(table))


def dispatch_kernel(shards, *refs):
    sources, refs = refs[:5], refs[5:]
    found_ref, *block_refs = refs[:-6]
    buffers, sems = refs[-6:-1], refs[-1]
    copies = start_copies(sources, buffers, sems)
    goes = [by_device([SENDS[i & 1][k][i >> 1] for i in range(SLOTS)]) for k in range(3)]
    for copy in copies[:-1]:
        copy.wait()
    found = targets(shards, goes, *buffers[:2], *[ref[...] for ref in buffers[2:-1]])
    found_ref[...] = jnp.concatenate(found, axis=0)
    tokens_ref = buffers[-1]
    size = block_refs[0].shape[0]
    line = lax.broadcasted_iota(jnp.int32, (size * len(block_refs), tokens_ref.shape[0]), 0)
    picked = functools.reduce(jnp.logical_or, [line == target for target in found])
    selector = jnp.where(picked, 1.0, 0.0).astype(jnp.bfloat16)
    copies[-1].wait()
    buffer = jnp.dot(selector, tokens_ref[...], preferred_element_type=jnp.float32)
    for b, block_ref in enumerate(block_refs):
        block_ref[...] = buffer[size * b : size * (b + 1)].astype(jnp.bfloat16)


def prepare_kernel(
    split, found_ref, combine_hbm, in_hbm, down_hbm, in_ref, down_ref, weight_ref, combine_ref, sems
):
    copies = start_copies(
        (combine_hbm, in_hbm, down_hbm), (combine_ref, in_ref, down_ref), sems
    )
    copies[0].wait()
    line = lax.broadcasted_iota(jnp.int32, (weight_ref.shape[1], combine_ref.shape[1]), 0)
    if split:
        even = (lax.axis_index("expert") & 1) == 0
        block = line // (2 * CAP)
        for at, steps in enumerate(zip(BACK[1], BACK[0]), 1):
            came = jnp.where(even, *steps)
            line = jnp.where(block == at, line + 2 * CAP * (came - at), line)
    weight = functools.reduce(
        jnp.add,
        [
            jnp.where(line == found_ref[k : k + 1], combine_ref[k : k + 1], 0.0)
            for k in range(found_ref.shape[0])
        ],
    ).T
    high = weight.astype(jnp.bfloat16)
    low = (weight - high.astype(jnp.float32)).astype(jnp.bfloat16)
    weight_ref[...] = jnp.concatenate([high, low], axis=0)
    for copy in copies[1:]:
        copy.wait()


def stack(refs):
    return jnp.concatenate([ref[...] for ref in refs], axis=0)


def hidden_kernel(split, in_ref, twin_in_ref, *refs):
    *refs, out_ref = refs
    odd = lax.axis_index("expert") & 1
    rows = stack(refs)
    half_size = refs[0].shape[0] // 2
    hidden = []
    for half, ref in enumerate((in_ref, twin_in_ref)):
        gate = jnp.dot(rows, ref[0], preferred_element_type=jnp.float32)
        up = jnp.dot(rows, ref[1], preferred_element_type=jnp.float32)
        value = jax.nn.silu(gate) * up
        if split:
            place = lax.broadcasted_iota(jnp.int32, value.shape, 0) // half_size
            value = jnp.where((place & 1) == (odd ^ half), value, 0.0)
        hidden.append(value.astype(jnp.bfloat16))
    out_ref[...] = jnp.concatenate(hidden, axis=1)


def down_kernel(split, hidden_ref, down_ref, twin_down_ref, *refs):
    units = down_ref.shape[0]
    own = hidden_ref[:, :units], down_ref[...]
    twin = hidden_ref[:, units:], twin_down_ref[...]
    piece = jnp.dot(*own, preferred_element_type=jnp.float32)
    piece += jnp.dot(*twin, preferred_element_type=jnp.float32)
    size = refs[0].shape[0]
    blocks = [piece[size * b : size * (b + 1)] for b in range(len(refs))]
    if split:
        even = (lax.axis_index("expert") & 1) == 0
        blocks[1:] = [jnp.where(even, blocks[e], blocks[o]) for e, o in zip(*BACK)]
    for block, out_ref in zip(blocks, refs):
        out_ref[...] = block.astype(jnp.bfloat16)


def mix_kernel(repeats, weight_ref, *refs):
    out_hbm, out_ref, sems = refs[-3:]
    refs = refs[:-3]
    rows, width = out_ref.shape
    parts = sems.shape[0]
    step = width // parts
    copies = []
    for part in range(parts):
        columns = slice(part * step, (part + 1) * step)
        pieces = [stack([ref.at[:, columns] for ref in refs[j::repeats]]) for j in range(repeats)]
        if repeats == 1:
            mixed = jnp.dot(weight_ref[...], pieces[0], preferred_element_type=jnp.float32)
        else:
            total = sum(piece.astype(jnp.float32) for piece in pieces)
            high = total.astype(jnp.bfloat16)
            low = (total - high.astype(jnp.float32)).astype(jnp.bfloat16)
            mixed = jnp.dot(weight_ref[...], high, preferred_element_type=jnp.float32)
            mixed += jnp.dot(weight_ref[...], low, preferred_element_type=jnp.float32)
        out_ref[:, columns] = (mixed[:rows] + mixed[rows:]).astype(jnp.bfloat16)
        copies.append(
            pltpu.make_async_copy(out_ref.at[:, columns], out_hbm.at[:, columns], sems.at[part])
        )
        copies[-1].start()
    for copy in copies:
        copy.wait()


def call(kernel, outs, args, flops, arg_specs=None, out_specs=None, scratch=()):
    arg_specs = arg_specs or [VMEM] * len(args)
    nbytes = sum(x.size * x.dtype.itemsize for x in jax.tree.leaves((outs, args)))
    return pl.pallas_call(
        kernel,
        out_shape=outs,
        in_specs=arg_specs,
        out_specs=out_specs or jax.tree.map(lambda _: VMEM, outs),
        scratch_shapes=scratch,
        compiler_params=pltpu.CompilerParams(vmem_limit_bytes=16 << 20),
        cost_estimate=pl.CostEstimate(flops=flops, bytes_accessed=nbytes, transcendentals=0),
    )(*[pltpu.with_memory_space_constraint(x, s.memory_space) for x, s in zip(args, arg_specs)])


def shape_of(array):
    return jax.ShapeDtypeStruct(array.shape, array.dtype)


def scratch_for(scalars, arrays):
    return [
        *[pltpu.SMEM(x.shape, x.dtype) for x in scalars],
        *[pltpu.VMEM(x.shape, x.dtype) for x in arrays],
        pltpu.SemaphoreType.DMA((len(scalars) + len(arrays),)),
    ]


def exchange(blocks, split, back=False):
    devices = lax.axis_size("expert")

    def sends(i, k):
        return 2 * SENDS[i & 1][k - 1][i >> 1] + (1 - (i & 1)) if split else i ^ 2 * k

    def sent_from(i, k):
        return next(j for j in range(devices) if sends(j, k) == i)

    result = [blocks[0]]
    for k in range(1, len(blocks)):
        if back and split:
            pairs = [(i, sent_from(i, BACK[i & 1][k - 1])) for i in range(devices)]
        else:
            pairs = [(i, sends(i, k)) for i in range(devices)]
        result.append(lax.ppermute(blocks[k], "expert", pairs))
    return result


def from_twin(array):
    pairs = [(i, i ^ 1) for i in range(lax.axis_size("expert"))]
    return lax.ppermute(array, "expert", pairs)


def body(tokens, w_in, w_down, old_place, new_place, expert_ids, replica, combine):
    devices = lax.axis_size("expert")
    shards = devices // SLOTS
    split = shards == 1
    repeats = max(shards // 2, 1)
    chips = devices // 2
    rows, width = tokens.shape
    hidden = w_down.shape[0]
    twin_in = from_twin(w_in)
    operands = (new_place, old_place, expert_ids.T, replica.T, tokens)
    combine = combine.T
    block = jax.ShapeDtypeStruct((CAP * (2 if split else 1), width), jnp.bfloat16)
    found, *blocks = call(
        functools.partial(dispatch_kernel, shards),
        [shape_of(operands[2])] + [block] * (chips // repeats),
        operands,
        2 * SLOTS * CAP * rows * width,
        [HBM] * len(operands),
        scratch=scratch_for(operands[:2], operands[2:]),
    )
    received = exchange([blocks[c // repeats] for c in range(chips)], split)
    twin_down = from_twin(lax.optimization_barrier((w_down, found))[0])
    own_in, own_down, weight = call(
        functools.partial(prepare_kernel, split),
        [
            shape_of(w_in),
            shape_of(w_down),
            jax.ShapeDtypeStruct((2 * rows, SLOTS * CAP), jnp.bfloat16),
        ],
        (found, combine, w_in, w_down),
        0,
        [VMEM, HBM, HBM, HBM],
        scratch=[pltpu.VMEM(combine.shape, combine.dtype), pltpu.SemaphoreType.DMA((3,))],
    )
    units = call(
        functools.partial(hidden_kernel, split),
        jax.ShapeDtypeStruct((chips * block.shape[0], 2 * hidden), jnp.bfloat16),
        (own_in, twin_in, *received),
        800 * chips * block.shape[0] * hidden * width,
    )
    pieces = call(
        functools.partial(down_kernel, split),
        [block] * chips,
        (units, own_down, twin_down),
        4 * chips * block.shape[0] * hidden * width,
    )
    returned = exchange(pieces, split, back=True)
    parts = 4 if width % 512 == 0 else 1
    return call(
        functools.partial(mix_kernel, repeats),
        shape_of(tokens),
        (weight, *returned),
        4 * SLOTS * CAP * rows * width,
        out_specs=HBM,
        scratch=[pltpu.VMEM(tokens.shape, tokens.dtype), pltpu.SemaphoreType.DMA((parts,))],
    )


def solution(mesh):
    placed = (
        P(("group", "expert"), None),
        P(None, None, ("group", "expert")),
        P(("group", "expert"), None),
        P("group"),
        P("group"),
        P(("group", "expert"), None),
        P(("group", "expert"), None),
        P(("group", "expert"), None),
    )
    return jax.shard_map(
        body, mesh=mesh, in_specs=placed, out_specs=P(("group", "expert"), None), check_vma=False
    )
```

```python
import functools

import jax
import jax.numpy as jnp
from jax import lax
from jax.experimental import pallas as pl
from jax.experimental.pallas import tpu as pltpu
from jax.sharding import PartitionSpec as P

SLOTS = 8
CAP = 4
SENDS = (
    ((3, 2, 0, 1), (2, 3, 1, 0), (1, 0, 3, 2)),
    ((1, 2, 3, 0), (2, 3, 0, 1), (3, 0, 1, 2)),
)
BACK = ((3, 2, 1), (2, 1, 3))

VMEM = pl.BlockSpec(memory_space=pltpu.VMEM)
HBM = pl.BlockSpec(memory_space=pltpu.HBM)


def slot_lines(shards, goes, new_ref, old_ref, rows):
    slots = new_ref.shape[0]
    mine = lax.axis_index("expert") // shards
    down = lax.broadcasted_iota(jnp.int32, (slots, rows), 0)
    expert, line, count, rank = [jnp.zeros((slots, rows), jnp.int32)] * 4
    for slot in range(slots):
        source = jnp.where(new_ref[slot] == old_ref[slot], slot, slot ^ 1)
        away = source ^ mine
        if shards == 1:
            step = sum(jnp.where(source >> 1 == chip, k, 0) for k, chip in enumerate(goes, 1))
            away = (source & 1) | (step << 1)
        expert = jnp.where(down == slot, new_ref[slot], expert)
        line = jnp.where(down == slot, CAP * away, line)
    for slot in range(slots):
        same = expert == new_ref[slot]
        count += jnp.where(same, 1, 0)
        rank += jnp.where(same & (down > slot), 1, 0)
    return expert, line.astype(jnp.float32), count, rank


def targets(slot_values, earlier, ids, replica):
    expert, line, count, rank = slot_values
    chosen = []
    for k in range(ids.shape[0]):
        hit = (ids[k : k + 1] == expert) & (rank == (replica[k : k + 1] & (count - 1)))
        chosen.append(jnp.where(hit, 1.0, 0.0))
    any_choice = functools.reduce(jnp.add, chosen).astype(jnp.bfloat16)
    position = jnp.dot(any_choice, earlier, preferred_element_type=jnp.float32)
    found = []
    for hit in chosen:
        place = jnp.where(position < CAP, line + position + 1.0, 0.0)
        found.append((jnp.sum(hit * place, axis=0, keepdims=True) - 1.0).astype(jnp.int32))
        position = position + hit
    return found


def start_copies(sources, buffers, sems):
    copies = [pltpu.make_async_copy(*pair, sems.at[i]) for i, pair in enumerate(zip(sources, buffers))]
    for copy in copies:
        copy.start()
    return copies


def by_device(table):
    device = lax.axis_index("expert")
    return sum(jnp.where(device == i, entry, 0) for i, entry in enumerate(table))


def dispatch_kernel(shards, *refs):
    sources, refs = refs[:5], refs[5:]
    found_ref, *block_refs = refs[:-6]
    buffers, sems = refs[-6:-1], refs[-1]
    copies = start_copies(sources, buffers, sems)
    tokens_ref = buffers[-1]
    rows = tokens_ref.shape[0]
    size = block_refs[0].shape[0]
    goes = [by_device([SENDS[i & 1][k][i >> 1] for i in range(SLOTS)]) for k in range(3)]
    earlier = lax.broadcasted_iota(jnp.int32, (rows, rows), 0) < lax.broadcasted_iota(
        jnp.int32, (rows, rows), 1
    )
    earlier = jnp.where(earlier, 1.0, 0.0).astype(jnp.bfloat16)
    line = lax.broadcasted_iota(jnp.int32, (size * len(block_refs), rows), 0)
    for copy in copies[:2]:
        copy.wait()
    slot_values = slot_lines(shards, goes, *buffers[:2], rows)
    for copy in copies[2:-1]:
        copy.wait()
    found = targets(slot_values, earlier, *[ref[...] for ref in buffers[2:-1]])
    picked = functools.reduce(jnp.logical_or, [line == target for target in found])
    selector = jnp.where(picked, 1.0, 0.0).astype(jnp.bfloat16)
    copies[-1].wait()
    buffer = jnp.dot(selector, tokens_ref[...], preferred_element_type=jnp.float32)
    found_ref[...] = jnp.concatenate(found, axis=0)
    for b, block_ref in enumerate(block_refs):
        block_ref[...] = buffer[size * b : size * (b + 1)].astype(jnp.bfloat16)


def prepare_kernel(
    split, found_ref, combine_hbm, in_hbm, down_hbm, in_ref, down_ref, weight_ref, combine_ref, sems
):
    copies = start_copies(
        (combine_hbm, in_hbm, down_hbm), (combine_ref, in_ref, down_ref), sems
    )
    copies[0].wait()
    line = lax.broadcasted_iota(jnp.int32, (weight_ref.shape[1], combine_ref.shape[1]), 0)
    if split:
        even = (lax.axis_index("expert") & 1) == 0
        block = line // (2 * CAP)
        for at, steps in enumerate(zip(BACK[1], BACK[0]), 1):
            came = jnp.where(even, *steps)
            line = jnp.where(block == at, line + 2 * CAP * (came - at), line)
    weight = functools.reduce(
        jnp.add,
        [
            jnp.where(line == found_ref[k : k + 1], combine_ref[k : k + 1], 0.0)
            for k in range(found_ref.shape[0])
        ],
    ).T
    high = weight.astype(jnp.bfloat16)
    low = (weight - high.astype(jnp.float32)).astype(jnp.bfloat16)
    weight_ref[...] = jnp.concatenate([high, low], axis=0)
    for copy in copies[1:]:
        copy.wait()


def stack(refs):
    return jnp.concatenate([ref[...] for ref in refs], axis=0)


def hidden_kernel(split, in_ref, twin_in_ref, *refs):
    *refs, out_ref = refs
    odd = lax.axis_index("expert") & 1
    rows = stack(refs)
    half_size = refs[0].shape[0] // 2
    hidden = []
    for half, ref in enumerate((in_ref, twin_in_ref)):
        gate = jnp.dot(rows, ref[0], preferred_element_type=jnp.float32)
        up = jnp.dot(rows, ref[1], preferred_element_type=jnp.float32)
        value = jax.nn.silu(gate) * up
        if split:
            place = lax.broadcasted_iota(jnp.int32, value.shape, 0) // half_size
            value = jnp.where((place & 1) == (odd ^ half), value, 0.0)
        hidden.append(value.astype(jnp.bfloat16))
    out_ref[...] = jnp.concatenate(hidden, axis=1)


def down_kernel(split, hidden_ref, down_ref, twin_down_ref, *refs):
    units = down_ref.shape[0]
    own = hidden_ref[:, :units], down_ref[...]
    twin = hidden_ref[:, units:], twin_down_ref[...]
    piece = jnp.dot(*own, preferred_element_type=jnp.float32)
    piece += jnp.dot(*twin, preferred_element_type=jnp.float32)
    size = refs[0].shape[0]
    blocks = [piece[size * b : size * (b + 1)] for b in range(len(refs))]
    if split:
        even = (lax.axis_index("expert") & 1) == 0
        blocks[1:] = [jnp.where(even, blocks[e], blocks[o]) for e, o in zip(*BACK)]
    for block, out_ref in zip(blocks, refs):
        out_ref[...] = block.astype(jnp.bfloat16)


def mix_kernel(repeats, weight_ref, *refs):
    out_hbm, out_ref, sems = refs[-3:]
    refs = refs[:-3]
    rows, width = out_ref.shape
    parts = sems.shape[0]
    step = width // parts
    copies = []
    for part in range(parts):
        columns = slice(part * step, (part + 1) * step)
        pieces = [stack([ref.at[:, columns] for ref in refs[j::repeats]]) for j in range(repeats)]
        if repeats == 1:
            mixed = jnp.dot(weight_ref[...], pieces[0], preferred_element_type=jnp.float32)
        else:
            total = sum(piece.astype(jnp.float32) for piece in pieces)
            high = total.astype(jnp.bfloat16)
            low = (total - high.astype(jnp.float32)).astype(jnp.bfloat16)
            mixed = jnp.dot(weight_ref[...], high, preferred_element_type=jnp.float32)
            mixed += jnp.dot(weight_ref[...], low, preferred_element_type=jnp.float32)
        out_ref[:, columns] = (mixed[:rows] + mixed[rows:]).astype(jnp.bfloat16)
        copies.append(
            pltpu.make_async_copy(out_ref.at[:, columns], out_hbm.at[:, columns], sems.at[part])
        )
        copies[-1].start()
    for copy in copies:
        copy.wait()


def call(kernel, outs, args, flops, arg_specs=None, out_specs=None, scratch=()):
    arg_specs = arg_specs or [VMEM] * len(args)
    nbytes = sum(x.size * x.dtype.itemsize for x in jax.tree.leaves((outs, args)))
    return pl.pallas_call(
        kernel,
        out_shape=outs,
        in_specs=arg_specs,
        out_specs=out_specs or jax.tree.map(lambda _: VMEM, outs),
        scratch_shapes=scratch,
        compiler_params=pltpu.CompilerParams(vmem_limit_bytes=16 << 20),
        cost_estimate=pl.CostEstimate(flops=flops, bytes_accessed=nbytes, transcendentals=0),
    )(*[pltpu.with_memory_space_constraint(x, s.memory_space) for x, s in zip(args, arg_specs)])


def shape_of(array):
    return jax.ShapeDtypeStruct(array.shape, array.dtype)


def scratch_for(scalars, arrays):
    return [
        *[pltpu.SMEM(x.shape, x.dtype) for x in scalars],
        *[pltpu.VMEM(x.shape, x.dtype) for x in arrays],
        pltpu.SemaphoreType.DMA((len(scalars) + len(arrays),)),
    ]


def exchange(blocks, split, back=False):
    devices = lax.axis_size("expert")

    def sends(i, k):
        return 2 * SENDS[i & 1][k - 1][i >> 1] + (1 - (i & 1)) if split else i ^ 2 * k

    def sent_from(i, k):
        return next(j for j in range(devices) if sends(j, k) == i)

    result = [blocks[0]]
    for k in range(1, len(blocks)):
        if back and split:
            pairs = [(i, sent_from(i, BACK[i & 1][k - 1])) for i in range(devices)]
        else:
            pairs = [(i, sends(i, k)) for i in range(devices)]
        result.append(lax.ppermute(blocks[k], "expert", pairs))
    return result


def from_twin(array):
    pairs = [(i, i ^ 1) for i in range(lax.axis_size("expert"))]
    return lax.ppermute(array, "expert", pairs)


def body(tokens, w_in, w_down, old_place, new_place, expert_ids, replica, combine):
    devices = lax.axis_size("expert")
    shards = devices // SLOTS
    split = shards == 1
    repeats = max(shards // 2, 1)
    chips = devices // 2
    rows, width = tokens.shape
    hidden = w_down.shape[0]
    twin_in = from_twin(w_in)
    operands = (new_place, old_place, expert_ids.T, replica.T, tokens)
    combine = combine.T
    block = jax.ShapeDtypeStruct((CAP * (2 if split else 1), width), jnp.bfloat16)
    found, *blocks = call(
        functools.partial(dispatch_kernel, shards),
        [shape_of(operands[2])] + [block] * (chips // repeats),
        operands,
        2 * SLOTS * CAP * rows * width,
        [HBM] * len(operands),
        scratch=scratch_for(operands[:2], operands[2:]),
    )
    received = exchange([blocks[c // repeats] for c in range(chips)], split)
    twin_down = from_twin(lax.optimization_barrier((w_down, found))[0])
    own_in, own_down, weight = call(
        functools.partial(prepare_kernel, split),
        [
            shape_of(w_in),
            shape_of(w_down),
            jax.ShapeDtypeStruct((2 * rows, SLOTS * CAP), jnp.bfloat16),
        ],
        (found, combine, w_in, w_down),
        0,
        [VMEM, HBM, HBM, HBM],
        scratch=[pltpu.VMEM(combine.shape, combine.dtype), pltpu.SemaphoreType.DMA((3,))],
    )
    units = call(
        functools.partial(hidden_kernel, split),
        jax.ShapeDtypeStruct((chips * block.shape[0], 2 * hidden), jnp.bfloat16),
        (own_in, twin_in, *received),
        800 * chips * block.shape[0] * hidden * width,
    )
    pieces = call(
        functools.partial(down_kernel, split),
        [block] * chips,
        (units, own_down, twin_down),
        4 * chips * block.shape[0] * hidden * width,
    )
    returned = exchange(pieces, split, back=True)
    parts = 4 if width % 512 == 0 else 1
    return call(
        functools.partial(mix_kernel, repeats),
        shape_of(tokens),
        (weight, *returned),
        4 * SLOTS * CAP * rows * width,
        out_specs=HBM,
        scratch=[pltpu.VMEM(tokens.shape, tokens.dtype), pltpu.SemaphoreType.DMA((parts,))],
    )


def solution(mesh):
    placed = (
        P(("group", "expert"), None),
        P(None, None, ("group", "expert")),
        P(("group", "expert"), None),
        P("group"),
        P("group"),
        P(("group", "expert"), None),
        P(("group", "expert"), None),
        P(("group", "expert"), None),
    )
    return jax.shard_map(
        body, mesh=mesh, in_specs=placed, out_specs=P(("group", "expert"), None), check_vma=False
    )
```

```python
import functools

import jax
import jax.numpy as jnp
from jax import lax
from jax.experimental import pallas as pl
from jax.experimental.pallas import tpu as pltpu
from jax.sharding import PartitionSpec as P

SLOTS = 8
CAP = 4
SENDS = (
    ((3, 2, 0, 1), (2, 3, 1, 0), (1, 0, 3, 2)),
    ((1, 2, 3, 0), (2, 3, 0, 1), (3, 0, 1, 2)),
)
BACK = ((3, 2, 1), (2, 1, 3))

VMEM = pl.BlockSpec(memory_space=pltpu.VMEM)
HBM = pl.BlockSpec(memory_space=pltpu.HBM)


def targets(shards, goes, new_ref, old_ref, ids, replica):
    slots, rows = new_ref.shape[0], ids.shape[1]
    device = lax.axis_index("expert")
    down = lax.broadcasted_iota(jnp.int32, (slots, rows), 0)
    expert = jnp.zeros((slots, rows), jnp.int32)
    line = jnp.zeros((slots, rows), jnp.int32)
    for slot in range(slots):
        source = jnp.where(new_ref[slot] == old_ref[slot], slot, slot ^ 1)
        away = source ^ (device // shards)
        if shards == 1:
            step = sum(jnp.where(source >> 1 == chip, k, 0) for k, chip in enumerate(goes, 1))
            away = (source & 1) | (step << 1)
        expert = jnp.where(down == slot, new_ref[slot], expert)
        line = jnp.where(down == slot, CAP * away, line)
    count = jnp.zeros((slots, rows), jnp.int32)
    rank = jnp.zeros((slots, rows), jnp.int32)
    for slot in range(slots):
        same = expert == new_ref[slot]
        count += jnp.where(same, 1, 0)
        rank += jnp.where(same & (down > slot), 1, 0)
    chosen = []
    for k in range(ids.shape[0]):
        hit = (ids[k : k + 1] == expert) & (rank == (replica[k : k + 1] & (count - 1)))
        chosen.append(jnp.where(hit, 1.0, 0.0))
    earlier = lax.broadcasted_iota(jnp.int32, (rows, rows), 0) < lax.broadcasted_iota(
        jnp.int32, (rows, rows), 1
    )
    any_choice = functools.reduce(jnp.add, chosen)
    position = jnp.dot(
        any_choice.astype(jnp.bfloat16),
        jnp.where(earlier, 1.0, 0.0).astype(jnp.bfloat16),
        preferred_element_type=jnp.float32,
    )
    line = line.astype(jnp.float32)
    found = []
    for hit in chosen:
        place = jnp.where(position < CAP, line + position + 1.0, 0.0)
        found.append((jnp.sum(hit * place, axis=0, keepdims=True) - 1.0).astype(jnp.int32))
        position = position + hit
    return found


def start_copies(sources, buffers, sems):
    copies = [pltpu.make_async_copy(*pair, sems.at[i]) for i, pair in enumerate(zip(sources, buffers))]
    for copy in copies:
        copy.start()
    return copies


def by_device(table):
    device = lax.axis_index("expert")
    return sum(jnp.where(device == i, entry, 0) for i, entry in enumerate(table))


def dispatch_kernel(shards, *refs):
    sources, refs = refs[:5], refs[5:]
    found_ref, *block_refs = refs[:-6]
    buffers, sems = refs[-6:-1], refs[-1]
    copies = start_copies(sources, buffers, sems)
    goes = [by_device([SENDS[i & 1][k][i >> 1] for i in range(SLOTS)]) for k in range(3)]
    for copy in copies[:-1]:
        copy.wait()
    found = targets(shards, goes, *buffers[:2], *[ref[...] for ref in buffers[2:-1]])
    found_ref[...] = jnp.concatenate(found, axis=0)
    tokens_ref = buffers[-1]
    size = block_refs[0].shape[0]
    line = lax.broadcasted_iota(jnp.int32, (size * len(block_refs), tokens_ref.shape[0]), 0)
    picked = functools.reduce(jnp.logical_or, [line == target for target in found])
    selector = jnp.where(picked, 1.0, 0.0).astype(jnp.bfloat16)
    copies[-1].wait()
    buffer = jnp.dot(selector, tokens_ref[...], preferred_element_type=jnp.float32)
    for b, block_ref in enumerate(block_refs):
        block_ref[...] = buffer[size * b : size * (b + 1)].astype(jnp.bfloat16)


def prepare_kernel(
    split, found_ref, combine_hbm, in_hbm, down_hbm, in_ref, down_ref, weight_ref, combine_ref, sems
):
    copies = start_copies(
        (combine_hbm, in_hbm, down_hbm), (combine_ref, in_ref, down_ref), sems
    )
    copies[0].wait()
    line = lax.broadcasted_iota(jnp.int32, (weight_ref.shape[1], combine_ref.shape[1]), 0)
    if split:
        even = (lax.axis_index("expert") & 1) == 0
        block = line // (2 * CAP)
        for at, steps in enumerate(zip(BACK[1], BACK[0]), 1):
            came = jnp.where(even, *steps)
            line = jnp.where(block == at, line + 2 * CAP * (came - at), line)
    weight = functools.reduce(
        jnp.add,
        [
            jnp.where(line == found_ref[k : k + 1], combine_ref[k : k + 1], 0.0)
            for k in range(found_ref.shape[0])
        ],
    ).T
    high = weight.astype(jnp.bfloat16)
    low = (weight - high.astype(jnp.float32)).astype(jnp.bfloat16)
    weight_ref[...] = jnp.concatenate([high, low], axis=0)
    for copy in copies[1:]:
        copy.wait()


def stack(refs):
    return jnp.concatenate([ref[...] for ref in refs], axis=0)


def hidden_kernel(split, in_ref, twin_in_ref, *refs):
    *refs, out_ref = refs
    odd = lax.axis_index("expert") & 1
    rows = stack(refs)
    half_size = refs[0].shape[0] // 2
    hidden = []
    for half, ref in enumerate((in_ref, twin_in_ref)):
        gate = jnp.dot(rows, ref[0], preferred_element_type=jnp.float32)
        up = jnp.dot(rows, ref[1], preferred_element_type=jnp.float32)
        value = jax.nn.silu(gate) * up
        if split:
            place = lax.broadcasted_iota(jnp.int32, value.shape, 0) // half_size
            value = jnp.where((place & 1) == (odd ^ half), value, 0.0)
        hidden.append(value.astype(jnp.bfloat16))
    out_ref[...] = jnp.concatenate(hidden, axis=1)


def down_kernel(split, hidden_ref, down_ref, twin_down_ref, *refs):
    units = down_ref.shape[0]
    own = hidden_ref[:, :units], down_ref[...]
    twin = hidden_ref[:, units:], twin_down_ref[...]
    piece = jnp.dot(*own, preferred_element_type=jnp.float32)
    piece += jnp.dot(*twin, preferred_element_type=jnp.float32)
    size = refs[0].shape[0]
    blocks = [piece[size * b : size * (b + 1)] for b in range(len(refs))]
    if split:
        even = (lax.axis_index("expert") & 1) == 0
        blocks[1:] = [jnp.where(even, blocks[e], blocks[o]) for e, o in zip(*BACK)]
    for block, out_ref in zip(blocks, refs):
        out_ref[...] = block.astype(jnp.bfloat16)


def early_kernel(weight_ref, *refs):
    *refs, late_ref, total_ref = refs
    rows = total_ref.shape[0]
    lines = weight_ref.shape[1] - late_ref.shape[1]
    late_ref[...] = weight_ref[:, lines:]
    mixed = jnp.dot(weight_ref[:, :lines], stack(refs), preferred_element_type=jnp.float32)
    total_ref[...] = mixed[:rows] + mixed[rows:]


def mix_kernel(repeats, early, weight_ref, *refs):
    out_hbm, out_ref, sems = refs[-3:]
    early_refs, refs = refs[:early], refs[early:-3]
    rows, width = out_ref.shape
    parts = sems.shape[0]
    step = width // parts
    copies = []
    for part in range(parts):
        columns = slice(part * step, (part + 1) * step)
        pieces = [stack([ref.at[:, columns] for ref in refs[j::repeats]]) for j in range(repeats)]
        if repeats == 1:
            mixed = jnp.dot(weight_ref[...], pieces[0], preferred_element_type=jnp.float32)
        else:
            total = sum(piece.astype(jnp.float32) for piece in pieces)
            high = total.astype(jnp.bfloat16)
            low = (total - high.astype(jnp.float32)).astype(jnp.bfloat16)
            mixed = jnp.dot(weight_ref[...], high, preferred_element_type=jnp.float32)
            mixed += jnp.dot(weight_ref[...], low, preferred_element_type=jnp.float32)
        mixed = mixed[:rows] + mixed[rows:]
        for ref in early_refs:
            mixed += ref[:, columns]
        out_ref[:, columns] = mixed.astype(jnp.bfloat16)
        copies.append(
            pltpu.make_async_copy(out_ref.at[:, columns], out_hbm.at[:, columns], sems.at[part])
        )
        copies[-1].start()
    for copy in copies:
        copy.wait()


def call(kernel, outs, args, flops, arg_specs=None, out_specs=None, scratch=()):
    arg_specs = arg_specs or [VMEM] * len(args)
    nbytes = sum(x.size * x.dtype.itemsize for x in jax.tree.leaves((outs, args)))
    return pl.pallas_call(
        kernel,
        out_shape=outs,
        in_specs=arg_specs,
        out_specs=out_specs or jax.tree.map(lambda _: VMEM, outs),
        scratch_shapes=scratch,
        compiler_params=pltpu.CompilerParams(vmem_limit_bytes=16 << 20),
        cost_estimate=pl.CostEstimate(flops=flops, bytes_accessed=nbytes, transcendentals=0),
    )(*[pltpu.with_memory_space_constraint(x, s.memory_space) for x, s in zip(args, arg_specs)])


def shape_of(array):
    return jax.ShapeDtypeStruct(array.shape, array.dtype)


def scratch_for(scalars, arrays):
    return [
        *[pltpu.SMEM(x.shape, x.dtype) for x in scalars],
        *[pltpu.VMEM(x.shape, x.dtype) for x in arrays],
        pltpu.SemaphoreType.DMA((len(scalars) + len(arrays),)),
    ]


def exchange(blocks, split, back=False):
    devices = lax.axis_size("expert")

    def sends(i, k):
        return 2 * SENDS[i & 1][k - 1][i >> 1] + (1 - (i & 1)) if split else i ^ 2 * k

    def sent_from(i, k):
        return next(j for j in range(devices) if sends(j, k) == i)

    result = [blocks[0]]
    for k in range(1, len(blocks)):
        if back and split:
            pairs = [(i, sent_from(i, BACK[i & 1][k - 1])) for i in range(devices)]
        else:
            pairs = [(i, sends(i, k)) for i in range(devices)]
        result.append(lax.ppermute(blocks[k], "expert", pairs))
    return result


def from_twin(array):
    pairs = [(i, i ^ 1) for i in range(lax.axis_size("expert"))]
    return lax.ppermute(array, "expert", pairs)


def body(tokens, w_in, w_down, old_place, new_place, expert_ids, replica, combine):
    devices = lax.axis_size("expert")
    shards = devices // SLOTS
    split = shards == 1
    repeats = max(shards // 2, 1)
    chips = devices // 2
    rows, width = tokens.shape
    hidden = w_down.shape[0]
    twin_in = from_twin(w_in)
    operands = (new_place, old_place, expert_ids.T, replica.T, tokens)
    combine = combine.T
    block = jax.ShapeDtypeStruct((CAP * (2 if split else 1), width), jnp.bfloat16)
    found, *blocks = call(
        functools.partial(dispatch_kernel, shards),
        [shape_of(operands[2])] + [block] * (chips // repeats),
        operands,
        2 * SLOTS * CAP * rows * width,
        [HBM] * len(operands),
        scratch=scratch_for(operands[:2], operands[2:]),
    )
    received = exchange([blocks[c // repeats] for c in range(chips)], split)
    twin_down = from_twin(lax.optimization_barrier((w_down, found))[0])
    own_in, own_down, weight = call(
        functools.partial(prepare_kernel, split),
        [
            shape_of(w_in),
            shape_of(w_down),
            jax.ShapeDtypeStruct((2 * rows, SLOTS * CAP), jnp.bfloat16),
        ],
        (found, combine, w_in, w_down),
        0,
        [VMEM, HBM, HBM, HBM],
        scratch=[pltpu.VMEM(combine.shape, combine.dtype), pltpu.SemaphoreType.DMA((3,))],
    )
    units = call(
        functools.partial(hidden_kernel, split),
        jax.ShapeDtypeStruct((chips * block.shape[0], 2 * hidden), jnp.bfloat16),
        (own_in, twin_in, *received),
        800 * chips * block.shape[0] * hidden * width,
    )
    pieces = call(
        functools.partial(down_kernel, split),
        [block] * chips,
        (units, own_down, twin_down),
        4 * chips * block.shape[0] * hidden * width,
    )
    returned = exchange(pieces, split, back=True)
    early = []
    if split:
        first, returned = returned[:2], returned[2:]
        late_lines = len(returned) * block.shape[0]
        weight, total = call(
            early_kernel,
            [
                jax.ShapeDtypeStruct((2 * rows, late_lines), jnp.bfloat16),
                jax.ShapeDtypeStruct((rows, width), jnp.float32),
            ],
            (weight, *first),
            4 * len(first) * block.shape[0] * rows * width,
        )
        early = [total]
    parts = 4 if width % 512 == 0 else 1
    return call(
        functools.partial(mix_kernel, repeats, len(early)),
        shape_of(tokens),
        (weight, *early, *returned),
        4 * SLOTS * CAP * rows * width,
        out_specs=HBM,
        scratch=[pltpu.VMEM(tokens.shape, tokens.dtype), pltpu.SemaphoreType.DMA((parts,))],
    )


def solution(mesh):
    placed = (
        P(("group", "expert"), None),
        P(None, None, ("group", "expert")),
        P(("group", "expert"), None),
        P("group"),
        P("group"),
        P(("group", "expert"), None),
        P(("group", "expert"), None),
        P(("group", "expert"), None),
    )
    return jax.shard_map(
        body, mesh=mesh, in_specs=placed, out_specs=P(("group", "expert"), None), check_vma=False
    )
```

```python
import functools

import jax
import jax.numpy as jnp
from jax import lax
from jax.experimental import pallas as pl
from jax.experimental.pallas import tpu as pltpu
from jax.sharding import PartitionSpec as P

SLOTS = 8
CAP = 4
SENDS = (
    ((3, 2, 0, 1), (2, 3, 1, 0), (1, 0, 3, 2)),
    ((1, 2, 3, 0), (2, 3, 0, 1), (3, 0, 1, 2)),
)
BACK = ((3, 2, 1), (2, 1, 3))

VMEM = pl.BlockSpec(memory_space=pltpu.VMEM)
HBM = pl.BlockSpec(memory_space=pltpu.HBM)


def targets(shards, goes, new_ref, old_ref, ids, replica):
    slots, rows = new_ref.shape[0], ids.shape[1]
    device = lax.axis_index("expert")
    down = lax.broadcasted_iota(jnp.int32, (slots, rows), 0)
    expert = jnp.zeros((slots, rows), jnp.int32)
    line = jnp.zeros((slots, rows), jnp.int32)
    for slot in range(slots):
        source = jnp.where(new_ref[slot] == old_ref[slot], slot, slot ^ 1)
        away = source ^ (device // shards)
        if shards == 1:
            step = sum(jnp.where(source >> 1 == chip, k, 0) for k, chip in enumerate(goes, 1))
            away = (source & 1) | (step << 1)
        expert = jnp.where(down == slot, new_ref[slot], expert)
        line = jnp.where(down == slot, CAP * away, line)
    count = jnp.zeros((slots, rows), jnp.int32)
    rank = jnp.zeros((slots, rows), jnp.int32)
    for slot in range(slots):
        same = expert == new_ref[slot]
        count += jnp.where(same, 1, 0)
        rank += jnp.where(same & (down > slot), 1, 0)
    chosen = []
    for k in range(ids.shape[0]):
        hit = (ids[k : k + 1] == expert) & (rank == (replica[k : k + 1] & (count - 1)))
        chosen.append(jnp.where(hit, 1.0, 0.0))
    earlier = lax.broadcasted_iota(jnp.int32, (rows, rows), 0) < lax.broadcasted_iota(
        jnp.int32, (rows, rows), 1
    )
    any_choice = functools.reduce(jnp.add, chosen)
    position = jnp.dot(
        any_choice.astype(jnp.bfloat16),
        jnp.where(earlier, 1.0, 0.0).astype(jnp.bfloat16),
        preferred_element_type=jnp.float32,
    )
    line = line.astype(jnp.float32)
    found = []
    for hit in chosen:
        place = jnp.where(position < CAP, line + position + 1.0, 0.0)
        found.append((jnp.sum(hit * place, axis=0, keepdims=True) - 1.0).astype(jnp.int32))
        position = position + hit
    return found


def start_copies(sources, buffers, sems):
    copies = [pltpu.make_async_copy(*pair, sems.at[i]) for i, pair in enumerate(zip(sources, buffers))]
    for copy in copies:
        copy.start()
    return copies


def by_device(table):
    device = lax.axis_index("expert")
    return sum(jnp.where(device == i, entry, 0) for i, entry in enumerate(table))


def dispatch_kernel(shards, *refs):
    sources, refs = refs[:5], refs[5:]
    found_ref, *block_refs = refs[:-6]
    buffers, sems = refs[-6:-1], refs[-1]
    copies = start_copies(sources, buffers, sems)
    goes = [by_device([SENDS[i & 1][k][i >> 1] for i in range(SLOTS)]) for k in range(3)]
    for copy in copies[:-1]:
        copy.wait()
    found = targets(shards, goes, *buffers[:2], *[ref[...] for ref in buffers[2:-1]])
    found_ref[...] = jnp.concatenate(found, axis=0)
    tokens_ref = buffers[-1]
    size = block_refs[0].shape[0]
    line = lax.broadcasted_iota(jnp.int32, (size * len(block_refs), tokens_ref.shape[0]), 0)
    picked = functools.reduce(jnp.logical_or, [line == target for target in found])
    selector = jnp.where(picked, 1.0, 0.0).astype(jnp.bfloat16)
    copies[-1].wait()
    buffer = jnp.dot(selector, tokens_ref[...], preferred_element_type=jnp.float32)
    for b, block_ref in enumerate(block_refs):
        block_ref[...] = buffer[size * b : size * (b + 1)].astype(jnp.bfloat16)


def prepare_kernel(
    split, found_ref, combine_hbm, in_hbm, down_hbm, in_ref, down_ref, weight_ref, combine_ref, sems
):
    copies = start_copies(
        (combine_hbm, in_hbm, down_hbm), (combine_ref, in_ref, down_ref), sems
    )
    copies[0].wait()
    line = lax.broadcasted_iota(jnp.int32, (weight_ref.shape[1], combine_ref.shape[1]), 0)
    if split:
        even = (lax.axis_index("expert") & 1) == 0
        block = line // (2 * CAP)
        for at, steps in enumerate(zip(BACK[1], BACK[0]), 1):
            came = jnp.where(even, *steps)
            line = jnp.where(block == at, line + 2 * CAP * (came - at), line)
    weight = functools.reduce(
        jnp.add,
        [
            jnp.where(line == found_ref[k : k + 1], combine_ref[k : k + 1], 0.0)
            for k in range(found_ref.shape[0])
        ],
    ).T
    high = weight.astype(jnp.bfloat16)
    low = (weight - high.astype(jnp.float32)).astype(jnp.bfloat16)
    weight_ref[...] = jnp.concatenate([high, low], axis=0)
    for copy in copies[1:]:
        copy.wait()


def stack(refs):
    return jnp.concatenate([ref[...] for ref in refs], axis=0)


def hidden_kernel(split, in_ref, twin_in_ref, *refs):
    *refs, out_ref = refs
    odd = lax.axis_index("expert") & 1
    rows = stack(refs)
    half_size = refs[0].shape[0] // 2
    hidden = []
    for half, ref in enumerate((in_ref, twin_in_ref)):
        gate = jnp.dot(rows, ref[0], preferred_element_type=jnp.float32)
        up = jnp.dot(rows, ref[1], preferred_element_type=jnp.float32)
        value = jax.nn.silu(gate) * up
        if split:
            place = lax.broadcasted_iota(jnp.int32, value.shape, 0) // half_size
            value = jnp.where((place & 1) == (odd ^ half), value, 0.0)
        hidden.append(value.astype(jnp.bfloat16))
    out_ref[...] = jnp.concatenate(hidden, axis=1)


def down_kernel(split, hidden_ref, down_ref, twin_down_ref, *refs):
    units = down_ref.shape[0]
    own = hidden_ref[:, :units], down_ref[...]
    twin = hidden_ref[:, units:], twin_down_ref[...]
    piece = jnp.dot(*own, preferred_element_type=jnp.float32)
    piece += jnp.dot(*twin, preferred_element_type=jnp.float32)
    size = refs[0].shape[0]
    blocks = [piece[size * b : size * (b + 1)] for b in range(len(refs))]
    if split:
        even = (lax.axis_index("expert") & 1) == 0
        blocks[1:] = [jnp.where(even, blocks[e], blocks[o]) for e, o in zip(*BACK)]
    for block, out_ref in zip(blocks, refs):
        out_ref[...] = block.astype(jnp.bfloat16)


def early_kernel(weight_ref, *refs):
    *refs, late_ref, total_ref = refs
    rows = total_ref.shape[0]
    lines = weight_ref.shape[1] - late_ref.shape[1]
    late_ref[...] = weight_ref[:, lines:]
    mixed = jnp.dot(weight_ref[:, :lines], stack(refs), preferred_element_type=jnp.float32)
    total_ref[...] = mixed[:rows] + mixed[rows:]


def mix_kernel(repeats, early, weight_ref, *refs):
    out_hbm, out_ref, sems = refs[-3:]
    early_refs, refs = refs[:early], refs[early:-3]
    rows, width = out_ref.shape
    parts = sems.shape[0]
    step = width // parts
    copies = []
    for part in range(parts):
        columns = slice(part * step, (part + 1) * step)
        pieces = [stack([ref.at[:, columns] for ref in refs[j::repeats]]) for j in range(repeats)]
        if repeats == 1:
            mixed = jnp.dot(weight_ref[...], pieces[0], preferred_element_type=jnp.float32)
        else:
            total = sum(piece.astype(jnp.float32) for piece in pieces)
            high = total.astype(jnp.bfloat16)
            low = (total - high.astype(jnp.float32)).astype(jnp.bfloat16)
            mixed = jnp.dot(weight_ref[...], high, preferred_element_type=jnp.float32)
            mixed += jnp.dot(weight_ref[...], low, preferred_element_type=jnp.float32)
        mixed = mixed[:rows] + mixed[rows:]
        for ref in early_refs:
            mixed += ref[:, columns]
        out_ref[:, columns] = mixed.astype(jnp.bfloat16)
        copies.append(
            pltpu.make_async_copy(out_ref.at[:, columns], out_hbm.at[:, columns], sems.at[part])
        )
        copies[-1].start()
    for copy in copies:
        copy.wait()


def call(kernel, outs, args, flops, arg_specs=None, out_specs=None, scratch=()):
    arg_specs = arg_specs or [VMEM] * len(args)
    nbytes = sum(x.size * x.dtype.itemsize for x in jax.tree.leaves((outs, args)))
    return pl.pallas_call(
        kernel,
        out_shape=outs,
        in_specs=arg_specs,
        out_specs=out_specs or jax.tree.map(lambda _: VMEM, outs),
        scratch_shapes=scratch,
        compiler_params=pltpu.CompilerParams(vmem_limit_bytes=16 << 20),
        cost_estimate=pl.CostEstimate(flops=flops, bytes_accessed=nbytes, transcendentals=0),
    )(*[pltpu.with_memory_space_constraint(x, s.memory_space) for x, s in zip(args, arg_specs)])


def shape_of(array):
    return jax.ShapeDtypeStruct(array.shape, array.dtype)


def scratch_for(scalars, arrays):
    return [
        *[pltpu.SMEM(x.shape, x.dtype) for x in scalars],
        *[pltpu.VMEM(x.shape, x.dtype) for x in arrays],
        pltpu.SemaphoreType.DMA((len(scalars) + len(arrays),)),
    ]


def exchange(blocks, split, back=False):
    devices = lax.axis_size("expert")

    def sends(i, k):
        return 2 * SENDS[i & 1][k - 1][i >> 1] + (1 - (i & 1)) if split else i ^ 2 * k

    def sent_from(i, k):
        return next(j for j in range(devices) if sends(j, k) == i)

    result = [blocks[0]]
    for k in range(1, len(blocks)):
        if back and split:
            pairs = [(i, sent_from(i, BACK[i & 1][k - 1])) for i in range(devices)]
        else:
            pairs = [(i, sends(i, k)) for i in range(devices)]
        result.append(lax.ppermute(blocks[k], "expert", pairs))
    return result


def from_twin(array):
    pairs = [(i, i ^ 1) for i in range(lax.axis_size("expert"))]
    return lax.ppermute(array, "expert", pairs)


def body(tokens, w_in, w_down, old_place, new_place, expert_ids, replica, combine):
    devices = lax.axis_size("expert")
    shards = devices // SLOTS
    split = shards == 1
    repeats = max(shards // 2, 1)
    chips = devices // 2
    rows, width = tokens.shape
    hidden = w_down.shape[0]
    twin_in = from_twin(w_in)
    operands = (new_place, old_place, expert_ids.T, replica.T, tokens)
    combine = combine.T
    block = jax.ShapeDtypeStruct((CAP * (2 if split else 1), width), jnp.bfloat16)
    found, *blocks = call(
        functools.partial(dispatch_kernel, shards),
        [shape_of(operands[2])] + [block] * (chips // repeats),
        operands,
        2 * SLOTS * CAP * rows * width,
        [HBM] * len(operands),
        scratch=scratch_for(operands[:2], operands[2:]),
    )
    received = exchange([blocks[c // repeats] for c in range(chips)], split)
    twin_down = from_twin(lax.optimization_barrier((w_down, found))[0])
    own_in, own_down, weight = call(
        functools.partial(prepare_kernel, split),
        [
            shape_of(w_in),
            shape_of(w_down),
            jax.ShapeDtypeStruct((2 * rows, SLOTS * CAP), jnp.bfloat16),
        ],
        (found, combine, w_in, w_down),
        0,
        [VMEM, HBM, HBM, HBM],
        scratch=[pltpu.VMEM(combine.shape, combine.dtype), pltpu.SemaphoreType.DMA((3,))],
    )
    units = call(
        functools.partial(hidden_kernel, split),
        jax.ShapeDtypeStruct((chips * block.shape[0], 2 * hidden), jnp.bfloat16),
        (own_in, twin_in, *received),
        800 * chips * block.shape[0] * hidden * width,
    )
    pieces = call(
        functools.partial(down_kernel, split),
        [block] * chips,
        (units, own_down, twin_down),
        4 * chips * block.shape[0] * hidden * width,
    )
    returned = exchange(pieces, split, back=True)
    early = []
    if split:
        first, returned = returned[:2], returned[2:]
        late_lines = len(returned) * block.shape[0]
        weight, total = call(
            early_kernel,
            [
                jax.ShapeDtypeStruct((2 * rows, late_lines), jnp.bfloat16),
                jax.ShapeDtypeStruct((rows, width), jnp.float32),
            ],
            (weight, *first),
            4 * len(first) * block.shape[0] * rows * width,
        )
        early = [total]
    parts = 1 if split or width % 512 else 4
    return call(
        functools.partial(mix_kernel, repeats, len(early)),
        shape_of(tokens),
        (weight, *early, *returned),
        4 * SLOTS * CAP * rows * width,
        out_specs=HBM,
        scratch=[pltpu.VMEM(tokens.shape, tokens.dtype), pltpu.SemaphoreType.DMA((parts,))],
    )


def solution(mesh):
    placed = (
        P(("group", "expert"), None),
        P(None, None, ("group", "expert")),
        P(("group", "expert"), None),
        P("group"),
        P("group"),
        P(("group", "expert"), None),
        P(("group", "expert"), None),
        P(("group", "expert"), None),
    )
    return jax.shard_map(
        body, mesh=mesh, in_specs=placed, out_specs=P(("group", "expert"), None), check_vma=False
    )
```

```python
import functools

import jax
import jax.numpy as jnp
from jax import lax
from jax.experimental import pallas as pl
from jax.experimental.pallas import tpu as pltpu
from jax.sharding import PartitionSpec as P

SLOTS = 8
CAP = 4
SENDS = (
    ((3, 2, 0, 1), (2, 3, 1, 0), (1, 0, 3, 2)),
    ((1, 2, 3, 0), (2, 3, 0, 1), (3, 0, 1, 2)),
)
BACK = ((3, 2, 1), (2, 1, 3))

VMEM = pl.BlockSpec(memory_space=pltpu.VMEM)
HBM = pl.BlockSpec(memory_space=pltpu.HBM)


def targets(shards, goes, new_ref, old_ref, ids, replica):
    slots, rows = new_ref.shape[0], ids.shape[1]
    device = lax.axis_index("expert")
    down = lax.broadcasted_iota(jnp.int32, (slots, rows), 0)
    expert = jnp.zeros((slots, rows), jnp.int32)
    line = jnp.zeros((slots, rows), jnp.int32)
    for slot in range(slots):
        source = jnp.where(new_ref[slot] == old_ref[slot], slot, slot ^ 1)
        away = source ^ (device // shards)
        if shards == 1:
            step = sum(jnp.where(source >> 1 == chip, k, 0) for k, chip in enumerate(goes, 1))
            away = (source & 1) | (step << 1)
        expert = jnp.where(down == slot, new_ref[slot], expert)
        line = jnp.where(down == slot, CAP * away, line)
    count = jnp.zeros((slots, rows), jnp.int32)
    rank = jnp.zeros((slots, rows), jnp.int32)
    for slot in range(slots):
        same = expert == new_ref[slot]
        count += jnp.where(same, 1, 0)
        rank += jnp.where(same & (down > slot), 1, 0)
    chosen = []
    for k in range(ids.shape[0]):
        hit = (ids[k : k + 1] == expert) & (rank == (replica[k : k + 1] & (count - 1)))
        chosen.append(jnp.where(hit, 1.0, 0.0))
    earlier = lax.broadcasted_iota(jnp.int32, (rows, rows), 0) < lax.broadcasted_iota(
        jnp.int32, (rows, rows), 1
    )
    any_choice = functools.reduce(jnp.add, chosen)
    position = jnp.dot(
        any_choice.astype(jnp.bfloat16),
        jnp.where(earlier, 1.0, 0.0).astype(jnp.bfloat16),
        preferred_element_type=jnp.float32,
    )
    line = line.astype(jnp.float32)
    found = []
    for hit in chosen:
        place = jnp.where(position < CAP, line + position + 1.0, 0.0)
        found.append((jnp.sum(hit * place, axis=0, keepdims=True) - 1.0).astype(jnp.int32))
        position = position + hit
    return found


def start_copies(sources, buffers, sems):
    copies = [pltpu.make_async_copy(*pair, sems.at[i]) for i, pair in enumerate(zip(sources, buffers))]
    for copy in copies:
        copy.start()
    return copies


def by_device(table):
    device = lax.axis_index("expert")
    return sum(jnp.where(device == i, entry, 0) for i, entry in enumerate(table))


def dispatch_kernel(shards, *refs):
    sources, refs = refs[:5], refs[5:]
    found_ref, *block_refs = refs[:-6]
    buffers, sems = refs[-6:-1], refs[-1]
    copies = start_copies(sources, buffers, sems)
    goes = [by_device([SENDS[i & 1][k][i >> 1] for i in range(SLOTS)]) for k in range(3)]
    for copy in copies[:-1]:
        copy.wait()
    found = targets(shards, goes, *buffers[:2], *[ref[...] for ref in buffers[2:-1]])
    found_ref[...] = jnp.concatenate(found, axis=0)
    tokens_ref = buffers[-1]
    size = block_refs[0].shape[0]
    line = lax.broadcasted_iota(jnp.int32, (size * len(block_refs), tokens_ref.shape[0]), 0)
    picked = functools.reduce(jnp.logical_or, [line == target for target in found])
    selector = jnp.where(picked, 1.0, 0.0).astype(jnp.bfloat16)
    copies[-1].wait()
    buffer = jnp.dot(selector, tokens_ref[...], preferred_element_type=jnp.float32)
    for b, block_ref in enumerate(block_refs):
        block_ref[...] = buffer[size * b : size * (b + 1)].astype(jnp.bfloat16)


def prepare_kernel(
    split, found_ref, combine_hbm, in_hbm, down_hbm, in_ref, down_ref, weight_ref, combine_ref, sems
):
    copies = start_copies(
        (combine_hbm, in_hbm, down_hbm), (combine_ref, in_ref, down_ref), sems
    )
    copies[0].wait()
    line = lax.broadcasted_iota(jnp.int32, (weight_ref.shape[1], combine_ref.shape[1]), 0)
    if split:
        even = (lax.axis_index("expert") & 1) == 0
        block = line // (2 * CAP)
        for at, steps in enumerate(zip(BACK[1], BACK[0]), 1):
            came = jnp.where(even, *steps)
            line = jnp.where(block == at, line + 2 * CAP * (came - at), line)
    weight = functools.reduce(
        jnp.add,
        [
            jnp.where(line == found_ref[k : k + 1], combine_ref[k : k + 1], 0.0)
            for k in range(found_ref.shape[0])
        ],
    ).T
    high = weight.astype(jnp.bfloat16)
    low = (weight - high.astype(jnp.float32)).astype(jnp.bfloat16)
    weight_ref[...] = jnp.concatenate([high, low], axis=0)
    for copy in copies[1:]:
        copy.wait()


def stack(refs):
    return jnp.concatenate([ref[...] for ref in refs], axis=0)


def hidden_kernel(split, in_ref, twin_in_ref, *refs):
    *refs, out_ref = refs
    odd = lax.axis_index("expert") & 1
    rows = stack(refs)
    half_size = refs[0].shape[0] // 2
    hidden = []
    for half, ref in enumerate((in_ref, twin_in_ref)):
        gate = jnp.dot(rows, ref[0], preferred_element_type=jnp.float32)
        up = jnp.dot(rows, ref[1], preferred_element_type=jnp.float32)
        value = jax.nn.silu(gate) * up
        if split:
            place = lax.broadcasted_iota(jnp.int32, value.shape, 0) // half_size
            value = jnp.where((place & 1) == (odd ^ half), value, 0.0)
        hidden.append(value.astype(jnp.bfloat16))
    out_ref[...] = jnp.concatenate(hidden, axis=1)


def down_kernel(split, hidden_ref, down_ref, twin_down_ref, *refs):
    units = down_ref.shape[0]
    own = hidden_ref[:, :units], down_ref[...]
    twin = hidden_ref[:, units:], twin_down_ref[...]
    piece = jnp.dot(*own, preferred_element_type=jnp.float32)
    piece += jnp.dot(*twin, preferred_element_type=jnp.float32)
    size = refs[0].shape[0]
    blocks = [piece[size * b : size * (b + 1)] for b in range(len(refs))]
    if split:
        even = (lax.axis_index("expert") & 1) == 0
        blocks[1:] = [jnp.where(even, blocks[e], blocks[o]) for e, o in zip(*BACK)]
    for block, out_ref in zip(blocks, refs):
        out_ref[...] = block.astype(jnp.bfloat16)


def mix_kernel(repeats, weight_ref, *refs):
    out_hbm, out_ref, sems = refs[-3:]
    refs = refs[:-3]
    rows, width = out_ref.shape
    parts = sems.shape[0]
    step = width // parts
    copies = []
    for part in range(parts):
        columns = slice(part * step, (part + 1) * step)
        pieces = [stack([ref.at[:, columns] for ref in refs[j::repeats]]) for j in range(repeats)]
        if repeats == 1:
            mixed = jnp.dot(weight_ref[...], pieces[0], preferred_element_type=jnp.float32)
        else:
            total = sum(piece.astype(jnp.float32) for piece in pieces)
            high = total.astype(jnp.bfloat16)
            low = (total - high.astype(jnp.float32)).astype(jnp.bfloat16)
            mixed = jnp.dot(weight_ref[...], high, preferred_element_type=jnp.float32)
            mixed += jnp.dot(weight_ref[...], low, preferred_element_type=jnp.float32)
        out_ref[:, columns] = (mixed[:rows] + mixed[rows:]).astype(jnp.bfloat16)
        copies.append(
            pltpu.make_async_copy(out_ref.at[:, columns], out_hbm.at[:, columns], sems.at[part])
        )
        copies[-1].start()
    for copy in copies:
        copy.wait()


def call(kernel, outs, args, flops, arg_specs=None, out_specs=None, scratch=()):
    arg_specs = arg_specs or [VMEM] * len(args)
    nbytes = sum(x.size * x.dtype.itemsize for x in jax.tree.leaves((outs, args)))
    return pl.pallas_call(
        kernel,
        out_shape=outs,
        in_specs=arg_specs,
        out_specs=out_specs or jax.tree.map(lambda _: VMEM, outs),
        scratch_shapes=scratch,
        compiler_params=pltpu.CompilerParams(vmem_limit_bytes=16 << 20),
        cost_estimate=pl.CostEstimate(flops=flops, bytes_accessed=nbytes, transcendentals=0),
    )(*[pltpu.with_memory_space_constraint(x, s.memory_space) for x, s in zip(args, arg_specs)])


def shape_of(array):
    return jax.ShapeDtypeStruct(array.shape, array.dtype)


def scratch_for(scalars, arrays):
    return [
        *[pltpu.SMEM(x.shape, x.dtype) for x in scalars],
        *[pltpu.VMEM(x.shape, x.dtype) for x in arrays],
        pltpu.SemaphoreType.DMA((len(scalars) + len(arrays),)),
    ]


def exchange(blocks, split, back=False):
    devices = lax.axis_size("expert")

    def sends(i, k):
        return 2 * SENDS[i & 1][k - 1][i >> 1] + (1 - (i & 1)) if split else i ^ 2 * k

    def sent_from(i, k):
        return next(j for j in range(devices) if sends(j, k) == i)

    result = [blocks[0]]
    for k in range(1, len(blocks)):
        if back and split:
            pairs = [(i, sent_from(i, BACK[i & 1][k - 1])) for i in range(devices)]
        else:
            pairs = [(i, sends(i, k)) for i in range(devices)]
        result.append(lax.ppermute(blocks[k], "expert", pairs))
    return result


def from_twin(array):
    pairs = [(i, i ^ 1) for i in range(lax.axis_size("expert"))]
    return lax.ppermute(array, "expert", pairs)


def body(tokens, w_in, w_down, old_place, new_place, expert_ids, replica, combine):
    devices = lax.axis_size("expert")
    shards = devices // SLOTS
    split = shards == 1
    repeats = max(shards // 2, 1)
    chips = devices // 2
    rows, width = tokens.shape
    hidden = w_down.shape[0]
    operands = (new_place, old_place, expert_ids.T, replica.T, tokens)
    combine = combine.T
    block = jax.ShapeDtypeStruct((CAP * (2 if split else 1), width), jnp.bfloat16)
    found, *blocks = call(
        functools.partial(dispatch_kernel, shards),
        [shape_of(operands[2])] + [block] * (chips // repeats),
        operands,
        2 * SLOTS * CAP * rows * width,
        [HBM] * len(operands),
        scratch=scratch_for(operands[:2], operands[2:]),
    )
    received = exchange([blocks[c // repeats] for c in range(chips)], split)
    after_in, after_down, _ = lax.optimization_barrier((w_in, w_down, found))
    twin_in, twin_down = from_twin(after_in), from_twin(after_down)
    own_in, own_down, weight = call(
        functools.partial(prepare_kernel, split),
        [
            shape_of(w_in),
            shape_of(w_down),
            jax.ShapeDtypeStruct((2 * rows, SLOTS * CAP), jnp.bfloat16),
        ],
        (found, combine, w_in, w_down),
        0,
        [VMEM, HBM, HBM, HBM],
        scratch=[pltpu.VMEM(combine.shape, combine.dtype), pltpu.SemaphoreType.DMA((3,))],
    )
    units = call(
        functools.partial(hidden_kernel, split),
        jax.ShapeDtypeStruct((chips * block.shape[0], 2 * hidden), jnp.bfloat16),
        (own_in, twin_in, *received),
        800 * chips * block.shape[0] * hidden * width,
    )
    pieces = call(
        functools.partial(down_kernel, split),
        [block] * chips,
        (units, own_down, twin_down),
        4 * chips * block.shape[0] * hidden * width,
    )
    returned = exchange(pieces, split, back=True)
    parts = 4 if width % 512 == 0 else 1
    return call(
        functools.partial(mix_kernel, repeats),
        shape_of(tokens),
        (weight, *returned),
        4 * SLOTS * CAP * rows * width,
        out_specs=HBM,
        scratch=[pltpu.VMEM(tokens.shape, tokens.dtype), pltpu.SemaphoreType.DMA((parts,))],
    )


def solution(mesh):
    placed = (
        P(("group", "expert"), None),
        P(None, None, ("group", "expert")),
        P(("group", "expert"), None),
        P("group"),
        P("group"),
        P(("group", "expert"), None),
        P(("group", "expert"), None),
        P(("group", "expert"), None),
    )
    return jax.shard_map(
        body, mesh=mesh, in_specs=placed, out_specs=P(("group", "expert"), None), check_vma=False
    )
```

```python
import functools

import jax
import jax.numpy as jnp
from jax import lax
from jax.experimental import pallas as pl
from jax.experimental.pallas import tpu as pltpu
from jax.sharding import PartitionSpec as P

SLOTS = 8
CAP = 4
SENDS = (
    ((3, 2, 0, 1), (2, 3, 1, 0), (1, 0, 3, 2)),
    ((1, 2, 3, 0), (2, 3, 0, 1), (3, 0, 1, 2)),
)
BACK = ((3, 2, 1), (2, 1, 3))

VMEM = pl.BlockSpec(memory_space=pltpu.VMEM)
HBM = pl.BlockSpec(memory_space=pltpu.HBM)


def targets(shards, goes, new_ref, old_ref, ids, replica):
    new, old = new_ref[...], old_ref[...]
    slots, rows = new.shape[1], ids.shape[1]
    across = lax.broadcasted_iota(jnp.int32, new.shape, 1)
    source = jnp.where(new == old, across, across ^ 1)
    away = source ^ (lax.axis_index("expert") // shards)
    if shards == 1:
        step = sum(jnp.where(source >> 1 == chip, k, 0) for k, chip in enumerate(goes, 1))
        away = (source & 1) | (step << 1)
    holds = [jnp.broadcast_to(new[:, slot : slot + 1], (slots, rows)) for slot in range(slots)]
    first = [jnp.broadcast_to(away[:, slot : slot + 1], (slots, rows)) for slot in range(slots)]
    down = lax.broadcasted_iota(jnp.int32, (slots, rows), 0)
    expert = jnp.zeros((slots, rows), jnp.int32)
    line = jnp.zeros((slots, rows), jnp.int32)
    for slot in range(slots):
        expert = jnp.where(down == slot, holds[slot], expert)
        line = jnp.where(down == slot, CAP * first[slot], line)
    count = jnp.zeros((slots, rows), jnp.int32)
    rank = jnp.zeros((slots, rows), jnp.int32)
    for slot in range(slots):
        same = expert == holds[slot]
        count += jnp.where(same, 1, 0)
        rank += jnp.where(same & (down > slot), 1, 0)
    chosen = []
    for k in range(ids.shape[0]):
        hit = (ids[k : k + 1] == expert) & (rank == (replica[k : k + 1] & (count - 1)))
        chosen.append(jnp.where(hit, 1.0, 0.0))
    earlier = lax.broadcasted_iota(jnp.int32, (rows, rows), 0) < lax.broadcasted_iota(
        jnp.int32, (rows, rows), 1
    )
    any_choice = functools.reduce(jnp.add, chosen)
    position = jnp.dot(
        any_choice.astype(jnp.bfloat16),
        jnp.where(earlier, 1.0, 0.0).astype(jnp.bfloat16),
        preferred_element_type=jnp.float32,
    )
    line = line.astype(jnp.float32)
    found = []
    for hit in chosen:
        place = jnp.where(position < CAP, line + position + 1.0, 0.0)
        found.append((jnp.sum(hit * place, axis=0, keepdims=True) - 1.0).astype(jnp.int32))
        position = position + hit
    return found


def start_copies(sources, buffers, sems):
    copies = [pltpu.make_async_copy(*pair, sems.at[i]) for i, pair in enumerate(zip(sources, buffers))]
    for copy in copies:
        copy.start()
    return copies


def by_device(table):
    device = lax.axis_index("expert")
    return sum(jnp.where(device == i, entry, 0) for i, entry in enumerate(table))


def dispatch_kernel(shards, *refs):
    sources, refs = refs[:5], refs[5:]
    found_ref, *block_refs = refs[:-6]
    buffers, sems = refs[-6:-1], refs[-1]
    copies = start_copies(sources, buffers, sems)
    goes = [by_device([SENDS[i & 1][k][i >> 1] for i in range(SLOTS)]) for k in range(3)]
    for copy in copies[:-1]:
        copy.wait()
    found = targets(shards, goes, *buffers[:2], *[ref[...] for ref in buffers[2:-1]])
    found_ref[...] = jnp.concatenate(found, axis=0)
    tokens_ref = buffers[-1]
    size = block_refs[0].shape[0]
    line = lax.broadcasted_iota(jnp.int32, (size * len(block_refs), tokens_ref.shape[0]), 0)
    picked = functools.reduce(jnp.logical_or, [line == target for target in found])
    selector = jnp.where(picked, 1.0, 0.0).astype(jnp.bfloat16)
    copies[-1].wait()
    buffer = jnp.dot(selector, tokens_ref[...], preferred_element_type=jnp.float32)
    for b, block_ref in enumerate(block_refs):
        block_ref[...] = buffer[size * b : size * (b + 1)].astype(jnp.bfloat16)


def prepare_kernel(
    split, found_ref, combine_hbm, in_hbm, down_hbm, in_ref, down_ref, weight_ref, combine_ref, sems
):
    copies = start_copies(
        (combine_hbm, in_hbm, down_hbm), (combine_ref, in_ref, down_ref), sems
    )
    copies[0].wait()
    line = lax.broadcasted_iota(jnp.int32, (weight_ref.shape[1], combine_ref.shape[1]), 0)
    if split:
        even = (lax.axis_index("expert") & 1) == 0
        block = line // (2 * CAP)
        for at, steps in enumerate(zip(BACK[1], BACK[0]), 1):
            came = jnp.where(even, *steps)
            line = jnp.where(block == at, line + 2 * CAP * (came - at), line)
    weight = functools.reduce(
        jnp.add,
        [
            jnp.where(line == found_ref[k : k + 1], combine_ref[k : k + 1], 0.0)
            for k in range(found_ref.shape[0])
        ],
    ).T
    high = weight.astype(jnp.bfloat16)
    low = (weight - high.astype(jnp.float32)).astype(jnp.bfloat16)
    weight_ref[...] = jnp.concatenate([high, low], axis=0)
    for copy in copies[1:]:
        copy.wait()


def stack(refs):
    return jnp.concatenate([ref[...] for ref in refs], axis=0)


def hidden_kernel(split, in_ref, twin_in_ref, *refs):
    *refs, out_ref = refs
    odd = lax.axis_index("expert") & 1
    rows = stack(refs)
    half_size = refs[0].shape[0] // 2
    hidden = []
    for half, ref in enumerate((in_ref, twin_in_ref)):
        gate = jnp.dot(rows, ref[0], preferred_element_type=jnp.float32)
        up = jnp.dot(rows, ref[1], preferred_element_type=jnp.float32)
        value = jax.nn.silu(gate) * up
        if split:
            place = lax.broadcasted_iota(jnp.int32, value.shape, 0) // half_size
            value = jnp.where((place & 1) == (odd ^ half), value, 0.0)
        hidden.append(value.astype(jnp.bfloat16))
    out_ref[...] = jnp.concatenate(hidden, axis=1)


def down_kernel(split, hidden_ref, down_ref, twin_down_ref, *refs):
    units = down_ref.shape[0]
    own = hidden_ref[:, :units], down_ref[...]
    twin = hidden_ref[:, units:], twin_down_ref[...]
    piece = jnp.dot(*own, preferred_element_type=jnp.float32)
    piece += jnp.dot(*twin, preferred_element_type=jnp.float32)
    size = refs[0].shape[0]
    blocks = [piece[size * b : size * (b + 1)] for b in range(len(refs))]
    if split:
        even = (lax.axis_index("expert") & 1) == 0
        blocks[1:] = [jnp.where(even, blocks[e], blocks[o]) for e, o in zip(*BACK)]
    for block, out_ref in zip(blocks, refs):
        out_ref[...] = block.astype(jnp.bfloat16)


def mix_kernel(repeats, weight_ref, *refs):
    out_hbm, out_ref, sems = refs[-3:]
    refs = refs[:-3]
    rows, width = out_ref.shape
    parts = sems.shape[0]
    step = width // parts
    copies = []
    for part in range(parts):
        columns = slice(part * step, (part + 1) * step)
        pieces = [stack([ref.at[:, columns] for ref in refs[j::repeats]]) for j in range(repeats)]
        if repeats == 1:
            mixed = jnp.dot(weight_ref[...], pieces[0], preferred_element_type=jnp.float32)
        else:
            total = sum(piece.astype(jnp.float32) for piece in pieces)
            high = total.astype(jnp.bfloat16)
            low = (total - high.astype(jnp.float32)).astype(jnp.bfloat16)
            mixed = jnp.dot(weight_ref[...], high, preferred_element_type=jnp.float32)
            mixed += jnp.dot(weight_ref[...], low, preferred_element_type=jnp.float32)
        out_ref[:, columns] = (mixed[:rows] + mixed[rows:]).astype(jnp.bfloat16)
        copies.append(
            pltpu.make_async_copy(out_ref.at[:, columns], out_hbm.at[:, columns], sems.at[part])
        )
        copies[-1].start()
    for copy in copies:
        copy.wait()


def call(kernel, outs, args, flops, arg_specs=None, out_specs=None, scratch=()):
    arg_specs = arg_specs or [VMEM] * len(args)
    nbytes = sum(x.size * x.dtype.itemsize for x in jax.tree.leaves((outs, args)))
    return pl.pallas_call(
        kernel,
        out_shape=outs,
        in_specs=arg_specs,
        out_specs=out_specs or jax.tree.map(lambda _: VMEM, outs),
        scratch_shapes=scratch,
        compiler_params=pltpu.CompilerParams(vmem_limit_bytes=16 << 20),
        cost_estimate=pl.CostEstimate(flops=flops, bytes_accessed=nbytes, transcendentals=0),
    )(*[pltpu.with_memory_space_constraint(x, s.memory_space) for x, s in zip(args, arg_specs)])


def shape_of(array):
    return jax.ShapeDtypeStruct(array.shape, array.dtype)


def scratch_for(arrays):
    return [
        *[pltpu.VMEM(x.shape, x.dtype) for x in arrays],
        pltpu.SemaphoreType.DMA((len(arrays),)),
    ]


def exchange(blocks, split, back=False):
    devices = lax.axis_size("expert")

    def sends(i, k):
        return 2 * SENDS[i & 1][k - 1][i >> 1] + (1 - (i & 1)) if split else i ^ 2 * k

    def sent_from(i, k):
        return next(j for j in range(devices) if sends(j, k) == i)

    result = [blocks[0]]
    for k in range(1, len(blocks)):
        if back and split:
            pairs = [(i, sent_from(i, BACK[i & 1][k - 1])) for i in range(devices)]
        else:
            pairs = [(i, sends(i, k)) for i in range(devices)]
        result.append(lax.ppermute(blocks[k], "expert", pairs))
    return result


def from_twin(array):
    pairs = [(i, i ^ 1) for i in range(lax.axis_size("expert"))]
    return lax.ppermute(array, "expert", pairs)


def body(tokens, w_in, w_down, old_place, new_place, expert_ids, replica, combine):
    devices = lax.axis_size("expert")
    shards = devices // SLOTS
    split = shards == 1
    repeats = max(shards // 2, 1)
    chips = devices // 2
    rows, width = tokens.shape
    hidden = w_down.shape[0]
    operands = (new_place[None], old_place[None], expert_ids.T, replica.T, tokens)
    combine = combine.T
    block = jax.ShapeDtypeStruct((CAP * (2 if split else 1), width), jnp.bfloat16)
    found, *blocks = call(
        functools.partial(dispatch_kernel, shards),
        [shape_of(operands[2])] + [block] * (chips // repeats),
        operands,
        2 * SLOTS * CAP * rows * width,
        [HBM] * len(operands),
        scratch=scratch_for(operands),
    )
    received = exchange([blocks[c // repeats] for c in range(chips)], split)
    after_in, after_down, _ = lax.optimization_barrier((w_in, w_down, found))
    twin_in, twin_down = from_twin(after_in), from_twin(after_down)
    own_in, own_down, weight = call(
        functools.partial(prepare_kernel, split),
        [
            shape_of(w_in),
            shape_of(w_down),
            jax.ShapeDtypeStruct((2 * rows, SLOTS * CAP), jnp.bfloat16),
        ],
        (found, combine, w_in, w_down),
        0,
        [VMEM, HBM, HBM, HBM],
        scratch=[pltpu.VMEM(combine.shape, combine.dtype), pltpu.SemaphoreType.DMA((3,))],
    )
    units = call(
        functools.partial(hidden_kernel, split),
        jax.ShapeDtypeStruct((chips * block.shape[0], 2 * hidden), jnp.bfloat16),
        (own_in, twin_in, *received),
        800 * chips * block.shape[0] * hidden * width,
    )
    pieces = call(
        functools.partial(down_kernel, split),
        [block] * chips,
        (units, own_down, twin_down),
        4 * chips * block.shape[0] * hidden * width,
    )
    returned = exchange(pieces, split, back=True)
    parts = 4 if width % 512 == 0 else 1
    return call(
        functools.partial(mix_kernel, repeats),
        shape_of(tokens),
        (weight, *returned),
        4 * SLOTS * CAP * rows * width,
        out_specs=HBM,
        scratch=[pltpu.VMEM(tokens.shape, tokens.dtype), pltpu.SemaphoreType.DMA((parts,))],
    )


def solution(mesh):
    placed = (
        P(("group", "expert"), None),
        P(None, None, ("group", "expert")),
        P(("group", "expert"), None),
        P("group"),
        P("group"),
        P(("group", "expert"), None),
        P(("group", "expert"), None),
        P(("group", "expert"), None),
    )
    return jax.shard_map(
        body, mesh=mesh, in_specs=placed, out_specs=P(("group", "expert"), None), check_vma=False
    )
```

```python
import functools

import jax
import jax.numpy as jnp
from jax import lax
from jax.experimental import pallas as pl
from jax.experimental.pallas import tpu as pltpu
from jax.sharding import PartitionSpec as P

SLOTS = 8
CAP = 4
SENDS = (
    ((3, 2, 0, 1), (2, 3, 1, 0), (1, 0, 3, 2)),
    ((1, 2, 3, 0), (2, 3, 0, 1), (3, 0, 1, 2)),
)
BACK = ((3, 2, 1), (2, 1, 3))

VMEM = pl.BlockSpec(memory_space=pltpu.VMEM)
HBM = pl.BlockSpec(memory_space=pltpu.HBM)


def targets(shards, goes, new_ref, old_ref, ids, replica):
    slots, rows = new_ref.shape[0], ids.shape[1]
    device = lax.axis_index("expert")
    down = lax.broadcasted_iota(jnp.int32, (slots, rows), 0)
    expert = jnp.zeros((slots, rows), jnp.int32)
    line = jnp.zeros((slots, rows), jnp.int32)
    for slot in range(slots):
        source = jnp.where(new_ref[slot] == old_ref[slot], slot, slot ^ 1)
        away = source ^ (device // shards)
        if shards == 1:
            step = sum(jnp.where(source >> 1 == chip, k, 0) for k, chip in enumerate(goes, 1))
            away = (source & 1) | (step << 1)
        expert = jnp.where(down == slot, new_ref[slot], expert)
        line = jnp.where(down == slot, CAP * away, line)
    count = jnp.zeros((slots, rows), jnp.int32)
    rank = jnp.zeros((slots, rows), jnp.int32)
    for slot in range(slots):
        same = expert == new_ref[slot]
        count += jnp.where(same, 1, 0)
        rank += jnp.where(same & (down > slot), 1, 0)
    chosen = []
    for k in range(ids.shape[0]):
        hit = (ids[k : k + 1] == expert) & (rank == (replica[k : k + 1] & (count - 1)))
        chosen.append(jnp.where(hit, 1.0, 0.0))
    earlier = lax.broadcasted_iota(jnp.int32, (rows, rows), 0) < lax.broadcasted_iota(
        jnp.int32, (rows, rows), 1
    )
    any_choice = functools.reduce(jnp.add, chosen)
    position = jnp.dot(
        any_choice.astype(jnp.bfloat16),
        jnp.where(earlier, 1.0, 0.0).astype(jnp.bfloat16),
        preferred_element_type=jnp.float32,
    )
    line = line.astype(jnp.float32)
    found = []
    for hit in chosen:
        place = jnp.where(position < CAP, line + position + 1.0, 0.0)
        found.append((jnp.sum(hit * place, axis=0, keepdims=True) - 1.0).astype(jnp.int32))
        position = position + hit
    return found


def start_copies(sources, buffers, sems):
    copies = [pltpu.make_async_copy(*pair, sems.at[i]) for i, pair in enumerate(zip(sources, buffers))]
    for copy in copies:
        copy.start()
    return copies


def by_device(table):
    device = lax.axis_index("expert")
    return sum(jnp.where(device == i, entry, 0) for i, entry in enumerate(table))


def dispatch_kernel(shards, *refs):
    sources, refs = refs[:5], refs[5:]
    found_ref, *block_refs = refs[:-6]
    buffers, sems = refs[-6:-1], refs[-1]
    copies = start_copies(sources, buffers, sems)
    goes = [by_device([SENDS[i & 1][k][i >> 1] for i in range(SLOTS)]) for k in range(3)]
    for copy in copies[:-1]:
        copy.wait()
    found = targets(shards, goes, *buffers[:2], *[ref[...] for ref in buffers[2:-1]])
    found_ref[...] = jnp.concatenate(found, axis=0)
    tokens_ref = buffers[-1]
    size = block_refs[0].shape[0]
    line = lax.broadcasted_iota(jnp.int32, (size * len(block_refs), tokens_ref.shape[0]), 0)
    picked = functools.reduce(jnp.logical_or, [line == target for target in found])
    selector = jnp.where(picked, 1.0, 0.0).astype(jnp.bfloat16)
    copies[-1].wait()
    buffer = jnp.dot(selector, tokens_ref[...], preferred_element_type=jnp.float32)
    for b, block_ref in enumerate(block_refs):
        block_ref[...] = buffer[size * b : size * (b + 1)].astype(jnp.bfloat16)


def prepare_kernel(
    split, found_ref, combine_hbm, in_hbm, down_hbm, in_ref, down_ref, weight_ref, combine_ref, sems
):
    copies = start_copies(
        (combine_hbm, in_hbm, down_hbm), (combine_ref, in_ref, down_ref), sems
    )
    copies[0].wait()
    line = lax.broadcasted_iota(jnp.int32, (weight_ref.shape[1], combine_ref.shape[1]), 0)
    if split:
        even = (lax.axis_index("expert") & 1) == 0
        block = line // (2 * CAP)
        for at, steps in enumerate(zip(BACK[1], BACK[0]), 1):
            came = jnp.where(even, *steps)
            line = jnp.where(block == at, line + 2 * CAP * (came - at), line)
    weight = functools.reduce(
        jnp.add,
        [
            jnp.where(line == found_ref[k : k + 1], combine_ref[k : k + 1], 0.0)
            for k in range(found_ref.shape[0])
        ],
    ).T
    high = weight.astype(jnp.bfloat16)
    low = (weight - high.astype(jnp.float32)).astype(jnp.bfloat16)
    weight_ref[...] = jnp.concatenate([high, low], axis=0)
    for copy in copies[1:]:
        copy.wait()


def stack(refs):
    return jnp.concatenate([ref[...] for ref in refs], axis=0)


def hidden_kernel(split, in_ref, twin_in_ref, *refs):
    *refs, out_ref = refs
    odd = lax.axis_index("expert") & 1
    rows = stack(refs)
    half_size = refs[0].shape[0] // 2
    hidden = []
    for half, ref in enumerate((in_ref, twin_in_ref)):
        gate = jnp.dot(rows, ref[0], preferred_element_type=jnp.float32)
        up = jnp.dot(rows, ref[1], preferred_element_type=jnp.float32)
        value = jax.nn.silu(gate) * up
        if split:
            place = lax.broadcasted_iota(jnp.int32, value.shape, 0) // half_size
            value = jnp.where((place & 1) == (odd ^ half), value, 0.0)
        hidden.append(value.astype(jnp.bfloat16))
    out_ref[...] = jnp.concatenate(hidden, axis=1)


def down_kernel(split, hidden_ref, down_ref, twin_down_ref, *refs):
    units = down_ref.shape[0]
    size = refs[0].shape[0]
    blocks = [
        hidden_ref[size * b : size * (b + 1)].astype(jnp.float32) for b in range(len(refs))
    ]
    if split:
        even = (lax.axis_index("expert") & 1) == 0
        blocks[1:] = [jnp.where(even, blocks[e], blocks[o]) for e, o in zip(*BACK)]
    hidden = jnp.concatenate(blocks, axis=0).astype(jnp.bfloat16)
    piece = jnp.dot(hidden[:, :units], down_ref[...], preferred_element_type=jnp.float32)
    piece += jnp.dot(hidden[:, units:], twin_down_ref[...], preferred_element_type=jnp.float32)
    for b, out_ref in enumerate(refs):
        out_ref[...] = piece[size * b : size * (b + 1)].astype(jnp.bfloat16)


def mix_kernel(repeats, weight_ref, *refs):
    out_hbm, out_ref, sems = refs[-3:]
    refs = refs[:-3]
    rows, width = out_ref.shape
    parts = sems.shape[0]
    step = width // parts
    copies = []
    for part in range(parts):
        columns = slice(part * step, (part + 1) * step)
        pieces = [stack([ref.at[:, columns] for ref in refs[j::repeats]]) for j in range(repeats)]
        if repeats == 1:
            mixed = jnp.dot(weight_ref[...], pieces[0], preferred_element_type=jnp.float32)
        else:
            total = sum(piece.astype(jnp.float32) for piece in pieces)
            high = total.astype(jnp.bfloat16)
            low = (total - high.astype(jnp.float32)).astype(jnp.bfloat16)
            mixed = jnp.dot(weight_ref[...], high, preferred_element_type=jnp.float32)
            mixed += jnp.dot(weight_ref[...], low, preferred_element_type=jnp.float32)
        out_ref[:, columns] = (mixed[:rows] + mixed[rows:]).astype(jnp.bfloat16)
        copies.append(
            pltpu.make_async_copy(out_ref.at[:, columns], out_hbm.at[:, columns], sems.at[part])
        )
        copies[-1].start()
    for copy in copies:
        copy.wait()


def call(kernel, outs, args, flops, arg_specs=None, out_specs=None, scratch=()):
    arg_specs = arg_specs or [VMEM] * len(args)
    nbytes = sum(x.size * x.dtype.itemsize for x in jax.tree.leaves((outs, args)))
    return pl.pallas_call(
        kernel,
        out_shape=outs,
        in_specs=arg_specs,
        out_specs=out_specs or jax.tree.map(lambda _: VMEM, outs),
        scratch_shapes=scratch,
        compiler_params=pltpu.CompilerParams(vmem_limit_bytes=16 << 20),
        cost_estimate=pl.CostEstimate(flops=flops, bytes_accessed=nbytes, transcendentals=0),
    )(*[pltpu.with_memory_space_constraint(x, s.memory_space) for x, s in zip(args, arg_specs)])


def shape_of(array):
    return jax.ShapeDtypeStruct(array.shape, array.dtype)


def scratch_for(scalars, arrays):
    return [
        *[pltpu.SMEM(x.shape, x.dtype) for x in scalars],
        *[pltpu.VMEM(x.shape, x.dtype) for x in arrays],
        pltpu.SemaphoreType.DMA((len(scalars) + len(arrays),)),
    ]


def exchange(blocks, split, back=False):
    devices = lax.axis_size("expert")

    def sends(i, k):
        return 2 * SENDS[i & 1][k - 1][i >> 1] + (1 - (i & 1)) if split else i ^ 2 * k

    def sent_from(i, k):
        return next(j for j in range(devices) if sends(j, k) == i)

    result = [blocks[0]]
    for k in range(1, len(blocks)):
        if back and split:
            pairs = [(i, sent_from(i, BACK[i & 1][k - 1])) for i in range(devices)]
        else:
            pairs = [(i, sends(i, k)) for i in range(devices)]
        result.append(lax.ppermute(blocks[k], "expert", pairs))
    return result


def from_twin(array):
    pairs = [(i, i ^ 1) for i in range(lax.axis_size("expert"))]
    return lax.ppermute(array, "expert", pairs)


def body(tokens, w_in, w_down, old_place, new_place, expert_ids, replica, combine):
    devices = lax.axis_size("expert")
    shards = devices // SLOTS
    split = shards == 1
    repeats = max(shards // 2, 1)
    chips = devices // 2
    rows, width = tokens.shape
    hidden = w_down.shape[0]
    operands = (new_place, old_place, expert_ids.T, replica.T, tokens)
    combine = combine.T
    block = jax.ShapeDtypeStruct((CAP * (2 if split else 1), width), jnp.bfloat16)
    found, *blocks = call(
        functools.partial(dispatch_kernel, shards),
        [shape_of(operands[2])] + [block] * (chips // repeats),
        operands,
        2 * SLOTS * CAP * rows * width,
        [HBM] * len(operands),
        scratch=scratch_for(operands[:2], operands[2:]),
    )
    received = exchange([blocks[c // repeats] for c in range(chips)], split)
    after_in, after_down, _ = lax.optimization_barrier((w_in, w_down, found))
    twin_in, twin_down = from_twin(after_in), from_twin(after_down)
    own_in, own_down, weight = call(
        functools.partial(prepare_kernel, split),
        [
            shape_of(w_in),
            shape_of(w_down),
            jax.ShapeDtypeStruct((2 * rows, SLOTS * CAP), jnp.bfloat16),
        ],
        (found, combine, w_in, w_down),
        0,
        [VMEM, HBM, HBM, HBM],
        scratch=[pltpu.VMEM(combine.shape, combine.dtype), pltpu.SemaphoreType.DMA((3,))],
    )
    units = call(
        functools.partial(hidden_kernel, split),
        jax.ShapeDtypeStruct((chips * block.shape[0], 2 * hidden), jnp.bfloat16),
        (own_in, twin_in, *received),
        800 * chips * block.shape[0] * hidden * width,
    )
    pieces = call(
        functools.partial(down_kernel, split),
        [block] * chips,
        (units, own_down, twin_down),
        4 * chips * block.shape[0] * hidden * width,
    )
    returned = exchange(pieces, split, back=True)
    parts = 4 if width % 512 == 0 else 1
    return call(
        functools.partial(mix_kernel, repeats),
        shape_of(tokens),
        (weight, *returned),
        4 * SLOTS * CAP * rows * width,
        out_specs=HBM,
        scratch=[pltpu.VMEM(tokens.shape, tokens.dtype), pltpu.SemaphoreType.DMA((parts,))],
    )


def solution(mesh):
    placed = (
        P(("group", "expert"), None),
        P(None, None, ("group", "expert")),
        P(("group", "expert"), None),
        P("group"),
        P("group"),
        P(("group", "expert"), None),
        P(("group", "expert"), None),
        P(("group", "expert"), None),
    )
    return jax.shard_map(
        body, mesh=mesh, in_specs=placed, out_specs=P(("group", "expert"), None), check_vma=False
    )
```

```python
import functools

import jax
import jax.numpy as jnp
from jax import lax
from jax.experimental import pallas as pl
from jax.experimental.pallas import tpu as pltpu
from jax.sharding import PartitionSpec as P

SLOTS = 8
CAP = 4
SENDS = (
    ((3, 2, 0, 1), (2, 3, 1, 0), (1, 0, 3, 2)),
    ((1, 2, 3, 0), (2, 3, 0, 1), (3, 0, 1, 2)),
)
BACK = ((3, 2, 1), (2, 1, 3))

VMEM = pl.BlockSpec(memory_space=pltpu.VMEM)
HBM = pl.BlockSpec(memory_space=pltpu.HBM)


def targets(shards, goes, new_ref, old_ref, ids, replica):
    slots, rows = new_ref.shape[0], ids.shape[1]
    device = lax.axis_index("expert")
    down = lax.broadcasted_iota(jnp.int32, (slots, rows), 0)
    expert = jnp.zeros((slots, rows), jnp.int32)
    line = jnp.zeros((slots, rows), jnp.int32)
    for slot in range(slots):
        source = jnp.where(new_ref[slot] == old_ref[slot], slot, slot ^ 1)
        away = source ^ (device // shards)
        if shards == 1:
            step = sum(jnp.where(source >> 1 == chip, k, 0) for k, chip in enumerate(goes, 1))
            away = (source & 1) | (step << 1)
        expert = jnp.where(down == slot, new_ref[slot], expert)
        line = jnp.where(down == slot, CAP * away, line)
    count = jnp.zeros((slots, rows), jnp.int32)
    rank = jnp.zeros((slots, rows), jnp.int32)
    for slot in range(slots):
        same = expert == new_ref[slot]
        count += jnp.where(same, 1, 0)
        rank += jnp.where(same & (down > slot), 1, 0)
    chosen = []
    for k in range(ids.shape[0]):
        hit = (ids[k : k + 1] == expert) & (rank == (replica[k : k + 1] & (count - 1)))
        chosen.append(jnp.where(hit, 1.0, 0.0))
    earlier = lax.broadcasted_iota(jnp.int32, (rows, rows), 0) < lax.broadcasted_iota(
        jnp.int32, (rows, rows), 1
    )
    any_choice = functools.reduce(jnp.add, chosen)
    position = jnp.dot(
        any_choice.astype(jnp.bfloat16),
        jnp.where(earlier, 1.0, 0.0).astype(jnp.bfloat16),
        preferred_element_type=jnp.float32,
    )
    line = line.astype(jnp.float32)
    found = []
    for hit in chosen:
        place = jnp.where(position < CAP, line + position + 1.0, 0.0)
        found.append((jnp.sum(hit * place, axis=0, keepdims=True) - 1.0).astype(jnp.int32))
        position = position + hit
    return found


def start_copies(sources, buffers, sems):
    copies = [pltpu.make_async_copy(*pair, sems.at[i]) for i, pair in enumerate(zip(sources, buffers))]
    for copy in copies:
        copy.start()
    return copies


def by_device(table):
    device = lax.axis_index("expert")
    return sum(jnp.where(device == i, entry, 0) for i, entry in enumerate(table))


def dispatch_kernel(shards, *refs):
    sources, refs = refs[:5], refs[5:]
    found_ref, *block_refs = refs[:-6]
    buffers, sems = refs[-6:-1], refs[-1]
    copies = start_copies(sources, buffers, sems)
    goes = [by_device([SENDS[i & 1][k][i >> 1] for i in range(SLOTS)]) for k in range(3)]
    for copy in copies[:-1]:
        copy.wait()
    found = targets(shards, goes, *buffers[:2], *[ref[...] for ref in buffers[2:-1]])
    found_ref[...] = jnp.concatenate(found, axis=0)
    tokens_ref = buffers[-1]
    size = block_refs[0].shape[0]
    line = lax.broadcasted_iota(jnp.int32, (size * len(block_refs), tokens_ref.shape[0]), 0)
    picked = functools.reduce(jnp.logical_or, [line == target for target in found])
    selector = jnp.where(picked, 1.0, 0.0).astype(jnp.bfloat16)
    copies[-1].wait()
    buffer = jnp.dot(selector, tokens_ref[...], preferred_element_type=jnp.float32)
    for b, block_ref in enumerate(block_refs):
        block_ref[...] = buffer[size * b : size * (b + 1)].astype(jnp.bfloat16)


def prepare_kernel(
    split, found_ref, combine_hbm, in_hbm, down_hbm, in_ref, down_ref, weight_ref, combine_ref, sems
):
    copies = start_copies(
        (combine_hbm, in_hbm, down_hbm), (combine_ref, in_ref, down_ref), sems
    )
    copies[0].wait()
    line = lax.broadcasted_iota(jnp.int32, (weight_ref.shape[1], combine_ref.shape[1]), 0)
    if split:
        even = (lax.axis_index("expert") & 1) == 0
        block = line // (2 * CAP)
        for at, steps in enumerate(zip(BACK[1], BACK[0]), 1):
            came = jnp.where(even, *steps)
            line = jnp.where(block == at, line + 2 * CAP * (came - at), line)
    weight = functools.reduce(
        jnp.add,
        [
            jnp.where(line == found_ref[k : k + 1], combine_ref[k : k + 1], 0.0)
            for k in range(found_ref.shape[0])
        ],
    ).T
    high = weight.astype(jnp.bfloat16)
    low = (weight - high.astype(jnp.float32)).astype(jnp.bfloat16)
    weight_ref[...] = jnp.concatenate([high, low], axis=0)
    for copy in copies[1:]:
        copy.wait()


def stack(refs):
    return jnp.concatenate([ref[...] for ref in refs], axis=0)


def hidden_kernel(split, in_ref, twin_in_ref, *refs):
    *refs, out_ref = refs
    odd = lax.axis_index("expert") & 1
    rows = stack(refs)
    half_size = refs[0].shape[0] // 2
    hidden = []
    for half, ref in enumerate((in_ref, twin_in_ref)):
        gate = jnp.dot(rows, ref[0], preferred_element_type=jnp.float32)
        up = jnp.dot(rows, ref[1], preferred_element_type=jnp.float32)
        value = jax.nn.silu(gate) * up
        if split:
            place = lax.broadcasted_iota(jnp.int32, value.shape, 0) // half_size
            value = jnp.where((place & 1) == (odd ^ half), value, 0.0)
        hidden.append(value.astype(jnp.bfloat16))
    out_ref[...] = jnp.concatenate(hidden, axis=1)


def down_kernel(split, hidden_ref, down_ref, twin_down_ref, *refs):
    units = down_ref.shape[0]
    own = hidden_ref[:, :units], down_ref[...]
    twin = hidden_ref[:, units:], twin_down_ref[...]
    piece = jnp.dot(*own, preferred_element_type=jnp.float32)
    piece += jnp.dot(*twin, preferred_element_type=jnp.float32)
    size = refs[0].shape[0]
    blocks = [piece[size * b : size * (b + 1)] for b in range(len(refs))]
    if split:
        even = (lax.axis_index("expert") & 1) == 0
        blocks[1:] = [jnp.where(even, blocks[e], blocks[o]) for e, o in zip(*BACK)]
    for block, out_ref in zip(blocks, refs):
        out_ref[...] = block.astype(jnp.bfloat16)


def early_kernel(weight_ref, *refs):
    *refs, late_ref, total_ref = refs
    rows = total_ref.shape[0]
    lines = weight_ref.shape[1] - late_ref.shape[1]
    late_ref[...] = weight_ref[:, lines:]
    mixed = jnp.dot(weight_ref[:, :lines], stack(refs), preferred_element_type=jnp.float32)
    total_ref[...] = mixed[:rows] + mixed[rows:]


def mix_kernel(repeats, early, weight_ref, *refs):
    out_hbm, out_ref, sems = refs[-3:]
    early_refs, refs = refs[:early], refs[early:-3]
    rows, width = out_ref.shape
    parts = sems.shape[0]
    step = width // parts
    copies = []
    for part in range(parts):
        columns = slice(part * step, (part + 1) * step)
        pieces = [stack([ref.at[:, columns] for ref in refs[j::repeats]]) for j in range(repeats)]
        if repeats == 1:
            mixed = jnp.dot(weight_ref[...], pieces[0], preferred_element_type=jnp.float32)
        else:
            total = sum(piece.astype(jnp.float32) for piece in pieces)
            high = total.astype(jnp.bfloat16)
            low = (total - high.astype(jnp.float32)).astype(jnp.bfloat16)
            mixed = jnp.dot(weight_ref[...], high, preferred_element_type=jnp.float32)
            mixed += jnp.dot(weight_ref[...], low, preferred_element_type=jnp.float32)
        mixed = mixed[:rows] + mixed[rows:]
        for ref in early_refs:
            mixed += ref[:, columns]
        out_ref[:, columns] = mixed.astype(jnp.bfloat16)
        copies.append(
            pltpu.make_async_copy(out_ref.at[:, columns], out_hbm.at[:, columns], sems.at[part])
        )
        copies[-1].start()
    for copy in copies:
        copy.wait()


def call(kernel, outs, args, flops, arg_specs=None, out_specs=None, scratch=()):
    arg_specs = arg_specs or [VMEM] * len(args)
    nbytes = sum(x.size * x.dtype.itemsize for x in jax.tree.leaves((outs, args)))
    return pl.pallas_call(
        kernel,
        out_shape=outs,
        in_specs=arg_specs,
        out_specs=out_specs or jax.tree.map(lambda _: VMEM, outs),
        scratch_shapes=scratch,
        compiler_params=pltpu.CompilerParams(vmem_limit_bytes=16 << 20),
        cost_estimate=pl.CostEstimate(flops=flops, bytes_accessed=nbytes, transcendentals=0),
    )(*[pltpu.with_memory_space_constraint(x, s.memory_space) for x, s in zip(args, arg_specs)])


def shape_of(array):
    return jax.ShapeDtypeStruct(array.shape, array.dtype)


def scratch_for(scalars, arrays):
    return [
        *[pltpu.SMEM(x.shape, x.dtype) for x in scalars],
        *[pltpu.VMEM(x.shape, x.dtype) for x in arrays],
        pltpu.SemaphoreType.DMA((len(scalars) + len(arrays),)),
    ]


def exchange(blocks, split, back=False):
    devices = lax.axis_size("expert")

    def sends(i, k):
        return 2 * SENDS[i & 1][k - 1][i >> 1] + (1 - (i & 1)) if split else i ^ 2 * k

    def sent_from(i, k):
        return next(j for j in range(devices) if sends(j, k) == i)

    result = [blocks[0]]
    for k in range(1, len(blocks)):
        if back and split:
            pairs = [(i, sent_from(i, BACK[i & 1][k - 1])) for i in range(devices)]
        else:
            pairs = [(i, sends(i, k)) for i in range(devices)]
        result.append(lax.ppermute(blocks[k], "expert", pairs))
    return result


def from_twin(array):
    pairs = [(i, i ^ 1) for i in range(lax.axis_size("expert"))]
    return lax.ppermute(array, "expert", pairs)


def body(tokens, w_in, w_down, old_place, new_place, expert_ids, replica, combine):
    devices = lax.axis_size("expert")
    shards = devices // SLOTS
    split = shards == 1
    repeats = max(shards // 2, 1)
    chips = devices // 2
    rows, width = tokens.shape
    hidden = w_down.shape[0]
    operands = (new_place, old_place, expert_ids.T, replica.T, tokens)
    combine = combine.T
    block = jax.ShapeDtypeStruct((CAP * (2 if split else 1), width), jnp.bfloat16)
    found, *blocks = call(
        functools.partial(dispatch_kernel, shards),
        [shape_of(operands[2])] + [block] * (chips // repeats),
        operands,
        2 * SLOTS * CAP * rows * width,
        [HBM] * len(operands),
        scratch=scratch_for(operands[:2], operands[2:]),
    )
    received = exchange([blocks[c // repeats] for c in range(chips)], split)
    after_in, after_down, _ = lax.optimization_barrier((w_in, w_down, found))
    twin_in, twin_down = from_twin(after_in), from_twin(after_down)
    own_in, own_down, weight = call(
        functools.partial(prepare_kernel, split),
        [
            shape_of(w_in),
            shape_of(w_down),
            jax.ShapeDtypeStruct((2 * rows, SLOTS * CAP), jnp.bfloat16),
        ],
        (found, combine, w_in, w_down),
        0,
        [VMEM, HBM, HBM, HBM],
        scratch=[pltpu.VMEM(combine.shape, combine.dtype), pltpu.SemaphoreType.DMA((3,))],
    )
    units = call(
        functools.partial(hidden_kernel, split),
        jax.ShapeDtypeStruct((chips * block.shape[0], 2 * hidden), jnp.bfloat16),
        (own_in, twin_in, *received),
        800 * chips * block.shape[0] * hidden * width,
    )
    pieces = call(
        functools.partial(down_kernel, split),
        [block] * chips,
        (units, own_down, twin_down),
        4 * chips * block.shape[0] * hidden * width,
    )
    returned = exchange(pieces, split, back=True)
    early = []
    if split:
        first, returned = returned[:2], returned[2:]
        late_lines = len(returned) * block.shape[0]
        weight, total = call(
            early_kernel,
            [
                jax.ShapeDtypeStruct((2 * rows, late_lines), jnp.bfloat16),
                jax.ShapeDtypeStruct((rows, width), jnp.float32),
            ],
            (weight, *first),
            4 * len(first) * block.shape[0] * rows * width,
        )
        early = [total]
    parts = 4 if width % 512 == 0 else 1
    return call(
        functools.partial(mix_kernel, repeats, len(early)),
        shape_of(tokens),
        (weight, *early, *returned),
        4 * SLOTS * CAP * rows * width,
        out_specs=HBM,
        scratch=[pltpu.VMEM(tokens.shape, tokens.dtype), pltpu.SemaphoreType.DMA((parts,))],
    )


def solution(mesh):
    placed = (
        P(("group", "expert"), None),
        P(None, None, ("group", "expert")),
        P(("group", "expert"), None),
        P("group"),
        P("group"),
        P(("group", "expert"), None),
        P(("group", "expert"), None),
        P(("group", "expert"), None),
    )
    return jax.shard_map(
        body, mesh=mesh, in_specs=placed, out_specs=P(("group", "expert"), None), check_vma=False
    )
```
